128 devices in a mesh: ctx: 16 (over z, y), tp: 8 (over x, core).
Axes of the slice: x: 4, y: 4, z: 4, core: 2. Of those that a mesh axis runs over, the one named last changes fastest.
Arguments:
- queries: bfloat16 [2048, 8192], P('ctx', 'tp'), may hold values from -240 to 240
- stored_key_rows: bfloat16 [32768, 1024], P('ctx', 'tp'), may hold values from -12 to 12
- stored_value_rows: bfloat16 [32768, 1024], P('ctx', 'tp'), may hold values from -6 to 6
- fresh_key_rows: bfloat16 [2048, 1024], P('ctx', 'tp'), may hold values from -12 to 12
- fresh_value_rows: bfloat16 [2048, 1024], P('ctx', 'tp'), may hold values from -6 to 6
- cached_slot_position: int32 [32768], P('ctx'), may hold values from 0 to 32767, each once
- new_order: int32 [2048], P('ctx'), may hold values from 0 to 2047, each once
- span_len: int32 [16], P('ctx'), may hold values from 0 to 128
Outputs:
- attended: bfloat16 [2048, 8192], P('ctx', 'tp')
- mass: float32 [2048, 64], P('ctx', 'tp')
The draws below stay inside these ranges and needn't reach their ends.
Inputs may be any that keep to these rules, and one draw needn't show every extreme that they name: cached_slot_position holds every position below 32768 once. new_order holds every place below 2048 once.
All inputs are finite; a program needn't handle non-finite values.
Results may differ from the reference program's by a relative error of at most 0.024.
Values may be sent and summed in bfloat16 or wider, within the bound.
No kernel may reach another device: no remote copies, remote signals or barrier semaphores. Data moves between devices by JAX's collectives and lax.ppermute only.
A program may use at most 128 MiB of HBM per device.

```python
import jax
import jax.numpy as jnp
from jax import lax

QUERY_HEADS = 64
KEY_VALUE_HEADS = 8
HEAD_SIZE = 128
KB = 512
SPAN_DEV = 128
CACHED_TOKENS = 32768
NEW_TOKENS = 2048
N_CTX = 16


def draw_queries(key, part):
    key = jax.random.fold_in(key, 11)
    noise_key = jax.random.fold_in(key, 0)
    values = jnp.clip(2.0 * jax.random.normal(noise_key, (NEW_TOKENS, QUERY_HEADS * HEAD_SIZE), jnp.float32), -12.0, 12.0)
    return values.astype(jnp.bfloat16)


def touch_ends(values, key, smallest, high):
    spot = [jax.random.randint(jax.random.fold_in(key, axis), (), 0, length) for axis, length in enumerate(values.shape)]
    main_axis = values.shape.index(max(values.shape))
    beside = spot[:main_axis] + [(spot[main_axis] + 1) % values.shape[main_axis]] + spot[main_axis + 1:]
    return values.at[tuple(spot)].set(smallest).at[tuple(beside)].set(high)


def steps_of(rng, extent, cuts, smallest, high):
    def one(position, blocks):
        steps = jax.random.uniform(jax.random.fold_in(jax.random.fold_in(rng, 6), position), (blocks,), jnp.float32, smallest / len(cuts), high / len(cuts))
        return jnp.repeat(jnp.exp(steps), extent[position] // blocks).reshape((-1,) + (1,) * (len(extent) - position - 1))

    level = one(*cuts[0])
    for cut in cuts[1:]:
        level = level * one(*cut)
    return level


def scatter_about(key, shape, width, reach, cuts=(), held_as=jnp.bfloat16):
    result = jax.random.normal(key, shape, jnp.float32) * width
    if len(cuts) > 0:
        result = steps_of(key, shape, cuts, -0.22, 0.18) * result
    return jnp.clip(result, min=-reach, max=reach).astype(held_as)


def setup_inputs(seed: int = 0) -> dict:
    key_list = jax.random.split(jax.random.key(seed), 9)
    queries = draw_queries(jax.random.fold_in(key_list[8], 71), 0)
    stored_key_rows = scatter_about(key_list[1], (CACHED_TOKENS, KEY_VALUE_HEADS * HEAD_SIZE), 2.0, 12.0, ((0, 16), (1, 8)))
    stored_value_rows = scatter_about(key_list[2], (CACHED_TOKENS, KEY_VALUE_HEADS * HEAD_SIZE), 1.0, 6.0, ((0, 16), (1, 8)))
    fresh_key_rows = scatter_about(key_list[3], (NEW_TOKENS, KEY_VALUE_HEADS * HEAD_SIZE), 2.0, 12.0, ((0, 16), (1, 8)))
    fresh_value_rows = scatter_about(key_list[4], (NEW_TOKENS, KEY_VALUE_HEADS * HEAD_SIZE), 1.0, 6.0, ((0, 16), (1, 8)))
    cached_slot_position = jax.random.permutation(key_list[5], CACHED_TOKENS).astype(jnp.int32)
    new_order = jax.random.permutation(key_list[6], NEW_TOKENS).astype(jnp.int32)
    span_len = touch_ends(jax.random.randint(key_list[7], (N_CTX,), 0, SPAN_DEV + 1), jax.random.fold_in(key_list[7], 1), 0, SPAN_DEV).astype(jnp.int32)
    return {"queries": queries, "stored_key_rows": stored_key_rows, "stored_value_rows": stored_value_rows, "fresh_key_rows": fresh_key_rows, "fresh_value_rows": fresh_value_rows, "cached_slot_position": cached_slot_position, "new_order": new_order, "span_len": span_len}


def apply_rotary_turn(values, positions):
    half_dim = HEAD_SIZE // 2
    inverse = 500000.0 ** (-2.0 * jnp.arange(half_dim, dtype=jnp.float32) / HEAD_SIZE)
    angles = positions.astype(jnp.float32)[:, None] * inverse[None, :]
    cosine = jnp.cos(angles)[:, None, :]
    sine = jnp.sin(angles)[:, None, :]
    floats = values.astype(jnp.float32)
    lower = floats[..., :half_dim]
    upper = floats[..., half_dim:]
    return jnp.concatenate([lower * cosine - upper * sine, upper * cosine + lower * sine], -1).astype(jnp.bfloat16)


def block_terms(q_head, key_block, value_block, visible):
    scores = jnp.einsum("qgd,kd->qgk", q_head.astype(jnp.float32), key_block.astype(jnp.float32)) * (HEAD_SIZE ** -0.5)
    if visible is None:
        largest = jnp.max(scores, -1)
        weights = jnp.exp(scores - largest[..., None])
    else:
        mask3 = visible[:, None, :]
        largest = jnp.max(jnp.where(mask3, scores, -1e30), -1)
        weights = jnp.where(mask3, jnp.exp(scores - largest[..., None]), 0.0)
    totals = jnp.sum(weights, -1)
    rounded = weights.astype(jnp.bfloat16)
    weighted = jnp.einsum("qgk,kd->qgd", rounded.astype(jnp.float32), value_block.astype(jnp.float32))
    return largest, totals, weighted


def merge(earlier, later):
    top = jnp.maximum(earlier[0], later[0])
    left = jnp.exp(earlier[0] - top)
    right = jnp.exp(later[0] - top)
    return (top, earlier[1] * left + later[1] * right, earlier[2] * left[..., None] + later[2] * right[..., None])


def reference(queries, stored_key_rows, stored_value_rows, fresh_key_rows, fresh_value_rows, cached_slot_position, new_order, span_len):
    query_group_width = QUERY_HEADS // KEY_VALUE_HEADS
    query_positions = (CACHED_TOKENS + new_order).astype(jnp.int32)
    query_rows_joined = apply_rotary_turn(queries.reshape(NEW_TOKENS, QUERY_HEADS, HEAD_SIZE), query_positions).reshape(NEW_TOKENS, KEY_VALUE_HEADS, query_group_width, HEAD_SIZE)
    cached_keys_rotated = apply_rotary_turn(stored_key_rows.reshape(CACHED_TOKENS, KEY_VALUE_HEADS, HEAD_SIZE), cached_slot_position)
    fresh_keys_rotated = apply_rotary_turn(fresh_key_rows.reshape(NEW_TOKENS, KEY_VALUE_HEADS, HEAD_SIZE), query_positions)
    cached_value_rows = stored_value_rows.reshape(CACHED_TOKENS, KEY_VALUE_HEADS, HEAD_SIZE)
    fresh_value_block = fresh_value_rows.reshape(NEW_TOKENS, KEY_VALUE_HEADS, HEAD_SIZE)
    in_block = jnp.arange(NEW_TOKENS, dtype=jnp.int32) % SPAN_DEV
    valid = in_block < jnp.repeat(span_len.astype(jnp.int32), SPAN_DEV)

    def per_head(inputs_all):
        q_head, keys_c, vals_c, keys_n, vals_n = inputs_all
        start_state = (jnp.full((NEW_TOKENS, query_group_width), -1e30, jnp.float32),
                       jnp.zeros((NEW_TOKENS, query_group_width), jnp.float32),
                       jnp.zeros((NEW_TOKENS, query_group_width, HEAD_SIZE), jnp.float32))

        def cached_step(running, pair):
            return merge(running, block_terms(q_head, pair[0], pair[1], None)), None

        running, unused = lax.scan(cached_step, start_state,
                                   (keys_c.reshape(CACHED_TOKENS // KB, KB, HEAD_SIZE), vals_c.reshape(CACHED_TOKENS // KB, KB, HEAD_SIZE)))

        def new_step(running, quad):
            key_block, value_block, key_order, key_valid = quad
            visible = (key_order[None, :] <= new_order[:, None]) & key_valid[None, :]
            return merge(running, block_terms(q_head, key_block, value_block, visible)), None

        running, unused = lax.scan(new_step, running,
                                   (keys_n.reshape(N_CTX, SPAN_DEV, HEAD_SIZE), vals_n.reshape(N_CTX, SPAN_DEV, HEAD_SIZE),
                                    new_order.reshape(N_CTX, SPAN_DEV), valid.reshape(N_CTX, SPAN_DEV)))
        return running

    largest, totals, weighted = lax.map(per_head, (query_rows_joined.transpose(1, 0, 2, 3), cached_keys_rotated.transpose(1, 0, 2),
                                                   cached_value_rows.transpose(1, 0, 2), fresh_keys_rotated.transpose(1, 0, 2),
                                                   fresh_value_block.transpose(1, 0, 2)))
    attended = (weighted / totals[..., None]).transpose(1, 0, 2, 3).reshape(NEW_TOKENS, QUERY_HEADS * HEAD_SIZE).astype(jnp.bfloat16)
    mass = (largest + jnp.log(totals)).transpose(1, 0, 2).reshape(NEW_TOKENS, QUERY_HEADS)
    return attended, mass
```

```python
import functools

import jax
import jax.numpy as jnp
import ml_dtypes
import numpy as np
from jax import lax
from jax.experimental import pallas as pl
from jax.experimental.pallas import tpu as pltpu
from jax.sharding import PartitionSpec as P

GROUP = 8
HEAD = 128
TOK = 128
ROWS = GROUP * TOK
CACHED = 32768
SIDE = 4
PART = 512
KT = 256
LOG2E = 1.4426950408889634
LN2 = 0.6931471805599453
LOW = -1e30
TOO_BIG = 2.0**100
META = 16

VMEM = pl.BlockSpec(memory_space=pltpu.VMEM)
SMEM = pl.BlockSpec(memory_space=pltpu.SMEM)


def shift(block, axis, step):
    pairs = []
    for i in range(SIDE * SIDE):
        z, y = divmod(i, SIDE)
        j = ((z + step) % SIDE) * SIDE + y if axis == "z" else z * SIDE + (y + step) % SIDE
        pairs.append((i, j))
    return lax.ppermute(block, "ctx", pairs)


def turn_table():
    turns = 500000.0 ** (-2.0 * np.arange(64) / HEAD) / (2 * np.pi)
    first = _bf(turns)
    second = _bf(turns - first)
    third = turns - first - second
    return np.repeat(np.stack([first, second, third])[:, :, None], TOK, 2).astype(np.float32)


def _bf(x):
    return np.asarray(x, np.float32).astype(ml_dtypes.bfloat16).astype(np.float64)


def _fit():
    t = np.cos(np.linspace(0, np.pi, 4001)) * 0.5
    u = t * t
    cos = np.polynomial.polynomial.polyfit(u, np.cos(2 * np.pi * t), 8)
    good = np.abs(t) > 1e-3
    sin = np.polynomial.polynomial.polyfit(u[good], np.sin(2 * np.pi * t[good]) / t[good], 7)
    return [float(c) for c in cos], [float(c) for c in sin]


COS, SIN = _fit()


def angles(positions, table_ref):
    a = positions * table_ref[0]
    a = a - jnp.round(a)
    b = positions * table_ref[1]
    t = a + (b - jnp.round(b)) + positions * table_ref[2]
    t = t - jnp.round(t)
    u = t * t
    cos = jnp.full_like(u, COS[-1])
    for c in COS[-2::-1]:
        cos = cos * u + c
    sin = jnp.full_like(u, SIN[-1])
    for c in SIN[-2::-1]:
        sin = sin * u + c
    return cos, sin * t


def turned(x, cos, sin):
    lower, upper = x[:64], x[64:]
    return jnp.concatenate([lower * cos - upper * sin, upper * cos + lower * sin], 0)


def query_kernel(q_ref, order_ref, table_ref, out_ref):
    cos, sin = angles((order_ref[...] + CACHED).astype(jnp.float32), table_ref)
    scale = HEAD**-0.5 * LOG2E
    cos, sin = cos * scale, sin * scale
    for g in range(GROUP):
        lanes = slice(g * HEAD, (g + 1) * HEAD)
        x = q_ref[:, lanes].astype(jnp.float32).T
        out_ref[:, lanes] = turned(x, cos, sin).astype(jnp.bfloat16)


def key_kernel(
    k_ref, v_ref, fk_ref, fv_ref, pos_ref, order_ref, span_ref, table_ref, a1_ref, a2_ref, b1_ref, b2_ref
):
    def keys(x, positions):
        cos, sin = angles(positions.astype(jnp.float32), table_ref)
        return turned(x.astype(jnp.float32).T, cos, sin).T.astype(jnp.bfloat16)

    def values(x):
        return x.astype(jnp.float32).T.astype(jnp.bfloat16)

    blocks = PART // TOK
    for c, ref in enumerate((a1_ref, a2_ref, b1_ref, b2_ref)):
        for j in range(blocks):
            b = c * blocks + j
            rows = slice(b * TOK, (b + 1) * TOK)
            ref[j * TOK : (j + 1) * TOK, :] = keys(k_ref[rows, :], pos_ref[b : b + 1, :])
            ref[PART + j * TOK : PART + (j + 1) * TOK, :] = values(v_ref[rows, :])
    order = order_ref[...]
    a2_ref[2 * PART : 2 * PART + TOK, :] = keys(fk_ref[...], order + CACHED)
    a2_ref[2 * PART + TOK : 2 * PART + 2 * TOK, :] = values(fv_ref[...])

    def coded(places):
        high = jnp.right_shift(places, 4)
        rows = lax.broadcasted_iota(jnp.int32, (META, TOK), 0)
        both = jnp.where(rows == 0, high, jnp.where(rows == 1, places - high * 16, 0))
        return both.astype(jnp.float32).astype(jnp.bfloat16)

    lane = lax.broadcasted_iota(jnp.int32, (1, TOK), 1)
    a2_ref[2 * PART + 2 * TOK :, :] = coded(jnp.where(lane < span_ref[0], order, 4000))
    b2_ref[2 * PART :, :] = coded(order)


def places_of(meta):
    meta = meta.astype(jnp.float32)
    return meta[0:1, :] * 16.0 + meta[1:2, :]


def dot(a, b):
    return lax.dot_general(a, b, (((1,), (0,)), ((), ())), preferred_element_type=jnp.float32)


def lookup(table, i):
    if len(set(table)) == 1:
        return table[0]
    value = jnp.int32(table[-1])
    for j in range(len(table) - 2, -1, -1):
        value = jnp.where(i == j, jnp.int32(table[j]), value)
    return value


def attend_kernel(plan, *refs):
    it = iter(refs)
    n_q = len(plan["items"])
    q_refs = [next(it) for _ in range(n_q)]
    chunk_refs = [next(it) for _ in range(plan["n_chunks"])]
    fresh_refs = [next(it) for _ in range(plan["n_fresh"])]
    meta_refs = [next(it) for _ in range(plan["n_meta"])]
    if not plan["start"]:
        acc_in, ml_in = next(it), next(it)
    if plan["finish"]:
        out_refs = [next(it) for _ in range(n_q)]
    else:
        acc_out, ml_out = next(it), next(it)
    q_s, k_s = next(it), next(it)
    if plan["n_fresh"]:
        f_s, place_s, qplace_s = next(it), next(it), next(it)
    if plan["finish"]:
        acc_out, ml_out = next(it), next(it)

    for i, r in enumerate(q_refs):
        q_s[i] = r[...]
    for i, r in enumerate(chunk_refs):
        k_s[i] = r[0 : 2 * PART, :]
    if plan["n_fresh"]:
        for i, r in enumerate(fresh_refs):
            f_s[i * TOK : (i + 1) * TOK, :] = r[2 * PART : 2 * PART + TOK, :]
            f_s[(4 + i) * TOK : (5 + i) * TOK, :] = r[2 * PART + TOK : 2 * PART + 2 * TOK, :]
            row = places_of(r[2 * PART + 2 * TOK :, :])
            place_s[i * TOK : (i + 1) * TOK, :] = jnp.broadcast_to(row, (TOK, TOK)).T
        for i, r in enumerate(meta_refs):
            qplace_s[i] = jnp.broadcast_to(places_of(r[2 * PART :, :]), (8, TOK))

    def v_tile(ref, first):
        return jnp.concatenate(
            [ref[pl.ds(first + j * TOK, TOK), :] for j in range(KT // TOK)], 1
        )

    def chunk_tiles(item):
        for p in range(len(plan["items"][0])):
            c = lookup([chunks[p] for chunks in plan["items"]], item)
            ref = k_s.at[c]
            for first in range(0, PART, KT):
                yield (
                    lambda ref=ref, first=first: ref[first : first + KT, :],
                    lambda ref=ref, first=first: v_tile(ref, PART + first),
                    None,
                )

    def fresh_tiles(item):
        for first in range(0, 4 * TOK, KT):

            def visible(first=first):
                mask = place_s[first : first + KT, :] <= qplace_s[item][0:1, :]
                return jnp.concatenate([mask] * GROUP, 1)

            yield (
                lambda first=first: f_s[first : first + KT, :],
                lambda first=first: v_tile(f_s, 4 * TOK + first),
                visible,
            )

    def scores(tile, q):
        s = dot(tile[0](), q)
        return s if tile[2] is None else jnp.where(tile[2](), s, LOW)

    def quick(item, tiles, old):
        q = q_s[item]
        ahead = scores(tiles[0], q)
        if old is None:
            m = jnp.max(ahead, 0, keepdims=True)
            total, acc = None, None
        else:
            m, total, acc = old
        part = jnp.zeros((8, ROWS), jnp.float32)
        for j, tile in enumerate(tiles):
            s = ahead
            if j + 1 < len(tiles):
                ahead = scores(tiles[j + 1], q)
            p = jnp.exp2(s - m)
            part = part + jnp.sum(p.reshape(KT // 8, 8, ROWS), 0)
            pv = dot(tile[1](), p.astype(jnp.bfloat16))
            acc = pv if acc is None else acc + pv
        part = jnp.sum(part, 0, keepdims=True)
        return m, part if total is None else total + part, acc

    def careful(item, tiles, old):
        q = q_s[item]
        if old is None:
            m = jnp.full((1, ROWS), LOW, jnp.float32)
            total = jnp.zeros((1, ROWS), jnp.float32)
            acc = jnp.zeros((HEAD, ROWS), jnp.float32)
        else:
            m, total, acc = old
        for tile in tiles:
            s = scores(tile, q)
            top = jnp.maximum(m, jnp.max(s, 0, keepdims=True))
            back = jnp.exp2(m - top)
            p = jnp.exp2(s - top)
            if tile[2] is not None:
                p = jnp.where(tile[2](), p, 0.0)
            total = total * back + jnp.sum(p, 0, keepdims=True)
            acc = acc * back + dot(tile[1](), p.astype(jnp.bfloat16))
            m = top
        return m, total, acc

    def put(item, state):
        m, total, acc = state
        acc_out[item] = acc
        ml_out[item] = jnp.concatenate([m, total, jnp.zeros((6, ROWS), jnp.float32)], 0)

    def get(acc_ref, ml_ref, item):
        return ml_ref[item][0:1, :], ml_ref[item][1:2, :], acc_ref[item]

    def go(step, tiles_of, count, first):
        def body(item, carry):
            if first:
                old = None if plan["start"] else get(acc_in, ml_in, item)
            else:
                old = get(acc_out, ml_out, item)
            put(item, step(item, list(tiles_of(item)), old))
            return carry

        if count == 1:
            body(0, 0)
        else:
            lax.fori_loop(0, count, body, 0)

    def everything(step):
        go(step, chunk_tiles, n_q, True)
        if plan["n_fresh"]:
            go(step, fresh_tiles, plan["fresh"], False)

    everything(quick)
    worst = ml_out[0][1:2, :]
    for i in range(1, n_q):
        worst = jnp.maximum(worst, ml_out[i][1:2, :])
    fine = jnp.min(jnp.where(worst < TOO_BIG, 1, 0)) == 1

    @pl.when(jnp.logical_not(fine))
    def _():
        everything(careful)

    if plan["finish"]:
        for i in range(n_q):
            m, total, acc = get(acc_out, ml_out, i)
            out_refs[i][0:HEAD, :] = (acc / total).astype(jnp.bfloat16)
            out_refs[i][HEAD:, :] = coded_mass(m + jnp.log2(total))


def coded_mass(mass):
    a = mass.astype(jnp.bfloat16).astype(jnp.float32)
    b = (mass - a).astype(jnp.bfloat16).astype(jnp.float32)
    c = mass - a - b
    rows = lax.broadcasted_iota(jnp.int32, (META, ROWS), 0)
    return jnp.where(rows == 0, a, jnp.where(rows == 1, b, jnp.where(rows == 2, c, 0.0))).astype(jnp.bfloat16)


def attend(name, items, queries, chunks, state=None, fresh=0, fresh_chunks=(), metas=(), finish=False):
    n_q = len(items)
    plan = dict(
        items=items,
        n_chunks=len(chunks),
        n_fresh=len(fresh_chunks),
        n_meta=len(metas),
        fresh=fresh,
        start=state is None,
        finish=finish,
    )
    acc = jax.ShapeDtypeStruct((n_q, HEAD, ROWS), jnp.float32)
    ml = jax.ShapeDtypeStruct((n_q, 8, ROWS), jnp.float32)
    scratch = [
        pltpu.VMEM((n_q, HEAD, ROWS), jnp.bfloat16),
        pltpu.VMEM((len(chunks), 2 * PART, HEAD), jnp.bfloat16),
    ]
    if fresh_chunks:
        scratch += [
            pltpu.VMEM((8 * TOK, HEAD), jnp.bfloat16),
            pltpu.VMEM((4 * TOK, TOK), jnp.float32),
            pltpu.VMEM((len(metas), 8, TOK), jnp.float32),
        ]
    if finish:
        outs = [jax.ShapeDtypeStruct((HEAD + META, ROWS), jnp.bfloat16)] * n_q
        scratch += [pltpu.VMEM(acc.shape, jnp.float32), pltpu.VMEM(ml.shape, jnp.float32)]
    else:
        outs = [acc, ml]
    args = list(queries) + list(chunks) + list(fresh_chunks) + list(metas) + list(state or ())
    pairs = sum(len(c) for c in items) * PART * ROWS + fresh * 4 * TOK * ROWS
    return pl.pallas_call(
        functools.partial(attend_kernel, plan),
        out_shape=outs,
        in_specs=[VMEM] * len(args),
        out_specs=[VMEM] * len(outs),
        scratch_shapes=scratch,
        compiler_params=pltpu.CompilerParams(vmem_limit_bytes=40 * 2**20),
        cost_estimate=pl.CostEstimate(flops=pairs * 1024, bytes_accessed=0, transcendentals=0),
        name=name,
    )(*args)


def combine_kernel(acc_ref, ml_ref, *refs):
    parts, (att_ref, mass_ref) = refs[:-2], refs[-2:]
    total = ml_ref[0][1:2, :]
    masses = [ml_ref[0][0:1, :] + jnp.log2(total)]
    for r in parts:
        rows = r[HEAD:, :].astype(jnp.float32)
        masses.append(rows[0:1, :] + rows[1:2, :] + rows[2:3, :])
    top = functools.reduce(jnp.maximum, masses)
    weights = [jnp.exp2(m - top) for m in masses]
    den = functools.reduce(jnp.add, weights)
    mass = (top + jnp.log2(den)) * LN2
    shares = [w / den for w in weights]
    shares[0] = shares[0] / total
    for g in range(GROUP):
        lanes = slice(g * TOK, (g + 1) * TOK)
        x = acc_ref[0, :, lanes] * shares[0][:, lanes]
        for r, w in zip(parts, shares[1:]):
            x = x + r[0:HEAD, lanes].astype(jnp.float32) * w[:, lanes]
        att_ref[:, lanes] = x.T.astype(jnp.bfloat16)
    stacked = jnp.concatenate([mass[:, g * TOK : (g + 1) * TOK] for g in range(GROUP)], 0)
    stacked = jnp.concatenate([stacked] * (TOK // GROUP), 0)
    mass_ref[...] = stacked.T[:, 0:GROUP]


def per_device(queries, k, v, fk, fv, positions, order, span):
    table = jnp.asarray(turn_table())
    order = order.reshape(1, TOK)
    q0 = pl.pallas_call(
        query_kernel,
        out_shape=jax.ShapeDtypeStruct((HEAD, ROWS), jnp.bfloat16),
        in_specs=[VMEM] * 3,
        out_specs=VMEM,
        name="turn_queries",
    )(queries, order, table)

    def around(x, axis):
        return shift(x, axis, -1), shift(x, axis, 1)

    q_z = around(q0, "z")
    q_y = around(q0, "y")
    q_z2 = shift(q0, "z", 2)
    q_y2 = shift(q0, "y", 2)

    blk = jax.ShapeDtypeStruct((2 * PART, HEAD), jnp.bfloat16)
    a1, a2, b1, b2 = pl.pallas_call(
        key_kernel,
        out_shape=[
            blk,
            jax.ShapeDtypeStruct((2 * PART + 2 * TOK + META, HEAD), jnp.bfloat16),
            blk,
            jax.ShapeDtypeStruct((2 * PART + META, HEAD), jnp.bfloat16),
        ],
        in_specs=[VMEM] * 6 + [SMEM, VMEM],
        out_specs=[VMEM] * 4,
        name="turn_keys",
    )(k, v, fk, fv, positions.reshape(16, TOK), order, span, table)

    a1n = around(a1, "y")
    b1n = around(b1, "z")
    a2n = around(a2, "y")
    b2n = around(b2, "z")
    a1f, a2f = shift(a1n[1], "y", 1), shift(a2n[0], "y", -1)
    b1f, b2f = shift(b1n[1], "z", 1), shift(b2n[0], "z", -1)

    near = [q_z[0], q_z[1], q_y[0], q_y[1]]
    far = [q_z2, q_y2]

    own = attend("own", [(0, 1, 2, 3)], [q0], [a1, a2, b1, b2])
    st = attend("near_own", [(0, 1), (0, 1), (2, 3), (2, 3)], near, [a1, a2, b1, b2])
    st = attend("near_first", [(0, 1), (0, 1), (2, 3), (2, 3)], near, [*a1n, *b1n], st)
    st = attend("near_second", [(0, 1), (0, 1), (2, 3), (2, 3)], near, [*a2n, *b2n], st)
    sf = attend(
        "far",
        [(0, 1, 2, 3, 4, 5), (6, 7, 8, 9, 10, 11)],
        far,
        [a1, a2, *a1n, *a2n, b1, b2, *b1n, *b2n],
    )
    fresh = [a2, *a2n, a2f]
    r_z2, r_y2 = attend(
        "far_last", [(0, 1), (2, 3)], far, [a1f, a2f, b1f, b2f], sf, 1, fresh, [b2f], finish=True
    )
    back_z2, back_y2 = shift(r_z2, "z", 2), shift(r_y2, "y", 2)
    r_z0, r_z1, r_y0, r_y1 = attend(
        "near_last",
        [(0, 1), (0, 1), (2, 3), (2, 3)],
        near,
        [a1f, a2f, b1f, b2f],
        st,
        2,
        fresh,
        [*b2n],
        finish=True,
    )
    back = [shift(r_z0, "z", 1), shift(r_z1, "z", -1), shift(r_y0, "y", 1), shift(r_y1, "y", -1)]
    own = attend(
        "own_rest",
        [tuple(range(12))],
        [q0],
        [*a1n, *a2n, a1f, a2f, *b1n, *b2n, b1f, b2f],
        own,
        1,
        fresh,
        [b2],
    )
    return pl.pallas_call(
        combine_kernel,
        out_shape=[
            jax.ShapeDtypeStruct((TOK, GROUP * HEAD), jnp.bfloat16),
            jax.ShapeDtypeStruct((TOK, GROUP), jnp.float32),
        ],
        in_specs=[VMEM] * 8,
        out_specs=[VMEM] * 2,
        name="combine",
    )(*own, back_z2, back_y2, *back)


def solution(mesh):
    spec = (P("ctx", "tp"),) * 5 + (P("ctx"),) * 3
    return jax.shard_map(
        per_device,
        mesh=mesh,
        in_specs=spec,
        out_specs=(P("ctx", "tp"), P("ctx", "tp")),
        check_vma=False,
    )
```

```python
import functools

import jax
import jax.numpy as jnp
import ml_dtypes
import numpy as np
from jax import lax
from jax.experimental import pallas as pl
from jax.experimental.pallas import tpu as pltpu
from jax.sharding import PartitionSpec as P

GROUP = 8
HEAD = 128
TOK = 128
ROWS = GROUP * TOK
CACHED = 32768
SIDE = 4
CHUNK = 1024
TP = 8
KT = 256
LOG2E = 1.4426950408889634
LN2 = 0.6931471805599453
LOW = -1e30
TOO_BIG = 2.0**100
TOO_SMALL = 2.0**-60
META = 16

VMEM = pl.BlockSpec(memory_space=pltpu.VMEM)
SMEM = pl.BlockSpec(memory_space=pltpu.SMEM)


def shift(block, kind, step):
    pairs = []
    for i in range(SIDE * SIDE):
        z, y = divmod(i, SIDE)
        for t in range(TP):
            if (t % 2 == 0) == (kind == "keys"):
                j = z * SIDE + (y + step) % SIDE
            else:
                j = ((z + step) % SIDE) * SIDE + y
            pairs.append((i * TP + t, j * TP + t))
    return lax.ppermute(block, ("ctx", "tp"), pairs)


def _bf(x):
    return np.asarray(x, np.float32).astype(ml_dtypes.bfloat16).astype(np.float64)


def _fit():
    t = np.cos(np.linspace(0, np.pi, 4001)) * 0.5
    u = t * t
    cos = np.polynomial.polynomial.polyfit(u, np.cos(2 * np.pi * t), 8)
    good = np.abs(t) > 1e-3
    sin = np.polynomial.polynomial.polyfit(u[good], np.sin(2 * np.pi * t[good]) / t[good], 7)
    return [float(c) for c in cos], [float(c) for c in sin]


COS, SIN = _fit()


def _turns():
    turns = 500000.0 ** (-2.0 * np.arange(64) / HEAD) / (2 * np.pi)
    first = _bf(turns)
    second = _bf(turns - first)
    return [[float(x) for x in piece] for piece in (first, second, turns - first - second)]


TURNS = _turns()


def spread(constants):
    row = lax.broadcasted_iota(jnp.int32, (8, TOK), 0)
    tiles = []
    for first in range(0, 64, 8):
        tile = jnp.full((8, TOK), constants[first + 7], jnp.float32)
        for i in range(7):
            tile = jnp.where(row == i, constants[first + i], tile)
        tiles.append(tile)
    return jnp.concatenate(tiles, 0)


def angles(positions, turns):
    a = positions * turns[0]
    a = a - jnp.round(a)
    b = positions * turns[1]
    t = a + (b - jnp.round(b)) + positions * turns[2]
    t = t - jnp.round(t)
    u = t * t
    cos = jnp.full_like(u, COS[-1])
    for c in COS[-2::-1]:
        cos = cos * u + c
    sin = jnp.full_like(u, SIN[-1])
    for c in SIN[-2::-1]:
        sin = sin * u + c
    return cos, sin * t


def turned(x, cos, sin):
    lower, upper = x[:64], x[64:]
    return jnp.concatenate([lower * cos - upper * sin, upper * cos + lower * sin], 0)


def coded(places):
    high = jnp.right_shift(places, 4)
    rows = lax.broadcasted_iota(jnp.int32, (META, TOK), 0)
    both = jnp.where(rows == 0, high, jnp.where(rows == 1, places - high * 16, 0))
    return both.astype(jnp.float32).astype(jnp.bfloat16)


def places_of(meta):
    meta = meta.astype(jnp.float32)
    return meta[0:1, :] * 16.0 + meta[1:2, :]


def query_kernel(q_any, order_any, out_ref, q_ref, order_ref, sems):
    copies = [
        pltpu.make_async_copy(q_any, q_ref, sems.at[0]),
        pltpu.make_async_copy(order_any, order_ref, sems.at[1]),
    ]
    for c in copies:
        c.start()
    turns = [spread(piece) for piece in TURNS]
    for c in copies[::-1]:
        c.wait()
    cos, sin = angles((order_ref[...] + CACHED).astype(jnp.float32), turns)
    scale = HEAD**-0.5 * LOG2E
    cos, sin = cos * scale, sin * scale
    for g in range(GROUP):
        lanes = slice(g * HEAD, (g + 1) * HEAD)
        x = q_ref[:, lanes].astype(jnp.float32).T
        out_ref[0:HEAD, lanes] = turned(x, cos, sin).astype(jnp.bfloat16)
    out_ref[HEAD:, :] = jnp.concatenate([coded(order_ref[...])] * GROUP, 1)


FRESH_KEYS = 2 * CHUNK
FRESH_VALUES = FRESH_KEYS + TOK
PLACES = FRESH_VALUES + TOK


def key_kernel(start, k_ref, v_ref, pos_ref, *refs):
    out_ref = refs[-1]
    turns = [spread(piece) for piece in TURNS]

    def keys(x, positions):
        cos, sin = angles(positions.astype(jnp.float32), turns)
        return turned(x.astype(jnp.float32).T, cos, sin).T.astype(jnp.bfloat16)

    def values(x):
        return x.astype(jnp.float32).T.astype(jnp.bfloat16)

    if len(refs) > 1:
        fk_ref, fv_ref, order_ref, span_ref = refs[:-1]
        order = order_ref[...]
        out_ref[FRESH_KEYS:FRESH_VALUES, :] = keys(fk_ref[...], order + CACHED)
        out_ref[FRESH_VALUES:PLACES, :] = values(fv_ref[...])
        lane = lax.broadcasted_iota(jnp.int32, (1, TOK), 1)
        out_ref[PLACES:, :] = coded(jnp.where(lane < span_ref[0], order, 4000))
    for b in range(CHUNK // TOK):
        rows = slice(start + b * TOK, start + (b + 1) * TOK)
        tile = start // TOK + b
        out_ref[b * TOK : (b + 1) * TOK, :] = keys(k_ref[rows, :], pos_ref[tile : tile + 1, :])
        out_ref[CHUNK + b * TOK : CHUNK + (b + 1) * TOK, :] = values(v_ref[rows, :])


def dot(a, b):
    return lax.dot_general(a, b, (((1,), (0,)), ((), ())), preferred_element_type=jnp.float32)


def attend_kernel(plan, *refs):
    it = iter(refs)
    n_q, n_fresh = plan["n_q"], plan["n_fresh"]
    q_refs = [next(it) for _ in range(n_q)]
    kv_refs = [next(it) for _ in range(plan["n_kv"])]
    fresh_refs = [next(it) for _ in range(n_fresh)]
    if not plan["start"]:
        acc_in, ml_in = next(it), next(it)
    if plan["finish"]:
        out_refs = [next(it) for _ in range(n_q)]
    else:
        acc_out, ml_out = next(it), next(it)
    q_s = next(it)
    if n_fresh:
        f_s, place_s = next(it), next(it)
    if plan["finish"]:
        acc_out, ml_out = next(it), next(it)

    for i, r in enumerate(q_refs):
        q_s[i] = r[...]
    for i, r in enumerate(fresh_refs):
        f_s[i * TOK : (i + 1) * TOK, :] = r[FRESH_KEYS:FRESH_VALUES, :]
        f_s[(n_fresh + i) * TOK : (n_fresh + i + 1) * TOK, :] = r[FRESH_VALUES:PLACES, :]
        place_s[i * TOK : (i + 1) * TOK, :] = jnp.broadcast_to(places_of(r[PLACES:, :]), (TOK, TOK)).T

    def aligned(i):
        return i if isinstance(i, int) else pl.multiple_of(i, TOK)

    def k_tile(ref, first):
        return ref[pl.ds(aligned(first), KT), :]

    def v_tile(ref, first):
        return jnp.concatenate([ref[pl.ds(aligned(first + j * TOK), TOK), :] for j in range(KT // TOK)], 1)

    def scores(ref, first, item, masked):
        s = dot(k_tile(ref, first), q_s[item, 0:HEAD, :])
        if masked:
            mine = places_of(q_s[item, HEAD:, 0:TOK])
            mask = place_s[pl.ds(aligned(first), KT), :] <= mine
            s = jnp.where(jnp.concatenate([mask] * GROUP, 1), s, LOW)
        return s

    sources = [(ref, CHUNK, CHUNK, False) for ref in kv_refs]
    if n_fresh:
        sources.append((f_s, n_fresh * TOK, n_fresh * TOK, True))

    def old_of(item):
        if plan["start"]:
            return None
        at = item + plan["skip"]
        return ml_in[at][0:1, :], ml_in[at][1:2, :], acc_in[at]

    def put(item, m, total, acc):
        acc_out[item] = acc
        ml_out[item] = jnp.concatenate([m, total, jnp.zeros((6, ROWS), jnp.float32)], 0)

    def quick(item):
        tiles = [(ref, first, values, masked) for ref, values, n, masked in sources for first in range(0, n, KT)]
        old = old_of(item)
        if old is None:
            m, total, acc = None, None, None
        else:
            m, total, acc = old
        part = jnp.zeros((8, ROWS), jnp.float32)

        def scores_of(tile):
            return scores(tile[0], tile[1], item, tile[3])

        ahead = scores_of(tiles[0])
        for j, (ref, first, values, _) in enumerate(tiles):
            s = ahead
            if j + 1 < len(tiles):
                ahead = scores_of(tiles[j + 1])
            p = jnp.exp2(s) if m is None else jnp.exp2(s - m)
            part = part + jnp.sum(p.reshape(KT // 8, 8, ROWS), 0)
            pv = dot(v_tile(ref, values + first), p.astype(jnp.bfloat16))
            acc = pv if acc is None else acc + pv
        part = jnp.sum(part, 0, keepdims=True)
        if m is None:
            m, total = jnp.zeros((1, ROWS), jnp.float32), part
        else:
            total = total + part
        put(item, m, total, acc)

    def careful(item):
        old = old_of(item)
        if old is None:
            m = jnp.full((1, ROWS), LOW, jnp.float32)
            put(item, m, jnp.zeros((1, ROWS), jnp.float32), jnp.zeros((HEAD, ROWS), jnp.float32))
        else:
            put(item, *old)
        for ref, values, n, masked in sources:

            def step(t, carry, ref=ref, values=values, masked=masked):
                first = t * KT
                m, total, acc = ml_out[item][0:1, :], ml_out[item][1:2, :], acc_out[item]
                s = scores(ref, first, item, masked)
                top = jnp.maximum(m, jnp.max(s, 0, keepdims=True))
                back = jnp.exp2(m - top)
                p = jnp.where(s > 0.5 * LOW, jnp.exp2(s - top), 0.0)
                total = total * back + jnp.sum(p, 0, keepdims=True)
                acc = acc * back + dot(v_tile(ref, values + first), p.astype(jnp.bfloat16))
                put(item, top, total, acc)
                return carry

            lax.fori_loop(0, n // KT, step, 0)

    def everything(step):
        def body(item, carry):
            step(item)
            return carry

        if n_q == 1:
            step(0)
        else:
            lax.fori_loop(0, n_q, body, 0)

    everything(quick)
    fine = None
    for i in range(n_q):
        total = ml_out[i][1:2, :]
        good = jnp.where((total < TOO_BIG) & (total > TOO_SMALL), 1.0, 0.0)
        fine = good if fine is None else jnp.minimum(fine, good)

    @pl.when(jnp.min(fine) < 0.5)
    def _():
        everything(careful)

    if plan["finish"]:
        for i in range(n_q):
            m, total = ml_out[i][0:1, :], ml_out[i][1:2, :]
            out_refs[i][0:HEAD, :] = (acc_out[i] * (1.0 / total)).astype(jnp.bfloat16)
            out_refs[i][HEAD:, :] = coded_mass(m + jnp.log2(total))


def coded_mass(mass):
    a = mass.astype(jnp.bfloat16).astype(jnp.float32)
    b = (mass - a).astype(jnp.bfloat16).astype(jnp.float32)
    c = mass - a - b
    rows = lax.broadcasted_iota(jnp.int32, (META, ROWS), 0)
    return jnp.where(rows == 0, a, jnp.where(rows == 1, b, jnp.where(rows == 2, c, 0.0))).astype(jnp.bfloat16)


def attend(name, queries, kvs, state=None, fresh=(), finish=False, skip=0):
    n_q = len(queries)
    plan = dict(n_q=n_q, n_kv=len(kvs), n_fresh=len(fresh), start=state is None, finish=finish, skip=skip)
    acc = jax.ShapeDtypeStruct((n_q, HEAD, ROWS), jnp.float32)
    ml = jax.ShapeDtypeStruct((n_q, 8, ROWS), jnp.float32)
    scratch = [pltpu.VMEM((n_q, HEAD + META, ROWS), jnp.bfloat16)]
    if fresh:
        scratch += [
            pltpu.VMEM((2 * len(fresh) * TOK, HEAD), jnp.bfloat16),
            pltpu.VMEM((len(fresh) * TOK, TOK), jnp.float32),
        ]
    if finish:
        outs = [jax.ShapeDtypeStruct((HEAD + META, ROWS), jnp.bfloat16)] * n_q
        scratch += [pltpu.VMEM(acc.shape, jnp.float32), pltpu.VMEM(ml.shape, jnp.float32)]
    else:
        outs = [acc, ml]
    args = list(queries) + list(kvs) + list(fresh) + list(state or ())
    pairs = n_q * (len(kvs) * CHUNK + len(fresh) * TOK) * ROWS
    return pl.pallas_call(
        functools.partial(attend_kernel, plan),
        out_shape=outs,
        in_specs=[VMEM] * len(args),
        out_specs=[VMEM] * len(outs),
        scratch_shapes=scratch,
        compiler_params=pltpu.CompilerParams(vmem_limit_bytes=24 * 2**20),
        cost_estimate=pl.CostEstimate(flops=pairs * 1024, bytes_accessed=0, transcendentals=0),
        name=name,
    )(*args)


def combine_kernel(acc_ref, ml_ref, *refs):
    parts, (att_ref, mass_ref) = refs[:-2], refs[-2:]
    total = ml_ref[0][1:2, :]
    masses = [ml_ref[0][0:1, :] + jnp.log2(total)]
    for r in parts:
        rows = r[HEAD:, :].astype(jnp.float32)
        masses.append(rows[0:1, :] + rows[1:2, :] + rows[2:3, :])
    top = functools.reduce(jnp.maximum, masses)
    weights = [jnp.exp2(m - top) for m in masses]
    den = functools.reduce(jnp.add, weights)
    mass = (top + jnp.log2(den)) * LN2
    shares = [w / den for w in weights]
    shares[0] = shares[0] / total
    for g in range(GROUP):
        lanes = slice(g * TOK, (g + 1) * TOK)
        x = acc_ref[0, :, lanes] * shares[0][:, lanes]
        for r, w in zip(parts, shares[1:]):
            x = x + r[0:HEAD, lanes].astype(jnp.float32) * w[:, lanes]
        att_ref[:, lanes] = x.T.astype(jnp.bfloat16)
    mass_ref[...] = jnp.concatenate([mass[:, g * TOK : (g + 1) * TOK] for g in range(GROUP)], 0)


def prepare(name, kernel, shape, args, specs, work, scratch=()):
    return pl.pallas_call(
        kernel,
        out_shape=jax.ShapeDtypeStruct(shape, jnp.bfloat16),
        in_specs=specs,
        out_specs=VMEM,
        scratch_shapes=scratch,
        compiler_params=pltpu.CompilerParams(vmem_limit_bytes=8 * 2**20),
        cost_estimate=pl.CostEstimate(flops=work, bytes_accessed=0, transcendentals=0),
        name=name,
    )(*args)


def per_device(queries, k, v, fk, fv, positions, order, span):
    order = order.reshape(1, TOK)
    positions = positions.reshape(2 * CHUNK // TOK, TOK)
    q0 = prepare(
        "turn_queries",
        query_kernel,
        (HEAD + META, ROWS),
        (queries, order),
        [pl.BlockSpec(memory_space=pltpu.HBM)] * 2,
        10**9,
        [
            pltpu.VMEM((TOK, ROWS), jnp.bfloat16),
            pltpu.VMEM((1, TOK), jnp.int32),
            pltpu.SemaphoreType.DMA((2,)),
        ],
    )
    q_near = [shift(q0, "queries", -1), shift(q0, "queries", 1)]
    q_far = shift(q0, "queries", 2)

    first = prepare(
        "turn_keys_first",
        functools.partial(key_kernel, 0),
        (PLACES + META, HEAD),
        (k, v, positions, fk, fv, order, span),
        [VMEM] * 6 + [SMEM],
        2 * 10**9,
    )
    first_near = [shift(first, "keys", -1), shift(first, "keys", 1)]
    second = prepare(
        "turn_keys_second",
        functools.partial(key_kernel, CHUNK),
        (2 * CHUNK, HEAD),
        (k, v, positions),
        [VMEM] * 3,
        2 * 10**9,
    )
    second_near = [shift(second, "keys", -1), shift(second, "keys", 1)]
    first_far = shift(first_near[1], "keys", 1)
    second_far = shift(second_near[0], "keys", -1)
    fresh = [first, *first_near, first_far]

    mine = attend("mine_own", [q0], [first, second])
    state = attend("others_own", [q_far, *q_near], [first, second])
    state = attend("others_near", [q_far, *q_near], [*first_near, *second_near], state)
    (r_far,) = attend("far_last", [q_far], [first_far, second_far], state, fresh, finish=True)
    r_ahead, r_behind = attend("near_last", q_near, [first_far, second_far], state, fresh, finish=True, skip=1)
    back = [shift(r_far, "queries", 2), shift(r_ahead, "queries", 1), shift(r_behind, "queries", -1)]
    mine = attend("mine_rest", [q0], [*first_near, *second_near, first_far, second_far], mine, fresh)
    attended, mass = pl.pallas_call(
        combine_kernel,
        out_shape=[
            jax.ShapeDtypeStruct((TOK, GROUP * HEAD), jnp.bfloat16),
            jax.ShapeDtypeStruct((GROUP, TOK), jnp.float32),
        ],
        in_specs=[VMEM] * 5,
        out_specs=[VMEM] * 2,
        compiler_params=pltpu.CompilerParams(vmem_limit_bytes=8 * 2**20),
        name="combine",
    )(*mine, *back)
    return attended, mass.T


def solution(mesh):
    spec = (P("ctx", "tp"),) * 5 + (P("ctx"),) * 3
    return jax.shard_map(
        per_device,
        mesh=mesh,
        in_specs=spec,
        out_specs=(P("ctx", "tp"), P("ctx", "tp")),
        check_vma=False,
    )
```

```python
import functools

import jax
import jax.numpy as jnp
import ml_dtypes
import numpy as np
from jax import lax
from jax.experimental import pallas as pl
from jax.experimental.pallas import tpu as pltpu
from jax.sharding import PartitionSpec as P

GROUP = 8
HEAD = 128
TOK = 128
ROWS = GROUP * TOK
CACHED = 32768
SIDE = 4
CHUNK = 1024
TP = 8
KT = 256
LOG2E = 1.4426950408889634
LN2 = 0.6931471805599453
LOW = -1e30
TOO_BIG = 2.0**100
TOO_SMALL = 2.0**-60
META = 16

VMEM = pl.BlockSpec(memory_space=pltpu.VMEM)
SMEM = pl.BlockSpec(memory_space=pltpu.SMEM)


def shift(block, kind, step):
    pairs = []
    for i in range(SIDE * SIDE):
        z, y = divmod(i, SIDE)
        for t in range(TP):
            if (t % 2 == 0) == (kind == "keys"):
                j = z * SIDE + (y + step) % SIDE
            else:
                j = ((z + step) % SIDE) * SIDE + y
            pairs.append((i * TP + t, j * TP + t))
    return lax.ppermute(block, ("ctx", "tp"), pairs)


def _bf(x):
    return np.asarray(x, np.float32).astype(ml_dtypes.bfloat16).astype(np.float64)


def _fit():
    t = np.cos(np.linspace(0, np.pi, 4001)) * 0.5
    u = t * t
    cos = np.polynomial.polynomial.polyfit(u, np.cos(2 * np.pi * t), 8)
    good = np.abs(t) > 1e-3
    sin = np.polynomial.polynomial.polyfit(u[good], np.sin(2 * np.pi * t[good]) / t[good], 7)
    return [float(c) for c in cos], [float(c) for c in sin]


COS, SIN = _fit()


def _turns():
    turns = 500000.0 ** (-2.0 * np.arange(64) / HEAD) / (2 * np.pi)
    first = _bf(turns)
    second = _bf(turns - first)
    return [[float(x) for x in piece] for piece in (first, second, turns - first - second)]


TURNS = _turns()


def spread(constants):
    row = lax.broadcasted_iota(jnp.int32, (8, TOK), 0)
    tiles = []
    for first in range(0, 64, 8):
        tile = jnp.full((8, TOK), constants[first + 7], jnp.float32)
        for i in range(7):
            tile = jnp.where(row == i, constants[first + i], tile)
        tiles.append(tile)
    return jnp.concatenate(tiles, 0)


def angles(positions, turns):
    a = positions * turns[0]
    a = a - jnp.round(a)
    b = positions * turns[1]
    t = a + (b - jnp.round(b)) + positions * turns[2]
    t = t - jnp.round(t)
    u = t * t
    cos = jnp.full_like(u, COS[-1])
    for c in COS[-2::-1]:
        cos = cos * u + c
    sin = jnp.full_like(u, SIN[-1])
    for c in SIN[-2::-1]:
        sin = sin * u + c
    return cos, sin * t


def turned(x, cos, sin):
    lower, upper = x[:64], x[64:]
    return jnp.concatenate([lower * cos - upper * sin, upper * cos + lower * sin], 0)


def coded(places):
    high = jnp.right_shift(places, 4)
    rows = lax.broadcasted_iota(jnp.int32, (META, TOK), 0)
    both = jnp.where(rows == 0, high, jnp.where(rows == 1, places - high * 16, 0))
    return both.astype(jnp.float32).astype(jnp.bfloat16)


def places_of(meta):
    meta = meta.astype(jnp.float32)
    return meta[0:1, :] * 16.0 + meta[1:2, :]


def query_kernel(q_any, order_any, out_ref, q_ref, order_ref, sems):
    copies = [
        pltpu.make_async_copy(q_any, q_ref, sems.at[0]),
        pltpu.make_async_copy(order_any, order_ref, sems.at[1]),
    ]
    for c in copies:
        c.start()
    turns = [spread(piece) for piece in TURNS]
    for c in copies[::-1]:
        c.wait()
    cos, sin = angles((order_ref[...] + CACHED).astype(jnp.float32), turns)
    scale = HEAD**-0.5 * LOG2E
    cos, sin = cos * scale, sin * scale
    for g in range(GROUP):
        lanes = slice(g * HEAD, (g + 1) * HEAD)
        x = q_ref[:, lanes].astype(jnp.float32).T
        out_ref[0:HEAD, lanes] = turned(x, cos, sin).astype(jnp.bfloat16)
    out_ref[HEAD:, :] = jnp.concatenate([coded(order_ref[...])] * GROUP, 1)


FRESH_KEYS = 2 * CHUNK
FRESH_VALUES = FRESH_KEYS + TOK
PLACES = FRESH_VALUES + TOK


def key_kernel(start, k_ref, v_ref, pos_ref, *refs):
    out_ref = refs[-1]
    turns = [spread(piece) for piece in TURNS]

    def keys(x, positions):
        cos, sin = angles(positions.astype(jnp.float32), turns)
        return turned(x.astype(jnp.float32).T, cos, sin).T.astype(jnp.bfloat16)

    def values(x):
        return x.astype(jnp.float32).T.astype(jnp.bfloat16)

    if len(refs) > 1:
        fk_ref, fv_ref, order_ref, span_ref = refs[:-1]
        order = order_ref[...]
        out_ref[FRESH_KEYS:FRESH_VALUES, :] = keys(fk_ref[...], order + CACHED)
        out_ref[FRESH_VALUES:PLACES, :] = values(fv_ref[...])
        lane = lax.broadcasted_iota(jnp.int32, (1, TOK), 1)
        out_ref[PLACES:, :] = coded(jnp.where(lane < span_ref[0], order, 4000))
    for b in range(CHUNK // TOK):
        rows = slice(start + b * TOK, start + (b + 1) * TOK)
        tile = start // TOK + b
        out_ref[b * TOK : (b + 1) * TOK, :] = keys(k_ref[rows, :], pos_ref[tile : tile + 1, :])
        out_ref[CHUNK + b * TOK : CHUNK + (b + 1) * TOK, :] = values(v_ref[rows, :])


def dot(a, b):
    return lax.dot_general(a, b, (((1,), (0,)), ((), ())), preferred_element_type=jnp.float32)


def attend_kernel(plan, *refs):
    it = iter(refs)
    n_q, n_fresh = plan["n_q"], plan["n_fresh"]
    q_refs = [next(it) for _ in range(n_q)]
    kv_refs = [next(it) for _ in range(plan["n_kv"])]
    fresh_refs = [next(it) for _ in range(n_fresh)]
    if not plan["start"]:
        acc_in, ml_in = next(it), next(it)
    if plan["finish"]:
        out_refs = [next(it) for _ in range(n_q)]
    else:
        acc_out, ml_out = next(it), next(it)
    q_s = next(it)
    if n_fresh:
        f_s, place_s = next(it), next(it)
    if plan["finish"]:
        acc_out, ml_out = next(it), next(it)

    for i, r in enumerate(q_refs):
        q_s[i] = r[...]
    for i, r in enumerate(fresh_refs):
        f_s[i * TOK : (i + 1) * TOK, :] = r[FRESH_KEYS:FRESH_VALUES, :]
        f_s[(n_fresh + i) * TOK : (n_fresh + i + 1) * TOK, :] = r[FRESH_VALUES:PLACES, :]
        place_s[i * TOK : (i + 1) * TOK, :] = jnp.broadcast_to(places_of(r[PLACES:, :]), (TOK, TOK)).T

    def aligned(i):
        return i if isinstance(i, int) else pl.multiple_of(i, TOK)

    def k_tile(ref, first):
        return ref[pl.ds(aligned(first), KT), :]

    def v_tile(ref, first):
        return jnp.concatenate([ref[pl.ds(aligned(first + j * TOK), TOK), :] for j in range(KT // TOK)], 1)

    def scores(ref, first, item, masked):
        s = dot(k_tile(ref, first), q_s[item, 0:HEAD, :])
        if masked:
            mine = places_of(q_s[item, HEAD:, 0:TOK])
            mask = place_s[pl.ds(aligned(first), KT), :] <= mine
            s = jnp.where(jnp.concatenate([mask] * GROUP, 1), s, LOW)
        return s

    sources = [(ref, CHUNK, CHUNK, False) for ref in kv_refs]
    if n_fresh:
        sources.append((f_s, n_fresh * TOK, n_fresh * TOK, True))

    def old_of(item):
        if plan["start"]:
            return None
        return ml_in[item][0:1, :], ml_in[item][1:2, :], acc_in[item]

    def put(item, m, total, acc):
        acc_out[item] = acc
        ml_out[item] = jnp.concatenate([m, total, jnp.zeros((6, ROWS), jnp.float32)], 0)

    def quick(item):
        tiles = [(ref, first, values, masked) for ref, values, n, masked in sources for first in range(0, n, KT)]
        old = old_of(item)
        if old is None:
            m, total, acc = None, None, None
        else:
            m, total, acc = old
        part = jnp.zeros((8, ROWS), jnp.float32)

        def scores_of(tile):
            return scores(tile[0], tile[1], item, tile[3])

        ahead = scores_of(tiles[0])
        for j, (ref, first, values, _) in enumerate(tiles):
            s = ahead
            if j + 1 < len(tiles):
                ahead = scores_of(tiles[j + 1])
            p = jnp.exp2(s) if m is None else jnp.exp2(s - m)
            part = part + jnp.sum(p.reshape(KT // 8, 8, ROWS), 0)
            pv = dot(v_tile(ref, values + first), p.astype(jnp.bfloat16))
            acc = pv if acc is None else acc + pv
        part = jnp.sum(part, 0, keepdims=True)
        if m is None:
            m, total = jnp.zeros((1, ROWS), jnp.float32), part
        else:
            total = total + part
        put(item, m, total, acc)

    def careful(item):
        old = old_of(item)
        if old is None:
            m = jnp.full((1, ROWS), LOW, jnp.float32)
            put(item, m, jnp.zeros((1, ROWS), jnp.float32), jnp.zeros((HEAD, ROWS), jnp.float32))
        else:
            put(item, *old)
        for ref, values, n, masked in sources:

            def step(t, carry, ref=ref, values=values, masked=masked):
                first = t * KT
                m, total, acc = ml_out[item][0:1, :], ml_out[item][1:2, :], acc_out[item]
                s = scores(ref, first, item, masked)
                top = jnp.maximum(m, jnp.max(s, 0, keepdims=True))
                back = jnp.exp2(m - top)
                p = jnp.where(s > 0.5 * LOW, jnp.exp2(s - top), 0.0)
                total = total * back + jnp.sum(p, 0, keepdims=True)
                acc = acc * back + dot(v_tile(ref, values + first), p.astype(jnp.bfloat16))
                put(item, top, total, acc)
                return carry

            lax.fori_loop(0, n // KT, step, 0)

    def everything(step):
        def body(item, carry):
            step(item)
            return carry

        if n_q == 1:
            step(0)
        else:
            lax.fori_loop(0, n_q, body, 0)

    everything(quick)
    fine = None
    for i in range(n_q):
        total = ml_out[i][1:2, :]
        good = jnp.where((total < TOO_BIG) & (total > TOO_SMALL), 1.0, 0.0)
        fine = good if fine is None else jnp.minimum(fine, good)

    @pl.when(jnp.min(fine) < 0.5)
    def _():
        everything(careful)

    if plan["finish"]:
        for i in range(n_q):
            m, total = ml_out[i][0:1, :], ml_out[i][1:2, :]
            out_refs[i][0:HEAD, :] = (acc_out[i] * (1.0 / total)).astype(jnp.bfloat16)
            out_refs[i][HEAD:, :] = coded_mass(m + jnp.log2(total))


def coded_mass(mass):
    a = mass.astype(jnp.bfloat16).astype(jnp.float32)
    b = (mass - a).astype(jnp.bfloat16).astype(jnp.float32)
    c = mass - a - b
    rows = lax.broadcasted_iota(jnp.int32, (META, ROWS), 0)
    return jnp.where(rows == 0, a, jnp.where(rows == 1, b, jnp.where(rows == 2, c, 0.0))).astype(jnp.bfloat16)


def attend(name, queries, kvs, state=None, fresh=(), finish=False, weight=1024):
    n_q = len(queries)
    plan = dict(n_q=n_q, n_kv=len(kvs), n_fresh=len(fresh), start=state is None, finish=finish)
    acc = jax.ShapeDtypeStruct((n_q, HEAD, ROWS), jnp.float32)
    ml = jax.ShapeDtypeStruct((n_q, 8, ROWS), jnp.float32)
    scratch = [pltpu.VMEM((n_q, HEAD + META, ROWS), jnp.bfloat16)]
    if fresh:
        scratch += [
            pltpu.VMEM((2 * len(fresh) * TOK, HEAD), jnp.bfloat16),
            pltpu.VMEM((len(fresh) * TOK, TOK), jnp.float32),
        ]
    if finish:
        outs = [jax.ShapeDtypeStruct((HEAD + META, ROWS), jnp.bfloat16)] * n_q
        scratch += [pltpu.VMEM(acc.shape, jnp.float32), pltpu.VMEM(ml.shape, jnp.float32)]
    else:
        outs = [acc, ml]
    args = list(queries) + list(kvs) + list(fresh) + list(state or ())
    pairs = n_q * (len(kvs) * CHUNK + len(fresh) * TOK) * ROWS
    return pl.pallas_call(
        functools.partial(attend_kernel, plan),
        out_shape=outs,
        in_specs=[VMEM] * len(args),
        out_specs=[VMEM] * len(outs),
        scratch_shapes=scratch,
        compiler_params=pltpu.CompilerParams(vmem_limit_bytes=24 * 2**20),
        cost_estimate=pl.CostEstimate(flops=pairs * weight, bytes_accessed=0, transcendentals=0),
        name=name,
    )(*args)


def combine_kernel(acc_ref, ml_ref, *refs):
    parts, (att_ref, mass_ref) = refs[:-2], refs[-2:]
    total = ml_ref[0][1:2, :]
    masses = [ml_ref[0][0:1, :] + jnp.log2(total)]
    for r in parts:
        rows = r[HEAD:, :].astype(jnp.float32)
        masses.append(rows[0:1, :] + rows[1:2, :] + rows[2:3, :])
    top = functools.reduce(jnp.maximum, masses)
    weights = [jnp.exp2(m - top) for m in masses]
    den = functools.reduce(jnp.add, weights)
    mass = (top + jnp.log2(den)) * LN2
    shares = [w / den for w in weights]
    shares[0] = shares[0] / total
    for g in range(GROUP):
        lanes = slice(g * TOK, (g + 1) * TOK)
        x = acc_ref[0, :, lanes] * shares[0][:, lanes]
        for r, w in zip(parts, shares[1:]):
            x = x + r[0:HEAD, lanes].astype(jnp.float32) * w[:, lanes]
        att_ref[:, lanes] = x.T.astype(jnp.bfloat16)
    mass_ref[...] = jnp.concatenate([mass[:, g * TOK : (g + 1) * TOK] for g in range(GROUP)], 0)


def prepare(name, kernel, shape, args, specs, work, scratch=()):
    return pl.pallas_call(
        kernel,
        out_shape=jax.ShapeDtypeStruct(shape, jnp.bfloat16),
        in_specs=specs,
        out_specs=VMEM,
        scratch_shapes=scratch,
        compiler_params=pltpu.CompilerParams(vmem_limit_bytes=8 * 2**20),
        cost_estimate=pl.CostEstimate(flops=work, bytes_accessed=0, transcendentals=0),
        name=name,
    )(*args)


def per_device(queries, k, v, fk, fv, positions, order, span):
    order = order.reshape(1, TOK)
    positions = positions.reshape(2 * CHUNK // TOK, TOK)
    q0 = prepare(
        "turn_queries",
        query_kernel,
        (HEAD + META, ROWS),
        (queries, order),
        [pl.BlockSpec(memory_space=pltpu.HBM)] * 2,
        10**9,
        [
            pltpu.VMEM((TOK, ROWS), jnp.bfloat16),
            pltpu.VMEM((1, TOK), jnp.int32),
            pltpu.SemaphoreType.DMA((2,)),
        ],
    )
    q_near = [shift(q0, "queries", -1), shift(q0, "queries", 1)]

    first = prepare(
        "turn_keys_first",
        functools.partial(key_kernel, 0),
        (PLACES + META, HEAD),
        (k, v, positions, fk, fv, order, span),
        [VMEM] * 6 + [SMEM],
        2 * 10**9,
    )
    first_near = [shift(first, "keys", -1), shift(first, "keys", 1)]
    second = prepare(
        "turn_keys_second",
        functools.partial(key_kernel, CHUNK),
        (2 * CHUNK, HEAD),
        (k, v, positions),
        [VMEM] * 3,
        2 * 10**9,
    )
    second_near = [shift(second, "keys", -1), shift(second, "keys", 1)]
    hold = lax.optimization_barrier
    mine = attend("mine_own", [q0], [first, second])
    mine, q_near = hold((mine, q_near))
    near = attend("near_own", q_near, [first, second])
    near, q0_late, behind = hold((near, q0, first_near[1]))
    q_far = shift(q0_late, "queries", 2)
    first_far = shift(behind, "keys", 1)
    near = attend("near_first", q_near, first_near, near)
    near, ahead = hold((near, second_near[0]))
    second_far = shift(ahead, "keys", -1)
    near = attend("near_second", q_near, second_near, near, weight=16)
    near, q_far = hold((near, q_far))
    far = attend("far", [q_far], [first, second, *first_near, *second_near], weight=16)
    fresh = [first, *first_near, first_far]
    near, far = hold((near, far))
    r_ahead, r_behind = attend("near_last", q_near, [first_far, second_far], near, fresh, finish=True)
    (r_far,) = attend("far_last", [q_far], [first_far, second_far], far, fresh, finish=True)
    back = [shift(r_far, "queries", 2), shift(r_ahead, "queries", 1), shift(r_behind, "queries", -1)]
    mine = attend("mine_rest", [q0], [*first_near, *second_near, first_far, second_far], mine, fresh)
    attended, mass = pl.pallas_call(
        combine_kernel,
        out_shape=[
            jax.ShapeDtypeStruct((TOK, GROUP * HEAD), jnp.bfloat16),
            jax.ShapeDtypeStruct((GROUP, TOK), jnp.float32),
        ],
        in_specs=[VMEM] * 5,
        out_specs=[VMEM] * 2,
        compiler_params=pltpu.CompilerParams(vmem_limit_bytes=8 * 2**20),
        name="combine",
    )(*mine, *back)
    return attended, mass.T


def solution(mesh):
    spec = (P("ctx", "tp"),) * 5 + (P("ctx"),) * 3
    return jax.shard_map(
        per_device,
        mesh=mesh,
        in_specs=spec,
        out_specs=(P("ctx", "tp"), P("ctx", "tp")),
        check_vma=False,
    )
```

```python
import functools

import jax
import jax.numpy as jnp
import ml_dtypes
import numpy as np
from jax import lax
from jax.experimental import pallas as pl
from jax.experimental.pallas import tpu as pltpu
from jax.sharding import PartitionSpec as P

GROUP = 8
HEAD = 128
TOK = 128
ROWS = GROUP * TOK
CACHED = 32768
SIDE = 4
CHUNK = 1024
TP = 8
KT = 256
LOG2E = 1.4426950408889634
LN2 = 0.6931471805599453
LOW = -1e30
TOO_BIG = 2.0**100
TOO_SMALL = 2.0**-60
META = 16

VMEM = pl.BlockSpec(memory_space=pltpu.VMEM)


def shift(block, kind, step):
    pairs = []
    for i in range(SIDE * SIDE):
        z, y = divmod(i, SIDE)
        for t in range(TP):
            if (t % 2 == 0) == (kind == "keys"):
                j = z * SIDE + (y + step) % SIDE
            else:
                j = ((z + step) % SIDE) * SIDE + y
            pairs.append((i * TP + t, j * TP + t))
    return lax.ppermute(block, ("ctx", "tp"), pairs)


def _bf(x):
    return np.asarray(x, np.float32).astype(ml_dtypes.bfloat16).astype(np.float64)


def _fit():
    t = np.cos(np.linspace(0, np.pi, 4001)) * 0.5
    u = t * t
    cos = np.polynomial.polynomial.polyfit(u, np.cos(2 * np.pi * t), 8)
    good = np.abs(t) > 1e-3
    sin = np.polynomial.polynomial.polyfit(u[good], np.sin(2 * np.pi * t[good]) / t[good], 7)
    return [float(c) for c in cos], [float(c) for c in sin]


COS, SIN = _fit()


def _turns():
    turns = 500000.0 ** (-2.0 * np.arange(64) / HEAD) / (2 * np.pi)
    first = _bf(turns)
    second = _bf(turns - first)
    return [[float(x) for x in piece] for piece in (first, second, turns - first - second)]


TURNS = _turns()


def spread(constants):
    row = lax.broadcasted_iota(jnp.int32, (8, TOK), 0)
    tiles = []
    for first in range(0, 64, 8):
        tile = jnp.full((8, TOK), constants[first + 7], jnp.float32)
        for i in range(7):
            tile = jnp.where(row == i, constants[first + i], tile)
        tiles.append(tile)
    return jnp.concatenate(tiles, 0)


def angles(positions, turns):
    a = positions * turns[0]
    a = a - jnp.round(a)
    b = positions * turns[1]
    t = a + (b - jnp.round(b)) + positions * turns[2]
    t = t - jnp.round(t)
    u = t * t
    cos = jnp.full_like(u, COS[-1])
    for c in COS[-2::-1]:
        cos = cos * u + c
    sin = jnp.full_like(u, SIN[-1])
    for c in SIN[-2::-1]:
        sin = sin * u + c
    return cos, sin * t


def turned(x, cos, sin):
    lower, upper = x[:64], x[64:]
    return jnp.concatenate([lower * cos - upper * sin, upper * cos + lower * sin], 0)


def coded(places):
    high = jnp.right_shift(places, 4)
    rows = lax.broadcasted_iota(jnp.int32, (META, TOK), 0)
    both = jnp.where(rows == 0, high, jnp.where(rows == 1, places - high * 16, 0))
    return both.astype(jnp.float32).astype(jnp.bfloat16)


def places_of(meta):
    meta = meta.astype(jnp.float32)
    return meta[0:1, :] * 16.0 + meta[1:2, :]


def query_kernel(q_any, order_any, out_ref, q_ref, order_ref, sems):
    copies = [
        pltpu.make_async_copy(q_any, q_ref, sems.at[0]),
        pltpu.make_async_copy(order_any, order_ref, sems.at[1]),
    ]
    for c in copies:
        c.start()
    turns = [spread(piece) for piece in TURNS]
    for c in copies[::-1]:
        c.wait()
    cos, sin = angles((order_ref[...] + CACHED).astype(jnp.float32), turns)
    scale = HEAD**-0.5 * LOG2E
    cos, sin = cos * scale, sin * scale
    for g in range(GROUP):
        lanes = slice(g * HEAD, (g + 1) * HEAD)
        x = q_ref[:, lanes].astype(jnp.float32).T
        out_ref[0:HEAD, lanes] = turned(x, cos, sin).astype(jnp.bfloat16)
    out_ref[HEAD:, :] = jnp.concatenate([coded(order_ref[...])] * GROUP, 1)


FRESH_KEYS = 2 * CHUNK
FRESH_VALUES = FRESH_KEYS + TOK
PLACES = FRESH_VALUES + TOK


def key_kernel(start, k_ref, v_ref, pos_ref, *refs):
    out_ref = refs[-1]
    turns = [spread(piece) for piece in TURNS]

    def keys(x, positions):
        cos, sin = angles(positions.astype(jnp.float32), turns)
        return turned(x.astype(jnp.float32).T, cos, sin).T.astype(jnp.bfloat16)

    def values(x):
        return x.astype(jnp.float32).T.astype(jnp.bfloat16)

    if len(refs) > 1:
        fk_ref, fv_ref, order_ref, span_ref = refs[:-1]
        order = order_ref[...]
        out_ref[FRESH_KEYS:FRESH_VALUES, :] = keys(fk_ref[...], order + CACHED)
        out_ref[FRESH_VALUES:PLACES, :] = values(fv_ref[...])
        lane = lax.broadcasted_iota(jnp.int32, (1, TOK), 1)
        out_ref[PLACES:, :] = coded(jnp.where(lane < span_ref[...], order, 4000))
    for b in range(CHUNK // TOK):
        rows = slice(start + b * TOK, start + (b + 1) * TOK)
        tile = start // TOK + b
        out_ref[b * TOK : (b + 1) * TOK, :] = keys(k_ref[rows, :], pos_ref[tile : tile + 1, :])
        out_ref[CHUNK + b * TOK : CHUNK + (b + 1) * TOK, :] = values(v_ref[rows, :])


def dot(a, b):
    return lax.dot_general(a, b, (((1,), (0,)), ((), ())), preferred_element_type=jnp.float32)


def attend_kernel(plan, *refs):
    it = iter(refs)
    n_q, n_fresh = plan["n_q"], plan["n_fresh"]
    q_refs = [next(it) for _ in range(n_q)]
    kv_refs = [next(it) for _ in range(plan["n_kv"])]
    fresh_refs = [next(it) for _ in range(n_fresh)]
    if not plan["start"]:
        acc_in, ml_in = next(it), next(it)
    if plan["finish"]:
        out_refs = [next(it) for _ in range(n_q)]
    else:
        acc_out, ml_out = next(it), next(it)
    q_s = next(it)
    if n_fresh:
        f_s, place_s = next(it), next(it)
    if plan["finish"]:
        acc_out, ml_out = next(it), next(it)

    for i, r in enumerate(q_refs):
        q_s[i] = r[...]
    for i, r in enumerate(fresh_refs):
        f_s[i * TOK : (i + 1) * TOK, :] = r[FRESH_KEYS:FRESH_VALUES, :]
        f_s[(n_fresh + i) * TOK : (n_fresh + i + 1) * TOK, :] = r[FRESH_VALUES:PLACES, :]
        place_s[i * TOK : (i + 1) * TOK, :] = jnp.broadcast_to(places_of(r[PLACES:, :]), (TOK, TOK)).T

    def aligned(i):
        return i if isinstance(i, int) else pl.multiple_of(i, TOK)

    def k_tile(ref, first):
        return ref[pl.ds(aligned(first), KT), :]

    def v_tile(ref, first):
        return jnp.concatenate([ref[pl.ds(aligned(first + j * TOK), TOK), :] for j in range(KT // TOK)], 1)

    def scores(ref, first, item, masked):
        s = dot(k_tile(ref, first), q_s[item, 0:HEAD, :])
        if masked:
            mine = places_of(q_s[item, HEAD:, 0:TOK])
            mask = place_s[pl.ds(aligned(first), KT), :] <= mine
            s = jnp.where(jnp.concatenate([mask] * GROUP, 1), s, LOW)
        return s

    sources = [(ref, CHUNK, CHUNK, False) for ref in kv_refs]
    if n_fresh:
        sources.append((f_s, n_fresh * TOK, n_fresh * TOK, True))

    def old_of(item):
        if plan["start"]:
            return None
        at = item + plan["skip"]
        return ml_in[at][0:1, :], ml_in[at][1:2, :], acc_in[at]

    def put(item, m, total, acc):
        acc_out[item] = acc
        ml_out[item] = jnp.concatenate([m, total, jnp.zeros((6, ROWS), jnp.float32)], 0)

    def quick(item):
        tiles = [(ref, first, values, masked) for ref, values, n, masked in sources for first in range(0, n, KT)]
        old = old_of(item)
        if old is None:
            m, total, acc = None, None, None
        else:
            m, total, acc = old
        part = jnp.zeros((8, ROWS), jnp.float32)

        def scores_of(tile):
            return scores(tile[0], tile[1], item, tile[3])

        ahead = scores_of(tiles[0])
        for j, (ref, first, values, _) in enumerate(tiles):
            s = ahead
            if j + 1 < len(tiles):
                ahead = scores_of(tiles[j + 1])
            p = jnp.exp2(s) if m is None else jnp.exp2(s - m)
            part = part + jnp.sum(p.reshape(KT // 8, 8, ROWS), 0)
            pv = dot(v_tile(ref, values + first), p.astype(jnp.bfloat16))
            acc = pv if acc is None else acc + pv
        part = jnp.sum(part, 0, keepdims=True)
        if m is None:
            m, total = jnp.zeros((1, ROWS), jnp.float32), part
        else:
            total = total + part
        put(item, m, total, acc)

    def careful(item):
        old = old_of(item)
        if old is None:
            m = jnp.full((1, ROWS), LOW, jnp.float32)
            put(item, m, jnp.zeros((1, ROWS), jnp.float32), jnp.zeros((HEAD, ROWS), jnp.float32))
        else:
            put(item, *old)
        for ref, values, n, masked in sources:

            def step(t, carry, ref=ref, values=values, masked=masked):
                first = t * KT
                m, total, acc = ml_out[item][0:1, :], ml_out[item][1:2, :], acc_out[item]
                s = scores(ref, first, item, masked)
                top = jnp.maximum(m, jnp.max(s, 0, keepdims=True))
                back = jnp.exp2(m - top)
                p = jnp.where(s > 0.5 * LOW, jnp.exp2(s - top), 0.0)
                total = total * back + jnp.sum(p, 0, keepdims=True)
                acc = acc * back + dot(v_tile(ref, values + first), p.astype(jnp.bfloat16))
                put(item, top, total, acc)
                return carry

            lax.fori_loop(0, n // KT, step, 0)

    def everything(step):
        def body(item, carry):
            step(item)
            return carry

        if n_q == 1:
            step(0)
        else:
            lax.fori_loop(0, n_q, body, 0)

    everything(quick)
    fine = None
    for i in range(n_q):
        total = ml_out[i][1:2, :]
        good = jnp.where((total < TOO_BIG) & (total > TOO_SMALL), 1.0, 0.0)
        fine = good if fine is None else jnp.minimum(fine, good)

    @pl.when(jnp.min(fine) < 0.5)
    def _():
        everything(careful)

    if plan["finish"]:
        for i in range(n_q):
            m, total = ml_out[i][0:1, :], ml_out[i][1:2, :]
            out_refs[i][0:HEAD, :] = (acc_out[i] * (1.0 / total)).astype(jnp.bfloat16)
            out_refs[i][HEAD:, :] = coded_mass(m + jnp.log2(total))


def coded_mass(mass):
    a = mass.astype(jnp.bfloat16).astype(jnp.float32)
    b = (mass - a).astype(jnp.bfloat16).astype(jnp.float32)
    c = mass - a - b
    rows = lax.broadcasted_iota(jnp.int32, (META, ROWS), 0)
    return jnp.where(rows == 0, a, jnp.where(rows == 1, b, jnp.where(rows == 2, c, 0.0))).astype(jnp.bfloat16)


def attend(name, queries, kvs, state=None, fresh=(), finish=False, skip=0):
    n_q = len(queries)
    plan = dict(n_q=n_q, n_kv=len(kvs), n_fresh=len(fresh), start=state is None, finish=finish, skip=skip)
    acc = jax.ShapeDtypeStruct((n_q, HEAD, ROWS), jnp.float32)
    ml = jax.ShapeDtypeStruct((n_q, 8, ROWS), jnp.float32)
    scratch = [pltpu.VMEM((n_q, HEAD + META, ROWS), jnp.bfloat16)]
    if fresh:
        scratch += [
            pltpu.VMEM((2 * len(fresh) * TOK, HEAD), jnp.bfloat16),
            pltpu.VMEM((len(fresh) * TOK, TOK), jnp.float32),
        ]
    if finish:
        outs = [jax.ShapeDtypeStruct((HEAD + META, ROWS), jnp.bfloat16)] * n_q
        scratch += [pltpu.VMEM(acc.shape, jnp.float32), pltpu.VMEM(ml.shape, jnp.float32)]
    else:
        outs = [acc, ml]
    args = list(queries) + list(kvs) + list(fresh) + list(state or ())
    pairs = n_q * (len(kvs) * CHUNK + len(fresh) * TOK) * ROWS
    return pl.pallas_call(
        functools.partial(attend_kernel, plan),
        out_shape=outs,
        in_specs=[VMEM] * len(args),
        out_specs=[VMEM] * len(outs),
        scratch_shapes=scratch,
        compiler_params=pltpu.CompilerParams(vmem_limit_bytes=24 * 2**20),
        cost_estimate=pl.CostEstimate(flops=pairs * 1024, bytes_accessed=0, transcendentals=0),
        name=name,
    )(*args)


def combine_kernel(acc_ref, ml_ref, *refs):
    parts, (att_ref, mass_ref) = refs[:-2], refs[-2:]
    total = ml_ref[0][1:2, :]
    masses = [ml_ref[0][0:1, :] + jnp.log2(total)]
    for r in parts:
        rows = r[HEAD:, :].astype(jnp.float32)
        masses.append(rows[0:1, :] + rows[1:2, :] + rows[2:3, :])
    top = functools.reduce(jnp.maximum, masses)
    weights = [jnp.exp2(m - top) for m in masses]
    den = functools.reduce(jnp.add, weights)
    mass = (top + jnp.log2(den)) * LN2
    shares = [w / den for w in weights]
    shares[0] = shares[0] / total
    for g in range(GROUP):
        lanes = slice(g * TOK, (g + 1) * TOK)
        x = acc_ref[0, :, lanes] * shares[0][:, lanes]
        for r, w in zip(parts, shares[1:]):
            x = x + r[0:HEAD, lanes].astype(jnp.float32) * w[:, lanes]
        att_ref[:, lanes] = x.T.astype(jnp.bfloat16)
    mass_ref[...] = jnp.concatenate([mass[:, g * TOK : (g + 1) * TOK] for g in range(GROUP)], 0)


def prepare(name, kernel, shape, args, specs, work, scratch=()):
    return pl.pallas_call(
        kernel,
        out_shape=jax.ShapeDtypeStruct(shape, jnp.bfloat16),
        in_specs=specs,
        out_specs=VMEM,
        scratch_shapes=scratch,
        compiler_params=pltpu.CompilerParams(vmem_limit_bytes=8 * 2**20),
        cost_estimate=pl.CostEstimate(flops=work, bytes_accessed=0, transcendentals=0),
        name=name,
    )(*args)


def per_device(queries, k, v, fk, fv, positions, order, span):
    order = order.reshape(1, TOK)
    positions = positions.reshape(2 * CHUNK // TOK, TOK)
    q0 = prepare(
        "turn_queries",
        query_kernel,
        (HEAD + META, ROWS),
        (queries, order),
        [pl.BlockSpec(memory_space=pltpu.HBM)] * 2,
        10**9,
        [
            pltpu.VMEM((TOK, ROWS), jnp.bfloat16),
            pltpu.VMEM((1, TOK), jnp.int32),
            pltpu.SemaphoreType.DMA((2,)),
        ],
    )
    q_near = [shift(q0, "queries", -1), shift(q0, "queries", 1)]
    q_far = shift(q0, "queries", 2)

    first = prepare(
        "turn_keys_first",
        functools.partial(key_kernel, 0),
        (PLACES + META, HEAD),
        (k, v, positions, fk, fv, order, span.reshape(1, 1)),
        [VMEM] * 7,
        2 * 10**9,
    )
    first_near = [shift(first, "keys", -1), shift(first, "keys", 1)]
    second = prepare(
        "turn_keys_second",
        functools.partial(key_kernel, CHUNK),
        (2 * CHUNK, HEAD),
        (k, v, positions),
        [VMEM] * 3,
        2 * 10**9,
    )
    second_near = [shift(second, "keys", -1), shift(second, "keys", 1)]
    others = [q_far, *q_near]
    mine = attend("mine_own", [q0], [first, second])
    state = attend("others_own", others, [first, second])
    first_far = shift(first_near[1], "keys", 1)
    fresh = [first, *first_near, first_far]
    state = attend("others_first", others, first_near, state)
    state, ahead = lax.optimization_barrier((state, second_near[0]))
    second_far = shift(ahead, "keys", -1)
    state = attend("others_second", others, [*second_near, first_far], state)
    r_ahead, r_behind = attend("near_last", q_near, [second_far], state, fresh, finish=True, skip=1)
    (r_far,) = attend("far_last", [q_far], [second_far], state, fresh, finish=True)
    back = [shift(r_far, "queries", 2), shift(r_ahead, "queries", 1), shift(r_behind, "queries", -1)]
    mine = attend("mine_rest", [q0], [*first_near, *second_near, first_far, second_far], mine, fresh)
    attended, mass = pl.pallas_call(
        combine_kernel,
        out_shape=[
            jax.ShapeDtypeStruct((TOK, GROUP * HEAD), jnp.bfloat16),
            jax.ShapeDtypeStruct((GROUP, TOK), jnp.float32),
        ],
        in_specs=[VMEM] * 5,
        out_specs=[VMEM] * 2,
        compiler_params=pltpu.CompilerParams(vmem_limit_bytes=8 * 2**20),
        name="combine",
    )(*mine, *back)
    return attended, mass.T


def solution(mesh):
    spec = (P("ctx", "tp"),) * 5 + (P("ctx"),) * 3
    return jax.shard_map(
        per_device,
        mesh=mesh,
        in_specs=spec,
        out_specs=(P("ctx", "tp"), P("ctx", "tp")),
        check_vma=False,
    )
```

```python
import functools

import jax
import jax.numpy as jnp
import ml_dtypes
import numpy as np
from jax import lax
from jax.experimental import pallas as pl
from jax.experimental.pallas import tpu as pltpu
from jax.sharding import PartitionSpec as P

GROUP = 8
HEAD = 128
TOK = 128
ROWS = GROUP * TOK
CACHED = 32768
SIDE = 4
CHUNK = 1024
TP = 8
KT = 256
LOG2E = 1.4426950408889634
LN2 = 0.6931471805599453
LOW = -1e30
TOO_BIG = 2.0**100
TOO_SMALL = 2.0**-60
META = 16

VMEM = pl.BlockSpec(memory_space=pltpu.VMEM)


def shift(block, kind, step):
    pairs = []
    for i in range(SIDE * SIDE):
        z, y = divmod(i, SIDE)
        for t in range(TP):
            if (t % 2 == 0) == (kind == "keys"):
                j = z * SIDE + (y + step) % SIDE
            else:
                j = ((z + step) % SIDE) * SIDE + y
            pairs.append((i * TP + t, j * TP + t))
    return lax.ppermute(block, ("ctx", "tp"), pairs)


def _bf(x):
    return np.asarray(x, np.float32).astype(ml_dtypes.bfloat16).astype(np.float64)


def _fit():
    t = np.cos(np.linspace(0, np.pi, 4001)) * 0.5
    u = t * t
    cos = np.polynomial.polynomial.polyfit(u, np.cos(2 * np.pi * t), 8)
    good = np.abs(t) > 1e-3
    sin = np.polynomial.polynomial.polyfit(u[good], np.sin(2 * np.pi * t[good]) / t[good], 7)
    return [float(c) for c in cos], [float(c) for c in sin]


COS, SIN = _fit()


def _turns():
    turns = 500000.0 ** (-2.0 * np.arange(64) / HEAD) / (2 * np.pi)
    first = _bf(turns)
    second = _bf(turns - first)
    return [[float(x) for x in piece] for piece in (first, second, turns - first - second)]


TURNS = _turns()


def spread(constants):
    row = lax.broadcasted_iota(jnp.int32, (8, TOK), 0)
    tiles = []
    for first in range(0, 64, 8):
        tile = jnp.full((8, TOK), constants[first + 7], jnp.float32)
        for i in range(7):
            tile = jnp.where(row == i, constants[first + i], tile)
        tiles.append(tile)
    return jnp.concatenate(tiles, 0)


def angles(positions, turns):
    a = positions * turns[0]
    a = a - jnp.round(a)
    b = positions * turns[1]
    t = a + (b - jnp.round(b)) + positions * turns[2]
    t = t - jnp.round(t)
    u = t * t
    cos = jnp.full_like(u, COS[-1])
    for c in COS[-2::-1]:
        cos = cos * u + c
    sin = jnp.full_like(u, SIN[-1])
    for c in SIN[-2::-1]:
        sin = sin * u + c
    return cos, sin * t


def turned(x, cos, sin):
    lower, upper = x[:64], x[64:]
    return jnp.concatenate([lower * cos - upper * sin, upper * cos + lower * sin], 0)


def coded(places):
    high = jnp.right_shift(places, 4)
    rows = lax.broadcasted_iota(jnp.int32, (META, TOK), 0)
    both = jnp.where(rows == 0, high, jnp.where(rows == 1, places - high * 16, 0))
    return both.astype(jnp.float32).astype(jnp.bfloat16)


def places_of(meta):
    meta = meta.astype(jnp.float32)
    return meta[0:1, :] * 16.0 + meta[1:2, :]


def angle_kernel(places_ref, out_ref):
    order = places_ref[0:1, :]
    turns = [spread(piece) for piece in TURNS]
    cos, sin = angles((order + CACHED).astype(jnp.float32), turns)
    scale = HEAD**-0.5 * LOG2E
    out_ref[0:64, :] = cos * scale
    out_ref[64:128, :] = sin * scale
    out_ref[128:, :] = coded(order).astype(jnp.float32)


def query_kernel(q_ref, angle_ref, out_ref):
    cos, sin = angle_ref[0:64, :], angle_ref[64:128, :]
    for g in range(GROUP):
        lanes = slice(g * HEAD, (g + 1) * HEAD)
        x = q_ref[:, lanes].astype(jnp.float32).T
        out_ref[0:HEAD, lanes] = turned(x, cos, sin).astype(jnp.bfloat16)
    out_ref[HEAD:, :] = jnp.concatenate([angle_ref[128:, :].astype(jnp.bfloat16)] * GROUP, 1)


FRESH_KEYS = 2 * CHUNK
FRESH_VALUES = FRESH_KEYS + TOK
PLACES = FRESH_VALUES + TOK


def key_kernel(start, k_ref, v_ref, pos_ref, *refs):
    with_fresh = len(refs) > 1
    if with_fresh:
        fk_ref, fv_ref, places_ref, out_ref = refs
    else:
        (out_ref,) = refs
    turns = [spread(piece) for piece in TURNS]

    def keys(x, positions):
        cos, sin = angles(positions.astype(jnp.float32), turns)
        return turned(x.astype(jnp.float32).T, cos, sin).T.astype(jnp.bfloat16)

    def values(x):
        return x.astype(jnp.float32).T.astype(jnp.bfloat16)

    for b in range(CHUNK // TOK):
        rows = slice(start + b * TOK, start + (b + 1) * TOK)
        tile = start // TOK + b
        out_ref[b * TOK : (b + 1) * TOK, :] = keys(k_ref[rows, :], pos_ref[tile : tile + 1, :])
        out_ref[CHUNK + b * TOK : CHUNK + (b + 1) * TOK, :] = values(v_ref[rows, :])
    if with_fresh:
        order, span = places_ref[0:1, :], places_ref[1:2, 0:1]
        out_ref[FRESH_KEYS:FRESH_VALUES, :] = keys(fk_ref[...], order + CACHED)
        out_ref[FRESH_VALUES:PLACES, :] = values(fv_ref[...])
        lane = lax.broadcasted_iota(jnp.int32, (1, TOK), 1)
        out_ref[PLACES:, :] = coded(jnp.where(lane < span, order, 4000))


def dot(a, b):
    return lax.dot_general(a, b, (((1,), (0,)), ((), ())), preferred_element_type=jnp.float32)


def attend_kernel(plan, *refs):
    it = iter(refs)
    n_q, n_fresh = plan["n_q"], plan["n_fresh"]
    q_refs = [next(it) for _ in range(n_q)]
    kv_refs = [next(it) for _ in range(plan["n_kv"])]
    fresh_refs = [next(it) for _ in range(n_fresh)]
    if not plan["start"]:
        acc_in, ml_in = next(it), next(it)
    if plan["finish"]:
        out_refs = [next(it) for _ in range(n_q)]
    else:
        acc_out, ml_out = next(it), next(it)
    q_s = next(it)
    if n_fresh:
        f_s, place_s = next(it), next(it)
    if plan["finish"]:
        acc_out, ml_out = next(it), next(it)

    for i, r in enumerate(q_refs):
        q_s[i] = r[...]
    for i, r in enumerate(fresh_refs):
        f_s[i * TOK : (i + 1) * TOK, :] = r[FRESH_KEYS:FRESH_VALUES, :]
        f_s[(n_fresh + i) * TOK : (n_fresh + i + 1) * TOK, :] = r[FRESH_VALUES:PLACES, :]
        place_s[i * TOK : (i + 1) * TOK, :] = jnp.broadcast_to(places_of(r[PLACES:, :]), (TOK, TOK)).T

    def aligned(i):
        return i if isinstance(i, int) else pl.multiple_of(i, TOK)

    def k_tile(ref, first):
        return ref[pl.ds(aligned(first), KT), :]

    def v_tile(ref, first):
        return jnp.concatenate([ref[pl.ds(aligned(first + j * TOK), TOK), :] for j in range(KT // TOK)], 1)

    def scores(ref, first, item, masked):
        s = dot(k_tile(ref, first), q_s[item, 0:HEAD, :])
        if masked:
            mine = places_of(q_s[item, HEAD:, 0:TOK])
            mask = place_s[pl.ds(aligned(first), KT), :] <= mine
            s = jnp.where(jnp.concatenate([mask] * GROUP, 1), s, LOW)
        return s

    sources = [(ref, CHUNK, CHUNK, False) for ref in kv_refs]
    if n_fresh:
        sources.append((f_s, n_fresh * TOK, n_fresh * TOK, True))

    def old_of(item):
        if plan["start"]:
            return None
        return ml_in[item][0:1, :], ml_in[item][1:2, :], acc_in[item]

    def put(item, m, total, acc):
        acc_out[item] = acc
        ml_out[item] = jnp.concatenate([m, total, jnp.zeros((6, ROWS), jnp.float32)], 0)

    def quick(item):
        tiles = [(ref, first, values, masked) for ref, values, n, masked in sources for first in range(0, n, KT)]
        old = old_of(item)
        if old is None:
            m, total, acc = None, None, None
        else:
            m, total, acc = old
        part = jnp.zeros((8, ROWS), jnp.float32)

        def scores_of(tile):
            return scores(tile[0], tile[1], item, tile[3])

        ahead = scores_of(tiles[0])
        for j, (ref, first, values, _) in enumerate(tiles):
            s = ahead
            if j + 1 < len(tiles):
                ahead = scores_of(tiles[j + 1])
            p = jnp.exp2(s) if m is None else jnp.exp2(s - m)
            part = part + jnp.sum(p.reshape(KT // 8, 8, ROWS), 0)
            pv = dot(v_tile(ref, values + first), p.astype(jnp.bfloat16))
            acc = pv if acc is None else acc + pv
        part = jnp.sum(part, 0, keepdims=True)
        if m is None:
            m, total = jnp.zeros((1, ROWS), jnp.float32), part
        else:
            total = total + part
        put(item, m, total, acc)

    def careful(item):
        old = old_of(item)
        if old is None:
            m = jnp.full((1, ROWS), LOW, jnp.float32)
            put(item, m, jnp.zeros((1, ROWS), jnp.float32), jnp.zeros((HEAD, ROWS), jnp.float32))
        else:
            put(item, *old)
        for ref, values, n, masked in sources:

            def step(t, carry, ref=ref, values=values, masked=masked):
                first = t * KT
                m, total, acc = ml_out[item][0:1, :], ml_out[item][1:2, :], acc_out[item]
                s = scores(ref, first, item, masked)
                top = jnp.maximum(m, jnp.max(s, 0, keepdims=True))
                back = jnp.exp2(m - top)
                p = jnp.where(s > 0.5 * LOW, jnp.exp2(s - top), 0.0)
                total = total * back + jnp.sum(p, 0, keepdims=True)
                acc = acc * back + dot(v_tile(ref, values + first), p.astype(jnp.bfloat16))
                put(item, top, total, acc)
                return carry

            lax.fori_loop(0, n // KT, step, 0)

    def everything(step):
        def body(item, carry):
            step(item)
            return carry

        if n_q == 1:
            step(0)
        else:
            lax.fori_loop(0, n_q, body, 0)

    everything(quick)
    fine = None
    for i in range(n_q):
        total = ml_out[i][1:2, :]
        good = jnp.where((total < TOO_BIG) & (total > TOO_SMALL), 1.0, 0.0)
        fine = good if fine is None else jnp.minimum(fine, good)

    @pl.when(jnp.min(fine) < 0.5)
    def _():
        everything(careful)

    if plan["finish"]:
        for i in range(n_q):
            m, total = ml_out[i][0:1, :], ml_out[i][1:2, :]
            out_refs[i][0:HEAD, :] = (acc_out[i] * (1.0 / total)).astype(jnp.bfloat16)
            out_refs[i][HEAD:, :] = coded_mass(m + jnp.log2(total))


def coded_mass(mass):
    a = mass.astype(jnp.bfloat16).astype(jnp.float32)
    b = (mass - a).astype(jnp.bfloat16).astype(jnp.float32)
    c = mass - a - b
    rows = lax.broadcasted_iota(jnp.int32, (META, ROWS), 0)
    return jnp.where(rows == 0, a, jnp.where(rows == 1, b, jnp.where(rows == 2, c, 0.0))).astype(jnp.bfloat16)


def attend(name, queries, kvs, state=None, fresh=(), finish=False, weight=1024):
    n_q = len(queries)
    plan = dict(n_q=n_q, n_kv=len(kvs), n_fresh=len(fresh), start=state is None, finish=finish)
    acc = jax.ShapeDtypeStruct((n_q, HEAD, ROWS), jnp.float32)
    ml = jax.ShapeDtypeStruct((n_q, 8, ROWS), jnp.float32)
    scratch = [pltpu.VMEM((n_q, HEAD + META, ROWS), jnp.bfloat16)]
    if fresh:
        scratch += [
            pltpu.VMEM((2 * len(fresh) * TOK, HEAD), jnp.bfloat16),
            pltpu.VMEM((len(fresh) * TOK, TOK), jnp.float32),
        ]
    if finish:
        outs = [jax.ShapeDtypeStruct((HEAD + META, ROWS), jnp.bfloat16)] * n_q
        scratch += [pltpu.VMEM(acc.shape, jnp.float32), pltpu.VMEM(ml.shape, jnp.float32)]
    else:
        outs = [acc, ml]
    args = list(queries) + list(kvs) + list(fresh) + list(state or ())
    pairs = n_q * (len(kvs) * CHUNK + len(fresh) * TOK) * ROWS
    return pl.pallas_call(
        functools.partial(attend_kernel, plan),
        out_shape=outs,
        in_specs=[VMEM] * len(args),
        out_specs=[VMEM] * len(outs),
        scratch_shapes=scratch,
        compiler_params=pltpu.CompilerParams(vmem_limit_bytes=24 * 2**20),
        cost_estimate=pl.CostEstimate(flops=pairs * weight, bytes_accessed=0, transcendentals=0),
        name=name,
    )(*args)


def combine_kernel(acc_ref, ml_ref, *refs):
    parts, (att_ref, mass_ref) = refs[:-2], refs[-2:]
    total = ml_ref[0][1:2, :]
    masses = [ml_ref[0][0:1, :] + jnp.log2(total)]
    for r in parts:
        rows = r[HEAD:, :].astype(jnp.float32)
        masses.append(rows[0:1, :] + rows[1:2, :] + rows[2:3, :])
    top = functools.reduce(jnp.maximum, masses)
    weights = [jnp.exp2(m - top) for m in masses]
    den = functools.reduce(jnp.add, weights)
    mass = (top + jnp.log2(den)) * LN2
    shares = [w / den for w in weights]
    shares[0] = shares[0] / total
    for g in range(GROUP):
        lanes = slice(g * TOK, (g + 1) * TOK)
        x = acc_ref[0, :, lanes] * shares[0][:, lanes]
        for r, w in zip(parts, shares[1:]):
            x = x + r[0:HEAD, lanes].astype(jnp.float32) * w[:, lanes]
        att_ref[:, lanes] = x.T.astype(jnp.bfloat16)
    mass_ref[...] = jnp.concatenate([mass[:, g * TOK : (g + 1) * TOK] for g in range(GROUP)], 0)


def prepare(name, kernel, shape, args, specs, work, scratch=()):
    return pl.pallas_call(
        kernel,
        out_shape=jax.ShapeDtypeStruct(shape, jnp.bfloat16),
        in_specs=specs,
        out_specs=VMEM,
        scratch_shapes=scratch,
        compiler_params=pltpu.CompilerParams(vmem_limit_bytes=8 * 2**20),
        cost_estimate=pl.CostEstimate(flops=work, bytes_accessed=0, transcendentals=0),
        name=name,
    )(*args)


def per_device(queries, k, v, fk, fv, positions, order, span):
    places = jnp.concatenate([order, lax.pad(span, jnp.int32(0), [(0, TOK - 1, 0)])]).reshape(2, TOK)
    positions = positions.reshape(2 * CHUNK // TOK, TOK)
    angle = pl.pallas_call(
        angle_kernel,
        out_shape=jax.ShapeDtypeStruct((HEAD + META, TOK), jnp.float32),
        in_specs=[VMEM],
        out_specs=VMEM,
        compiler_params=pltpu.CompilerParams(vmem_limit_bytes=8 * 2**20),
        cost_estimate=pl.CostEstimate(flops=10**9, bytes_accessed=0, transcendentals=0),
        name="angles",
    )(places)
    q0 = prepare("turn_queries", query_kernel, (HEAD + META, ROWS), (queries, angle), [VMEM] * 2, 10**9)
    q_near = [shift(q0, "queries", -1), shift(q0, "queries", 1)]

    first = prepare(
        "turn_keys_first",
        functools.partial(key_kernel, 0),
        (PLACES + META, HEAD),
        (k, v, positions, fk, fv, places),
        [VMEM] * 6,
        2 * 10**9,
    )
    first_near = [shift(first, "keys", -1), shift(first, "keys", 1)]
    second = prepare(
        "turn_keys_second",
        functools.partial(key_kernel, CHUNK),
        (2 * CHUNK, HEAD),
        (k, v, positions),
        [VMEM] * 3,
        2 * 10**9,
    )

    hold = lax.optimization_barrier
    second, q0_late = hold((second, q0))
    q_far = shift(q0_late, "queries", 2)
    mine = attend("mine_own", [q0], [first, second])
    near = attend("near_own", q_near, [first, second])
    near, second_late = hold((near, second))
    second_near = [shift(second_late, "keys", -1), shift(second_late, "keys", 1)]
    far = attend("far_own", [q_far], [first, second])
    near = attend("near_first", q_near, first_near, near)
    far = attend("far_first", [q_far], first_near, far)
    near, far, mine, behind, ahead = hold((near, far, mine, first_near[1], second_near[0]))
    first_far = shift(behind, "keys", 1)
    second_far = shift(ahead, "keys", -1)
    near = attend("near_second", q_near, second_near, near)
    far = attend("far_second", [q_far], second_near, far)
    mine = attend("mine_first", [q0], first_near, mine)
    near, far, mine = hold((near, far, mine))
    fresh = [first, *first_near, first_far]
    r_ahead, r_behind = attend("near_last", q_near, [first_far, second_far], near, fresh, finish=True)
    (r_far,) = attend("far_last", [q_far], [first_far, second_far], far, fresh, finish=True)
    back = [shift(r_far, "queries", 2), shift(r_ahead, "queries", 1), shift(r_behind, "queries", -1)]
    mine = attend("mine_rest", [q0], [*second_near, first_far, second_far], mine, fresh)
    attended, mass = pl.pallas_call(
        combine_kernel,
        out_shape=[
            jax.ShapeDtypeStruct((TOK, GROUP * HEAD), jnp.bfloat16),
            jax.ShapeDtypeStruct((GROUP, TOK), jnp.float32),
        ],
        in_specs=[VMEM] * 5,
        out_specs=[VMEM] * 2,
        compiler_params=pltpu.CompilerParams(vmem_limit_bytes=8 * 2**20),
        name="combine",
    )(*mine, *back)
    return attended, mass.T


def solution(mesh):
    spec = (P("ctx", "tp"),) * 5 + (P("ctx"),) * 3
    return jax.shard_map(
        per_device,
        mesh=mesh,
        in_specs=spec,
        out_specs=(P("ctx", "tp"), P("ctx", "tp")),
        check_vma=False,
    )
```

```python
import functools

import jax
import jax.numpy as jnp
import ml_dtypes
import numpy as np
from jax import lax
from jax.experimental import pallas as pl
from jax.experimental.pallas import tpu as pltpu
from jax.sharding import PartitionSpec as P

GROUP = 8
HEAD = 128
TOK = 128
ROWS = GROUP * TOK
CACHED = 32768
SIDE = 4
CHUNK = 1024
TP = 8
KT = 256
LOG2E = 1.4426950408889634
LN2 = 0.6931471805599453
LOW = -1e30
TOO_BIG = 2.0**100
TOO_SMALL = 2.0**-60
META = 16

VMEM = pl.BlockSpec(memory_space=pltpu.VMEM)


def shift(block, kind, step):
    pairs = []
    for i in range(SIDE * SIDE):
        z, y = divmod(i, SIDE)
        for t in range(TP):
            if (t % 2 == 0) == (kind == "keys"):
                j = z * SIDE + (y + step) % SIDE
            else:
                j = ((z + step) % SIDE) * SIDE + y
            pairs.append((i * TP + t, j * TP + t))
    return lax.ppermute(block, ("ctx", "tp"), pairs)


def _bf(x):
    return np.asarray(x, np.float32).astype(ml_dtypes.bfloat16).astype(np.float64)


def _fit():
    t = np.cos(np.linspace(0, np.pi, 4001)) * 0.5
    u = t * t
    cos = np.polynomial.polynomial.polyfit(u, np.cos(2 * np.pi * t), 8)
    good = np.abs(t) > 1e-3
    sin = np.polynomial.polynomial.polyfit(u[good], np.sin(2 * np.pi * t[good]) / t[good], 7)
    return [float(c) for c in cos], [float(c) for c in sin]


COS, SIN = _fit()


def _turns():
    turns = 500000.0 ** (-2.0 * np.arange(64) / HEAD) / (2 * np.pi)
    first = _bf(turns)
    second = _bf(turns - first)
    return [[float(x) for x in piece] for piece in (first, second, turns - first - second)]


TURNS = _turns()


def spread(constants):
    row = lax.broadcasted_iota(jnp.int32, (8, TOK), 0)
    tiles = []
    for first in range(0, 64, 8):
        tile = jnp.full((8, TOK), constants[first + 7], jnp.float32)
        for i in range(7):
            tile = jnp.where(row == i, constants[first + i], tile)
        tiles.append(tile)
    return jnp.concatenate(tiles, 0)


def angles(positions, turns):
    a = positions * turns[0]
    a = a - jnp.round(a)
    b = positions * turns[1]
    t = a + (b - jnp.round(b)) + positions * turns[2]
    t = t - jnp.round(t)
    u = t * t
    cos = jnp.full_like(u, COS[-1])
    for c in COS[-2::-1]:
        cos = cos * u + c
    sin = jnp.full_like(u, SIN[-1])
    for c in SIN[-2::-1]:
        sin = sin * u + c
    return cos, sin * t


def turned(x, cos, sin):
    lower, upper = x[:64], x[64:]
    return jnp.concatenate([lower * cos - upper * sin, upper * cos + lower * sin], 0)


def coded(places):
    high = jnp.right_shift(places, 4)
    rows = lax.broadcasted_iota(jnp.int32, (META, TOK), 0)
    both = jnp.where(rows == 0, high, jnp.where(rows == 1, places - high * 16, 0))
    return both.astype(jnp.float32).astype(jnp.bfloat16)


def places_of(meta):
    meta = meta.astype(jnp.float32)
    return meta[0:1, :] * 16.0 + meta[1:2, :]


def angle_kernel(places_ref, out_ref):
    order = places_ref[0:1, :]
    turns = [spread(piece) for piece in TURNS]
    cos, sin = angles((order + CACHED).astype(jnp.float32), turns)
    scale = HEAD**-0.5 * LOG2E
    out_ref[0:64, :] = cos * scale
    out_ref[64:128, :] = sin * scale
    out_ref[128:, :] = coded(order).astype(jnp.float32)


def query_kernel(q_ref, angle_ref, out_ref):
    cos, sin = angle_ref[0:64, :], angle_ref[64:128, :]
    for g in range(GROUP):
        lanes = slice(g * HEAD, (g + 1) * HEAD)
        x = q_ref[:, lanes].astype(jnp.float32).T
        out_ref[0:HEAD, lanes] = turned(x, cos, sin).astype(jnp.bfloat16)
    out_ref[HEAD:, :] = jnp.concatenate([angle_ref[128:, :].astype(jnp.bfloat16)] * GROUP, 1)


FRESH_KEYS = 2 * CHUNK
FRESH_VALUES = FRESH_KEYS + TOK
PLACES = FRESH_VALUES + TOK


def key_kernel(start, k_ref, v_ref, pos_ref, *refs):
    with_fresh = len(refs) > 1
    if with_fresh:
        fk_ref, fv_ref, places_ref, out_ref = refs
    else:
        (out_ref,) = refs
    turns = [spread(piece) for piece in TURNS]

    def keys(x, positions):
        cos, sin = angles(positions.astype(jnp.float32), turns)
        return turned(x.astype(jnp.float32).T, cos, sin).T.astype(jnp.bfloat16)

    def values(x):
        return x.astype(jnp.float32).T.astype(jnp.bfloat16)

    for b in range(CHUNK // TOK):
        rows = slice(start + b * TOK, start + (b + 1) * TOK)
        tile = start // TOK + b
        out_ref[b * TOK : (b + 1) * TOK, :] = keys(k_ref[rows, :], pos_ref[tile : tile + 1, :])
        out_ref[CHUNK + b * TOK : CHUNK + (b + 1) * TOK, :] = values(v_ref[rows, :])
    if with_fresh:
        order, span = places_ref[0:1, :], places_ref[1:2, 0:1]
        out_ref[FRESH_KEYS:FRESH_VALUES, :] = keys(fk_ref[...], order + CACHED)
        out_ref[FRESH_VALUES:PLACES, :] = values(fv_ref[...])
        lane = lax.broadcasted_iota(jnp.int32, (1, TOK), 1)
        out_ref[PLACES:, :] = coded(jnp.where(lane < span, order, 4000))


def dot(a, b):
    return lax.dot_general(a, b, (((1,), (0,)), ((), ())), preferred_element_type=jnp.float32)


def attend_kernel(plan, *refs):
    it = iter(refs)
    n_q, n_fresh = plan["n_q"], plan["n_fresh"]
    q_refs = [next(it) for _ in range(n_q)]
    kv_refs = [next(it) for _ in range(plan["n_kv"])]
    fresh_refs = [next(it) for _ in range(n_fresh)]
    if not plan["start"]:
        acc_in, ml_in = next(it), next(it)
    if plan["into"]:
        next(it), next(it)
    if plan["finish"]:
        out_refs = [next(it) for _ in range(n_q)]
    else:
        acc_out, ml_out = next(it), next(it)
    q_s = next(it)
    if n_fresh:
        f_s, place_s = next(it), next(it)
    if plan["finish"]:
        acc_out, ml_out = next(it), next(it)

    for i, r in enumerate(q_refs):
        q_s[i] = r[...]
    for i, r in enumerate(fresh_refs):
        f_s[i * TOK : (i + 1) * TOK, :] = r[FRESH_KEYS:FRESH_VALUES, :]
        f_s[(n_fresh + i) * TOK : (n_fresh + i + 1) * TOK, :] = r[FRESH_VALUES:PLACES, :]
        place_s[i * TOK : (i + 1) * TOK, :] = jnp.broadcast_to(places_of(r[PLACES:, :]), (TOK, TOK)).T

    def aligned(i):
        return i if isinstance(i, int) else pl.multiple_of(i, TOK)

    def k_tile(ref, first):
        return ref[pl.ds(aligned(first), KT), :]

    def v_tile(ref, first):
        return jnp.concatenate([ref[pl.ds(aligned(first + j * TOK), TOK), :] for j in range(KT // TOK)], 1)

    def scores(ref, first, item, masked):
        s = dot(k_tile(ref, first), q_s[item, 0:HEAD, :])
        if masked:
            mine = places_of(q_s[item, HEAD:, 0:TOK])
            mask = place_s[pl.ds(aligned(first), KT), :] <= mine
            s = jnp.where(jnp.concatenate([mask] * GROUP, 1), s, LOW)
        return s

    sources = [(ref, CHUNK, CHUNK, False) for ref in kv_refs]
    if n_fresh:
        sources.append((f_s, n_fresh * TOK, n_fresh * TOK, True))

    def old_of(item):
        if plan["start"]:
            return None
        return ml_in[item][0:1, :], ml_in[item][1:2, :], acc_in[item]

    base = plan["base"]

    def put(item, m, total, acc):
        acc_out[item + base] = acc
        ml_out[item + base] = jnp.concatenate([m, total, jnp.zeros((6, ROWS), jnp.float32)], 0)

    def quick(item):
        tiles = [(ref, first, values, masked) for ref, values, n, masked in sources for first in range(0, n, KT)]
        old = old_of(item)
        if old is None:
            m, total, acc = None, None, None
        else:
            m, total, acc = old
        part = jnp.zeros((8, ROWS), jnp.float32)

        def scores_of(tile):
            return scores(tile[0], tile[1], item, tile[3])

        ahead = scores_of(tiles[0])
        for j, (ref, first, values, _) in enumerate(tiles):
            s = ahead
            if j + 1 < len(tiles):
                ahead = scores_of(tiles[j + 1])
            p = jnp.exp2(s) if m is None else jnp.exp2(s - m)
            part = part + jnp.sum(p.reshape(KT // 8, 8, ROWS), 0)
            pv = dot(v_tile(ref, values + first), p.astype(jnp.bfloat16))
            acc = pv if acc is None else acc + pv
        part = jnp.sum(part, 0, keepdims=True)
        if m is None:
            m, total = jnp.zeros((1, ROWS), jnp.float32), part
        else:
            total = total + part
        put(item, m, total, acc)

    def careful(item):
        def group(g, carry):
            lanes = pl.ds(aligned(g * TOK), TOK)
            if plan["start"]:
                m = jnp.full((1, TOK), LOW, jnp.float32)
                total = jnp.zeros((1, TOK), jnp.float32)
                acc = jnp.zeros((HEAD, TOK), jnp.float32)
            else:
                m, total, acc = ml_in[item, 0:1, lanes], ml_in[item, 1:2, lanes], acc_in[item, :, lanes]
            q = q_s[item, 0:HEAD, lanes]
            for ref, values, n, masked in sources:

                def step(t, state, ref=ref, values=values, masked=masked):
                    m, total, acc = state
                    first = t * KT
                    s = dot(k_tile(ref, first), q)
                    if masked:
                        mine = places_of(q_s[item, HEAD:, 0:TOK])
                        s = jnp.where(place_s[pl.ds(aligned(first), KT), :] <= mine, s, LOW)
                    top = jnp.maximum(m, jnp.max(s, 0, keepdims=True))
                    back = jnp.exp2(m - top)
                    p = jnp.where(s > 0.5 * LOW, jnp.exp2(s - top), 0.0)
                    total = total * back + jnp.sum(p, 0, keepdims=True)
                    acc = acc * back + dot(v_tile(ref, values + first), p.astype(jnp.bfloat16))
                    return top, total, acc

                m, total, acc = lax.fori_loop(0, n // KT, step, (m, total, acc))
            acc_out[item + base, :, lanes] = acc
            ml_out[item + base, 0:1, lanes] = m
            ml_out[item + base, 1:2, lanes] = total
            return carry

        lax.fori_loop(0, GROUP, group, 0)

    def everything(step):
        def body(item, carry):
            step(item)
            return carry

        if n_q == 1:
            step(0)
        else:
            lax.fori_loop(0, n_q, body, 0)

    everything(quick)
    fine = None
    for i in range(base, base + n_q):
        total = ml_out[i][1:2, :]
        good = jnp.where((total < TOO_BIG) & (total > TOO_SMALL), 1.0, 0.0)
        fine = good if fine is None else jnp.minimum(fine, good)

    @pl.when(jnp.min(fine) < 0.5)
    def _():
        everything(careful)

    if plan["finish"]:
        for i in range(n_q):
            m, total = ml_out[i][0:1, :], ml_out[i][1:2, :]
            out_refs[i][0:HEAD, :] = (acc_out[i] * (1.0 / total)).astype(jnp.bfloat16)
            out_refs[i][HEAD:, :] = coded_mass(m + jnp.log2(total))


def coded_mass(mass):
    a = mass.astype(jnp.bfloat16).astype(jnp.float32)
    b = (mass - a).astype(jnp.bfloat16).astype(jnp.float32)
    c = mass - a - b
    rows = lax.broadcasted_iota(jnp.int32, (META, ROWS), 0)
    return jnp.where(rows == 0, a, jnp.where(rows == 1, b, jnp.where(rows == 2, c, 0.0))).astype(jnp.bfloat16)


def attend(name, queries, kvs, state=None, fresh=(), finish=False, room=None, base=0, into=None):
    n_q = len(queries)
    room = room or n_q
    plan = dict(
        n_q=n_q,
        n_kv=len(kvs),
        n_fresh=len(fresh),
        start=state is None,
        finish=finish,
        base=base,
        into=into is not None,
    )
    acc = jax.ShapeDtypeStruct((room, HEAD, ROWS), jnp.float32)
    ml = jax.ShapeDtypeStruct((room, 8, ROWS), jnp.float32)
    scratch = [pltpu.VMEM((n_q, HEAD + META, ROWS), jnp.bfloat16)]
    if fresh:
        scratch += [
            pltpu.VMEM((2 * len(fresh) * TOK, HEAD), jnp.bfloat16),
            pltpu.VMEM((len(fresh) * TOK, TOK), jnp.float32),
        ]
    if finish:
        outs = [jax.ShapeDtypeStruct((HEAD + META, ROWS), jnp.bfloat16)] * n_q
        scratch += [pltpu.VMEM(acc.shape, jnp.float32), pltpu.VMEM(ml.shape, jnp.float32)]
    else:
        outs = [acc, ml]
    args = list(queries) + list(kvs) + list(fresh) + list(state or ()) + list(into or ())
    pairs = n_q * (len(kvs) * CHUNK + len(fresh) * TOK) * ROWS
    return pl.pallas_call(
        functools.partial(attend_kernel, plan),
        out_shape=outs,
        in_specs=[VMEM] * len(args),
        out_specs=[VMEM] * len(outs),
        scratch_shapes=scratch,
        input_output_aliases={len(args) - 2: 0, len(args) - 1: 1} if into else {},
        compiler_params=pltpu.CompilerParams(vmem_limit_bytes=24 * 2**20),
        cost_estimate=pl.CostEstimate(flops=pairs * 1024, bytes_accessed=0, transcendentals=0),
        name=name,
    )(*args)


def combine_kernel(acc_ref, ml_ref, *refs):
    parts, (att_ref, mass_ref) = refs[:-2], refs[-2:]
    total = ml_ref[0][1:2, :]
    masses = [ml_ref[0][0:1, :] + jnp.log2(total)]
    for r in parts:
        rows = r[HEAD:, :].astype(jnp.float32)
        masses.append(rows[0:1, :] + rows[1:2, :] + rows[2:3, :])
    top = functools.reduce(jnp.maximum, masses)
    weights = [jnp.exp2(m - top) for m in masses]
    den = functools.reduce(jnp.add, weights)
    mass = (top + jnp.log2(den)) * LN2
    shares = [w / den for w in weights]
    shares[0] = shares[0] / total
    for g in range(GROUP):
        lanes = slice(g * TOK, (g + 1) * TOK)
        x = acc_ref[0, :, lanes] * shares[0][:, lanes]
        for r, w in zip(parts, shares[1:]):
            x = x + r[0:HEAD, lanes].astype(jnp.float32) * w[:, lanes]
        att_ref[:, lanes] = x.T.astype(jnp.bfloat16)
    mass_ref[...] = jnp.concatenate([mass[:, g * TOK : (g + 1) * TOK] for g in range(GROUP)], 0)


def prepare(name, kernel, shape, args, specs, work, scratch=()):
    return pl.pallas_call(
        kernel,
        out_shape=jax.ShapeDtypeStruct(shape, jnp.bfloat16),
        in_specs=specs,
        out_specs=VMEM,
        scratch_shapes=scratch,
        compiler_params=pltpu.CompilerParams(vmem_limit_bytes=8 * 2**20),
        cost_estimate=pl.CostEstimate(flops=work, bytes_accessed=0, transcendentals=0),
        name=name,
    )(*args)


def per_device(queries, k, v, fk, fv, positions, order, span):
    places = jnp.concatenate([order, lax.pad(span, jnp.int32(0), [(0, TOK - 1, 0)])]).reshape(2, TOK)
    positions = positions.reshape(2 * CHUNK // TOK, TOK)
    angle = pl.pallas_call(
        angle_kernel,
        out_shape=jax.ShapeDtypeStruct((HEAD + META, TOK), jnp.float32),
        in_specs=[VMEM],
        out_specs=VMEM,
        compiler_params=pltpu.CompilerParams(vmem_limit_bytes=8 * 2**20),
        cost_estimate=pl.CostEstimate(flops=10**9, bytes_accessed=0, transcendentals=0),
        name="angles",
    )(places)
    q0 = prepare("turn_queries", query_kernel, (HEAD + META, ROWS), (queries, angle), [VMEM] * 2, 10**9)
    q_near = [shift(q0, "queries", -1), shift(q0, "queries", 1)]

    first = prepare(
        "turn_keys_first",
        functools.partial(key_kernel, 0),
        (PLACES + META, HEAD),
        (k, v, positions, fk, fv, places),
        [VMEM] * 6,
        2 * 10**9,
    )
    first_near = [shift(first, "keys", -1), shift(first, "keys", 1)]
    second = prepare(
        "turn_keys_second",
        functools.partial(key_kernel, CHUNK),
        (2 * CHUNK, HEAD),
        (k, v, positions),
        [VMEM] * 3,
        2 * 10**9,
    )

    hold = lax.optimization_barrier
    second, q0_late = hold((second, q0))
    q_far = shift(q0_late, "queries", 2)
    mine = attend("mine_own", [q0], [first, second])
    near = attend("near_own", q_near, [first, second])
    near, second_late = hold((near, second))
    second_near = [shift(second_late, "keys", -1), shift(second_late, "keys", 1)]
    far = attend("far_own", [q_far], [first, second])
    near = attend("near_first", q_near, first_near, near)
    near, far, behind, ahead = hold((near, far, first_near[1], second_near[0]))
    first_far = shift(behind, "keys", 1)
    second_far = shift(ahead, "keys", -1)
    both = attend("far_near", [q_far], [*first_near, *second_near], far, room=3)
    both = attend("near_second", q_near, second_near, near, room=3, base=1, into=both)
    fresh = [first, *first_near, first_far]
    results = attend("others_last", [q_far, *q_near], [first_far, second_far], both, fresh, finish=True)
    results, mine = hold((results, mine))
    back = [shift(r, "queries", step) for r, step in zip(results, (2, 1, -1))]
    mine = attend("mine_rest", [q0], [*first_near, *second_near, first_far, second_far], mine, fresh)
    attended, mass = pl.pallas_call(
        combine_kernel,
        out_shape=[
            jax.ShapeDtypeStruct((TOK, GROUP * HEAD), jnp.bfloat16),
            jax.ShapeDtypeStruct((GROUP, TOK), jnp.float32),
        ],
        in_specs=[VMEM] * 5,
        out_specs=[VMEM] * 2,
        compiler_params=pltpu.CompilerParams(vmem_limit_bytes=8 * 2**20),
        name="combine",
    )(*mine, *back)
    return attended, mass.T


def solution(mesh):
    spec = (P("ctx", "tp"),) * 5 + (P("ctx"),) * 3
    return jax.shard_map(
        per_device,
        mesh=mesh,
        in_specs=spec,
        out_specs=(P("ctx", "tp"), P("ctx", "tp")),
        check_vma=False,
    )
```

```python
import functools

import jax
import jax.numpy as jnp
import ml_dtypes
import numpy as np
from jax import lax
from jax.experimental import pallas as pl
from jax.experimental.pallas import tpu as pltpu
from jax.sharding import PartitionSpec as P

GROUP = 8
HEAD = 128
TOK = 128
ROWS = GROUP * TOK
CACHED = 32768
SIDE = 4
CHUNK = 1024
TP = 8
KT = 256
LOG2E = 1.4426950408889634
LN2 = 0.6931471805599453
LOW = -1e30
TOO_BIG = 2.0**100
TOO_SMALL = 2.0**-60
META = 16

VMEM = pl.BlockSpec(memory_space=pltpu.VMEM)


def shift(block, kind, step):
    pairs = []
    for i in range(SIDE * SIDE):
        z, y = divmod(i, SIDE)
        for t in range(TP):
            if (t % 2 == 0) == (kind == "keys"):
                j = z * SIDE + (y + step) % SIDE
            else:
                j = ((z + step) % SIDE) * SIDE + y
            pairs.append((i * TP + t, j * TP + t))
    return lax.ppermute(block, ("ctx", "tp"), pairs)


def _bf(x):
    return np.asarray(x, np.float32).astype(ml_dtypes.bfloat16).astype(np.float64)


def _fit():
    t = np.cos(np.linspace(0, np.pi, 4001)) * 0.5
    u = t * t
    cos = np.polynomial.polynomial.polyfit(u, np.cos(2 * np.pi * t), 8)
    good = np.abs(t) > 1e-3
    sin = np.polynomial.polynomial.polyfit(u[good], np.sin(2 * np.pi * t[good]) / t[good], 7)
    return [float(c) for c in cos], [float(c) for c in sin]


COS, SIN = _fit()


def _turns():
    turns = 500000.0 ** (-2.0 * np.arange(64) / HEAD) / (2 * np.pi)
    first = _bf(turns)
    second = _bf(turns - first)
    return [[float(x) for x in piece] for piece in (first, second, turns - first - second)]


TURNS = _turns()


def spread(constants):
    row = lax.broadcasted_iota(jnp.int32, (8, TOK), 0)
    tiles = []
    for first in range(0, 64, 8):
        tile = jnp.full((8, TOK), constants[first + 7], jnp.float32)
        for i in range(7):
            tile = jnp.where(row == i, constants[first + i], tile)
        tiles.append(tile)
    return jnp.concatenate(tiles, 0)


def angles(positions, turns):
    a = positions * turns[0]
    a = a - jnp.round(a)
    b = positions * turns[1]
    t = a + (b - jnp.round(b)) + positions * turns[2]
    t = t - jnp.round(t)
    u = t * t
    cos = jnp.full_like(u, COS[-1])
    for c in COS[-2::-1]:
        cos = cos * u + c
    sin = jnp.full_like(u, SIN[-1])
    for c in SIN[-2::-1]:
        sin = sin * u + c
    return cos, sin * t


def turned(x, cos, sin):
    lower, upper = x[:64], x[64:]
    return jnp.concatenate([lower * cos - upper * sin, upper * cos + lower * sin], 0)


def coded(places):
    high = jnp.right_shift(places, 4)
    rows = lax.broadcasted_iota(jnp.int32, (META, TOK), 0)
    both = jnp.where(rows == 0, high, jnp.where(rows == 1, places - high * 16, 0))
    return both.astype(jnp.float32).astype(jnp.bfloat16)


def places_of(meta):
    meta = meta.astype(jnp.float32)
    return meta[0:1, :] * 16.0 + meta[1:2, :]


def angle_kernel(order_ref, out_ref):
    order = order_ref[...]
    turns = [spread(piece) for piece in TURNS]
    cos, sin = angles((order + CACHED).astype(jnp.float32), turns)
    scale = HEAD**-0.5 * LOG2E
    out_ref[0:64, :] = cos * scale
    out_ref[64:128, :] = sin * scale
    out_ref[128:, :] = coded(order).astype(jnp.float32)


def query_kernel(q_ref, angle_ref, out_ref):
    cos, sin = angle_ref[0:64, :], angle_ref[64:128, :]
    for g in range(GROUP):
        lanes = slice(g * HEAD, (g + 1) * HEAD)
        x = q_ref[:, lanes].astype(jnp.float32).T
        out_ref[0:HEAD, lanes] = turned(x, cos, sin).astype(jnp.bfloat16)
    out_ref[HEAD:, :] = jnp.concatenate([angle_ref[128:, :].astype(jnp.bfloat16)] * GROUP, 1)


FRESH_KEYS = 2 * CHUNK
FRESH_VALUES = FRESH_KEYS + TOK
PLACES = FRESH_VALUES + TOK


def key_kernel(start, k_ref, v_ref, pos_ref, *refs):
    with_fresh = len(refs) > 1
    if with_fresh:
        fk_ref, fv_ref, order_ref, span_ref, out_ref = refs
    else:
        (out_ref,) = refs
    turns = [spread(piece) for piece in TURNS]

    def keys(x, positions):
        cos, sin = angles(positions.astype(jnp.float32), turns)
        return turned(x.astype(jnp.float32).T, cos, sin).T.astype(jnp.bfloat16)

    def values(x):
        return x.astype(jnp.float32).T.astype(jnp.bfloat16)

    for b in range(CHUNK // TOK):
        rows = slice(start + b * TOK, start + (b + 1) * TOK)
        tile = start // TOK + b
        out_ref[b * TOK : (b + 1) * TOK, :] = keys(k_ref[rows, :], pos_ref[tile : tile + 1, :])
        out_ref[CHUNK + b * TOK : CHUNK + (b + 1) * TOK, :] = values(v_ref[rows, :])
    if with_fresh:
        order = order_ref[...]
        out_ref[FRESH_KEYS:FRESH_VALUES, :] = keys(fk_ref[...], order + CACHED)
        out_ref[FRESH_VALUES:PLACES, :] = values(fv_ref[...])
        lane = lax.broadcasted_iota(jnp.int32, (1, TOK), 1)
        out_ref[PLACES:, :] = coded(jnp.where(lane < span_ref[0], order, 4000))


def dot(a, b):
    return lax.dot_general(a, b, (((1,), (0,)), ((), ())), preferred_element_type=jnp.float32)


def attend_kernel(plan, *refs):
    it = iter(refs)
    n_q, n_fresh = plan["n_q"], plan["n_fresh"]
    q_refs = [next(it) for _ in range(n_q)]
    kv_refs = [next(it) for _ in range(plan["n_kv"])]
    fresh_refs = [next(it) for _ in range(n_fresh)]
    if not plan["start"]:
        acc_in, ml_in = next(it), next(it)
    if plan["finish"]:
        out_refs = [next(it) for _ in range(n_q)]
    else:
        acc_out, ml_out = next(it), next(it)
    q_s = next(it)
    if n_fresh:
        f_s, place_s = next(it), next(it)
    if plan["finish"]:
        acc_out, ml_out = next(it), next(it)

    for i, r in enumerate(q_refs):
        q_s[i] = r[...]
    for i, r in enumerate(fresh_refs):
        f_s[i * TOK : (i + 1) * TOK, :] = r[FRESH_KEYS:FRESH_VALUES, :]
        f_s[(n_fresh + i) * TOK : (n_fresh + i + 1) * TOK, :] = r[FRESH_VALUES:PLACES, :]
        place_s[i * TOK : (i + 1) * TOK, :] = jnp.broadcast_to(places_of(r[PLACES:, :]), (TOK, TOK)).T

    def aligned(i):
        return i if isinstance(i, int) else pl.multiple_of(i, TOK)

    def k_tile(ref, first):
        return ref[pl.ds(aligned(first), KT), :]

    def v_tile(ref, first):
        return jnp.concatenate([ref[pl.ds(aligned(first + j * TOK), TOK), :] for j in range(KT // TOK)], 1)

    def scores(ref, first, item, masked):
        s = dot(k_tile(ref, first), q_s[item, 0:HEAD, :])
        if masked:
            mine = places_of(q_s[item, HEAD:, 0:TOK])
            mask = place_s[pl.ds(aligned(first), KT), :] <= mine
            s = jnp.where(jnp.concatenate([mask] * GROUP, 1), s, LOW)
        return s

    sources = [(ref, CHUNK, CHUNK, False) for ref in kv_refs]
    if n_fresh:
        sources.append((f_s, n_fresh * TOK, n_fresh * TOK, True))

    def old_of(item):
        if plan["start"]:
            return None
        at = item + plan["skip"]
        return ml_in[at][0:1, :], ml_in[at][1:2, :], acc_in[at]

    skip = plan["skip"]

    def put(item, m, total, acc):
        acc_out[item] = acc
        ml_out[item] = jnp.concatenate([m, total, jnp.zeros((6, ROWS), jnp.float32)], 0)

    def quick(item):
        tiles = [(ref, first, values, masked) for ref, values, n, masked in sources for first in range(0, n, KT)]
        old = old_of(item)
        if old is None:
            m, total, acc = None, None, None
        else:
            m, total, acc = old
        part = jnp.zeros((8, ROWS), jnp.float32)

        def scores_of(tile):
            return scores(tile[0], tile[1], item, tile[3])

        ahead = scores_of(tiles[0])
        for j, (ref, first, values, _) in enumerate(tiles):
            s = ahead
            if j + 1 < len(tiles):
                ahead = scores_of(tiles[j + 1])
            p = jnp.exp2(s) if m is None else jnp.exp2(s - m)
            part = part + jnp.sum(p.reshape(KT // 8, 8, ROWS), 0)
            pv = dot(v_tile(ref, values + first), p.astype(jnp.bfloat16))
            acc = pv if acc is None else acc + pv
        part = jnp.sum(part, 0, keepdims=True)
        if m is None:
            m, total = jnp.zeros((1, ROWS), jnp.float32), part
        else:
            total = total + part
        put(item, m, total, acc)

    def careful(item):
        def group(g, carry):
            lanes = pl.ds(aligned(g * TOK), TOK)
            if plan["start"]:
                m = jnp.full((1, TOK), LOW, jnp.float32)
                total = jnp.zeros((1, TOK), jnp.float32)
                acc = jnp.zeros((HEAD, TOK), jnp.float32)
            else:
                at = item + skip
                m, total, acc = ml_in[at, 0:1, lanes], ml_in[at, 1:2, lanes], acc_in[at, :, lanes]
            q = q_s[item, 0:HEAD, lanes]
            for ref, values, n, masked in sources:

                def step(t, state, ref=ref, values=values, masked=masked):
                    m, total, acc = state
                    first = t * KT
                    s = dot(k_tile(ref, first), q)
                    if masked:
                        mine = places_of(q_s[item, HEAD:, 0:TOK])
                        s = jnp.where(place_s[pl.ds(aligned(first), KT), :] <= mine, s, LOW)
                    top = jnp.maximum(m, jnp.max(s, 0, keepdims=True))
                    back = jnp.exp2(m - top)
                    p = jnp.where(s > 0.5 * LOW, jnp.exp2(s - top), 0.0)
                    total = total * back + jnp.sum(p, 0, keepdims=True)
                    acc = acc * back + dot(v_tile(ref, values + first), p.astype(jnp.bfloat16))
                    return top, total, acc

                m, total, acc = lax.fori_loop(0, n // KT, step, (m, total, acc))
            acc_out[item, :, lanes] = acc
            ml_out[item, 0:1, lanes] = m
            ml_out[item, 1:2, lanes] = total
            return carry

        lax.fori_loop(0, GROUP, group, 0)

    def everything(step):
        def body(item, carry):
            step(item)
            return carry

        if n_q == 1:
            step(0)
        else:
            lax.fori_loop(0, n_q, body, 0)

    everything(quick)
    fine = None
    for i in range(n_q):
        total = ml_out[i][1:2, :]
        good = jnp.where((total < TOO_BIG) & (total > TOO_SMALL), 1.0, 0.0)
        fine = good if fine is None else jnp.minimum(fine, good)

    @pl.when(jnp.min(fine) < 0.5)
    def _():
        everything(careful)

    if plan["finish"]:
        for i in range(n_q):
            m, total = ml_out[i][0:1, :], ml_out[i][1:2, :]
            out_refs[i][0:HEAD, :] = (acc_out[i] * (1.0 / total)).astype(jnp.bfloat16)
            out_refs[i][HEAD:, :] = coded_mass(m + jnp.log2(total))


def coded_mass(mass):
    a = mass.astype(jnp.bfloat16).astype(jnp.float32)
    b = (mass - a).astype(jnp.bfloat16).astype(jnp.float32)
    c = mass - a - b
    rows = lax.broadcasted_iota(jnp.int32, (META, ROWS), 0)
    return jnp.where(rows == 0, a, jnp.where(rows == 1, b, jnp.where(rows == 2, c, 0.0))).astype(jnp.bfloat16)


def attend(name, queries, kvs, state=None, fresh=(), finish=False, skip=0):
    n_q = len(queries)
    plan = dict(
        n_q=n_q,
        n_kv=len(kvs),
        n_fresh=len(fresh),
        start=state is None,
        finish=finish,
        skip=skip,
    )
    acc = jax.ShapeDtypeStruct((n_q, HEAD, ROWS), jnp.float32)
    ml = jax.ShapeDtypeStruct((n_q, 8, ROWS), jnp.float32)
    scratch = [pltpu.VMEM((n_q, HEAD + META, ROWS), jnp.bfloat16)]
    if fresh:
        scratch += [
            pltpu.VMEM((2 * len(fresh) * TOK, HEAD), jnp.bfloat16),
            pltpu.VMEM((len(fresh) * TOK, TOK), jnp.float32),
        ]
    if finish:
        outs = [jax.ShapeDtypeStruct((HEAD + META, ROWS), jnp.bfloat16)] * n_q
        scratch += [pltpu.VMEM(acc.shape, jnp.float32), pltpu.VMEM(ml.shape, jnp.float32)]
    else:
        outs = [acc, ml]
    args = list(queries) + list(kvs) + list(fresh) + list(state or ())
    pairs = n_q * (len(kvs) * CHUNK + len(fresh) * TOK) * ROWS
    return pl.pallas_call(
        functools.partial(attend_kernel, plan),
        out_shape=outs,
        in_specs=[VMEM] * len(args),
        out_specs=[VMEM] * len(outs),
        scratch_shapes=scratch,
        compiler_params=pltpu.CompilerParams(vmem_limit_bytes=24 * 2**20),
        cost_estimate=pl.CostEstimate(flops=pairs * 1024, bytes_accessed=0, transcendentals=0),
        name=name,
    )(*args)


def combine_kernel(acc_ref, ml_ref, *refs):
    parts, (att_ref, mass_ref) = refs[:-2], refs[-2:]
    total = ml_ref[0][1:2, :]
    masses = [ml_ref[0][0:1, :] + jnp.log2(total)]
    for r in parts:
        rows = r[HEAD:, :].astype(jnp.float32)
        masses.append(rows[0:1, :] + rows[1:2, :] + rows[2:3, :])
    top = functools.reduce(jnp.maximum, masses)
    weights = [jnp.exp2(m - top) for m in masses]
    den = functools.reduce(jnp.add, weights)
    mass = (top + jnp.log2(den)) * LN2
    shares = [w / den for w in weights]
    shares[0] = shares[0] / total
    for g in range(GROUP):
        lanes = slice(g * TOK, (g + 1) * TOK)
        x = acc_ref[0, :, lanes] * shares[0][:, lanes]
        for r, w in zip(parts, shares[1:]):
            x = x + r[0:HEAD, lanes].astype(jnp.float32) * w[:, lanes]
        att_ref[:, lanes] = x.T.astype(jnp.bfloat16)
    mass_ref[...] = jnp.concatenate([mass[:, g * TOK : (g + 1) * TOK] for g in range(GROUP)], 0)


def prepare(name, kernel, shape, args, specs, work, dtype=jnp.bfloat16):
    return pl.pallas_call(
        kernel,
        out_shape=jax.ShapeDtypeStruct(shape, dtype),
        in_specs=specs,
        out_specs=VMEM,
        compiler_params=pltpu.CompilerParams(vmem_limit_bytes=8 * 2**20),
        cost_estimate=pl.CostEstimate(flops=work, bytes_accessed=0, transcendentals=0),
        name=name,
    )(*args)


def per_device(queries, k, v, fk, fv, positions, order, span):
    order = order.reshape(1, TOK)
    positions = positions.reshape(2 * CHUNK // TOK, TOK)
    angle = prepare("angles", angle_kernel, (HEAD + META, TOK), (order,), [VMEM], 10**9, jnp.float32)
    q0 = prepare("turn_queries", query_kernel, (HEAD + META, ROWS), (queries, angle), [VMEM] * 2, 10**9)
    q_near = [shift(q0, "queries", -1), shift(q0, "queries", 1)]
    q_far = shift(q0, "queries", 2)

    first = prepare(
        "turn_keys_first",
        functools.partial(key_kernel, 0),
        (2 * CHUNK, HEAD),
        (k, v, positions),
        [VMEM] * 3,
        2 * 10**9,
    )
    first_near = [shift(first, "keys", -1), shift(first, "keys", 1)]
    second = prepare(
        "turn_keys_second",
        functools.partial(key_kernel, CHUNK),
        (PLACES + META, HEAD),
        (k, v, positions, fk, fv, order, span),
        [VMEM] * 6 + [pl.BlockSpec(memory_space=pltpu.SMEM)],
        2 * 10**9,
    )
    second_near = [shift(second, "keys", -1), shift(second, "keys", 1)]

    mine = attend("mine_own", [q0], [first, second])
    state = attend("others_own", [q_far, *q_near], [first, second])
    far = attend("far_first", [q_far], first_near, state)
    far, state, behind, ahead = lax.optimization_barrier((far, state, first_near[1], second_near[0]))
    first_far = shift(behind, "keys", 1)
    second_far = shift(ahead, "keys", -1)
    near = attend("near_near", q_near, [*first_near, *second_near], state, skip=1)
    fresh = [second, *second_near, second_far]
    r_ahead, r_behind = attend("near_last", q_near, [first_far, second_far], near, fresh, finish=True)
    (r_far,) = attend("far_last", [q_far], [*second_near, first_far, second_far], far, fresh, finish=True)
    back = [shift(r_far, "queries", 2), shift(r_ahead, "queries", 1), shift(r_behind, "queries", -1)]
    mine = attend("mine_rest", [q0], [*first_near, *second_near, first_far, second_far], mine, fresh)
    attended, mass = pl.pallas_call(
        combine_kernel,
        out_shape=[
            jax.ShapeDtypeStruct((TOK, GROUP * HEAD), jnp.bfloat16),
            jax.ShapeDtypeStruct((GROUP, TOK), jnp.float32),
        ],
        in_specs=[VMEM] * 5,
        out_specs=[VMEM] * 2,
        compiler_params=pltpu.CompilerParams(vmem_limit_bytes=8 * 2**20),
        name="combine",
    )(*mine, *back)
    return attended, mass.T


def solution(mesh):
    spec = (P("ctx", "tp"),) * 5 + (P("ctx"),) * 3
    return jax.shard_map(
        per_device,
        mesh=mesh,
        in_specs=spec,
        out_specs=(P("ctx", "tp"), P("ctx", "tp")),
        check_vma=False,
    )
```

```python
import functools

import jax
import jax.numpy as jnp
import ml_dtypes
import numpy as np
from jax import lax
from jax.experimental import pallas as pl
from jax.experimental.pallas import tpu as pltpu
from jax.sharding import PartitionSpec as P

GROUP = 8
HEAD = 128
TOK = 128
ROWS = GROUP * TOK
CACHED = 32768
SIDE = 4
CHUNK = 1024
TP = 8
KT = 256
SCALE = HEAD**-0.5 * 1.4426950408889634
LN2 = 0.6931471805599453
LOW = -1e30
TOO_BIG = 2.0**100
TOO_SMALL = 2.0**-60
META = 16

VMEM = pl.BlockSpec(memory_space=pltpu.VMEM)


def shift(block, kind, step):
    pairs = []
    for i in range(SIDE * SIDE):
        z, y = divmod(i, SIDE)
        for t in range(TP):
            if (t % 2 == 0) == (kind == "keys"):
                j = z * SIDE + (y + step) % SIDE
            else:
                j = ((z + step) % SIDE) * SIDE + y
            pairs.append((i * TP + t, j * TP + t))
    return lax.ppermute(block, ("ctx", "tp"), pairs)


def _bf(x):
    return np.asarray(x, np.float32).astype(ml_dtypes.bfloat16).astype(np.float64)


def _fit():
    t = np.cos(np.linspace(0, np.pi, 4001)) * 0.5
    u = t * t
    cos = np.polynomial.polynomial.polyfit(u, np.cos(2 * np.pi * t), 8)
    good = np.abs(t) > 1e-3
    sin = np.polynomial.polynomial.polyfit(u[good], np.sin(2 * np.pi * t[good]) / t[good], 7)
    return [float(c) for c in cos], [float(c) for c in sin]


COS, SIN = _fit()


def _turns():
    turns = 500000.0 ** (-2.0 * np.arange(64) / HEAD) / (2 * np.pi)
    first = _bf(turns)
    second = _bf(turns - first)
    return [[float(x) for x in piece] for piece in (first, second, turns - first - second)]


TURNS = _turns()


def spread(constants):
    row = lax.broadcasted_iota(jnp.int32, (8, TOK), 0)
    tiles = []
    for first in range(0, 64, 8):
        tile = jnp.full((8, TOK), constants[first + 7], jnp.float32)
        for i in range(7):
            tile = jnp.where(row == i, constants[first + i], tile)
        tiles.append(tile)
    return jnp.concatenate(tiles, 0)


def angles(positions, turns):
    a = positions * turns[0]
    a = a - jnp.round(a)
    b = positions * turns[1]
    t = a + (b - jnp.round(b)) + positions * turns[2]
    t = t - jnp.round(t)
    u = t * t
    cos = jnp.full_like(u, COS[-1])
    for c in COS[-2::-1]:
        cos = cos * u + c
    sin = jnp.full_like(u, SIN[-1])
    for c in SIN[-2::-1]:
        sin = sin * u + c
    return cos, sin * t


def turned(x, cos, sin):
    lower, upper = x[:64], x[64:]
    return jnp.concatenate([lower * cos - upper * sin, upper * cos + lower * sin], 0)


def coded(places):
    high = jnp.right_shift(places, 4)
    rows = lax.broadcasted_iota(jnp.int32, (META, TOK), 0)
    both = jnp.where(rows == 0, high, jnp.where(rows == 1, places - high * 16, 0))
    return both.astype(jnp.float32).astype(jnp.bfloat16)


def places_of(meta):
    meta = meta.astype(jnp.float32)
    return meta[0:1, :] * 16.0 + meta[1:2, :]


def angle_kernel(order_ref, out_ref):
    order = order_ref[...]
    turns = [spread(piece) for piece in TURNS]
    cos, sin = angles((order + CACHED).astype(jnp.float32), turns)
    out_ref[0:64, :] = cos
    out_ref[64:128, :] = sin
    out_ref[128:, :] = coded(order).astype(jnp.float32)


def query_kernel(q_ref, angle_ref, out_ref):
    cos, sin = angle_ref[0:64, :], angle_ref[64:128, :]
    for g in range(GROUP):
        lanes = slice(g * HEAD, (g + 1) * HEAD)
        x = q_ref[:, lanes].astype(jnp.float32).T
        out_ref[0:HEAD, lanes] = turned(x, cos, sin).astype(jnp.bfloat16)
    out_ref[HEAD:, :] = jnp.concatenate([angle_ref[128:, :].astype(jnp.bfloat16)] * GROUP, 1)


FRESH_KEYS = 2 * CHUNK
FRESH_VALUES = FRESH_KEYS + TOK
PLACES = FRESH_VALUES + TOK


def key_kernel(start, k_ref, v_ref, pos_ref, *refs):
    with_fresh = len(refs) > 1
    if with_fresh:
        fk_ref, fv_ref, order_ref, span_ref, out_ref = refs
    else:
        (out_ref,) = refs
    turns = [spread(piece) for piece in TURNS]

    def keys(x, positions):
        cos, sin = angles(positions.astype(jnp.float32), turns)
        return turned(x.astype(jnp.float32).T, cos, sin).T.astype(jnp.bfloat16)

    def values(x):
        return x.astype(jnp.float32).T.astype(jnp.bfloat16)

    for b in range(CHUNK // TOK):
        rows = slice(start + b * TOK, start + (b + 1) * TOK)
        tile = start // TOK + b
        out_ref[b * TOK : (b + 1) * TOK, :] = keys(k_ref[rows, :], pos_ref[tile : tile + 1, :])
        out_ref[CHUNK + b * TOK : CHUNK + (b + 1) * TOK, :] = values(v_ref[rows, :])
    if with_fresh:
        order = order_ref[...]
        out_ref[FRESH_KEYS:FRESH_VALUES, :] = keys(fk_ref[...], order + CACHED)
        out_ref[FRESH_VALUES:PLACES, :] = values(fv_ref[...])
        lane = lax.broadcasted_iota(jnp.int32, (1, TOK), 1)
        out_ref[PLACES:, :] = coded(jnp.where(lane < span_ref[0], order, 4000))


def dot(a, b):
    return lax.dot_general(a, b, (((1,), (0,)), ((), ())), preferred_element_type=jnp.float32)


def attend_kernel(plan, *refs):
    it = iter(refs)
    n_q, n_fresh = plan["n_q"], plan["n_fresh"]
    q_refs = [next(it) for _ in range(n_q)]
    kv_refs = [next(it) for _ in range(plan["n_kv"])]
    fresh_refs = [next(it) for _ in range(n_fresh)]
    if not plan["start"]:
        acc_in, ml_in = next(it), next(it)
    if plan["finish"]:
        out_refs = [next(it) for _ in range(n_q)]
    else:
        acc_out, ml_out = next(it), next(it)
    q_s = next(it)
    if n_fresh:
        f_s, place_s = next(it), next(it)
    if plan["finish"]:
        acc_out, ml_out = next(it), next(it)

    for i, r in enumerate(q_refs):
        q_s[i] = r[...]
    for i, r in enumerate(fresh_refs):
        f_s[i * TOK : (i + 1) * TOK, :] = r[FRESH_KEYS:FRESH_VALUES, :]
        f_s[(n_fresh + i) * TOK : (n_fresh + i + 1) * TOK, :] = r[FRESH_VALUES:PLACES, :]
        place_s[i * TOK : (i + 1) * TOK, :] = jnp.broadcast_to(places_of(r[PLACES:, :]), (TOK, TOK)).T

    def aligned(i):
        return i if isinstance(i, int) else pl.multiple_of(i, TOK)

    def k_tile(ref, first):
        return ref[pl.ds(aligned(first), KT), :]

    def v_tile(ref, first):
        return jnp.concatenate([ref[pl.ds(aligned(first + j * TOK), TOK), :] for j in range(KT // TOK)], 1)

    def scores(ref, first, item, masked):
        s = dot(k_tile(ref, first), q_s[item, 0:HEAD, :]) * SCALE
        if masked:
            mine = places_of(q_s[item, HEAD:, 0:TOK])
            mask = place_s[pl.ds(aligned(first), KT), :] <= mine
            s = jnp.where(jnp.concatenate([mask] * GROUP, 1), s, LOW)
        return s

    sources = [(ref, CHUNK, CHUNK, False) for ref in kv_refs]
    if n_fresh:
        sources.append((f_s, n_fresh * TOK, n_fresh * TOK, True))

    def old_of(item):
        if plan["start"]:
            return None
        at = item + plan["skip"]
        return ml_in[at][0:1, :], ml_in[at][1:2, :], acc_in[at]

    skip = plan["skip"]

    def put(item, m, total, acc):
        acc_out[item] = acc
        ml_out[item] = jnp.concatenate([m, total, jnp.zeros((6, ROWS), jnp.float32)], 0)

    def quick(item):
        tiles = [(ref, first, values, masked) for ref, values, n, masked in sources for first in range(0, n, KT)]
        old = old_of(item)
        if old is None:
            m, total, acc = None, None, None
        else:
            m, total, acc = old
        part = jnp.zeros((8, ROWS), jnp.float32)

        def scores_of(tile):
            return scores(tile[0], tile[1], item, tile[3])

        ahead = scores_of(tiles[0])
        for j, (ref, first, values, _) in enumerate(tiles):
            s = ahead
            if j + 1 < len(tiles):
                ahead = scores_of(tiles[j + 1])
            p = jnp.exp2(s) if m is None else jnp.exp2(s - m)
            part = part + jnp.sum(p.reshape(KT // 8, 8, ROWS), 0)
            pv = dot(v_tile(ref, values + first), p.astype(jnp.bfloat16))
            acc = pv if acc is None else acc + pv
        part = jnp.sum(part, 0, keepdims=True)
        if m is None:
            m, total = jnp.zeros((1, ROWS), jnp.float32), part
        else:
            total = total + part
        put(item, m, total, acc)

    def careful(item):
        def group(g, carry):
            lanes = pl.ds(aligned(g * TOK), TOK)
            if plan["start"]:
                m = jnp.full((1, TOK), LOW, jnp.float32)
                total = jnp.zeros((1, TOK), jnp.float32)
                acc = jnp.zeros((HEAD, TOK), jnp.float32)
            else:
                at = item + skip
                m, total, acc = ml_in[at, 0:1, lanes], ml_in[at, 1:2, lanes], acc_in[at, :, lanes]
            q = q_s[item, 0:HEAD, lanes]
            for ref, values, n, masked in sources:

                def step(t, state, ref=ref, values=values, masked=masked):
                    m, total, acc = state
                    first = t * KT
                    s = dot(k_tile(ref, first), q) * SCALE
                    if masked:
                        mine = places_of(q_s[item, HEAD:, 0:TOK])
                        s = jnp.where(place_s[pl.ds(aligned(first), KT), :] <= mine, s, LOW)
                    top = jnp.maximum(m, jnp.max(s, 0, keepdims=True))
                    back = jnp.exp2(m - top)
                    p = jnp.where(s > 0.5 * LOW, jnp.exp2(s - top), 0.0)
                    total = total * back + jnp.sum(p, 0, keepdims=True)
                    acc = acc * back + dot(v_tile(ref, values + first), p.astype(jnp.bfloat16))
                    return top, total, acc

                m, total, acc = lax.fori_loop(0, n // KT, step, (m, total, acc))
            acc_out[item, :, lanes] = acc
            ml_out[item, 0:1, lanes] = m
            ml_out[item, 1:2, lanes] = total
            return carry

        lax.fori_loop(0, GROUP, group, 0)

    def everything(step):
        def body(item, carry):
            step(item)
            return carry

        if n_q == 1:
            step(0)
        else:
            lax.fori_loop(0, n_q, body, 0)

    everything(quick)
    fine = None
    for i in range(n_q):
        total = ml_out[i][1:2, :]
        good = jnp.where((total < TOO_BIG) & (total > TOO_SMALL), 1.0, 0.0)
        fine = good if fine is None else jnp.minimum(fine, good)

    @pl.when(jnp.min(fine) < 0.5)
    def _():
        everything(careful)

    if plan["finish"]:
        for i in range(n_q):
            m, total = ml_out[i][0:1, :], ml_out[i][1:2, :]
            out_refs[i][0:HEAD, :] = (acc_out[i] * (1.0 / total)).astype(jnp.bfloat16)
            out_refs[i][HEAD:, :] = coded_mass(m + jnp.log2(total))


def coded_mass(mass):
    a = mass.astype(jnp.bfloat16).astype(jnp.float32)
    b = (mass - a).astype(jnp.bfloat16).astype(jnp.float32)
    c = mass - a - b
    rows = lax.broadcasted_iota(jnp.int32, (META, ROWS), 0)
    return jnp.where(rows == 0, a, jnp.where(rows == 1, b, jnp.where(rows == 2, c, 0.0))).astype(jnp.bfloat16)


def attend(name, queries, kvs, state=None, fresh=(), finish=False, skip=0):
    n_q = len(queries)
    plan = dict(
        n_q=n_q,
        n_kv=len(kvs),
        n_fresh=len(fresh),
        start=state is None,
        finish=finish,
        skip=skip,
    )
    acc = jax.ShapeDtypeStruct((n_q, HEAD, ROWS), jnp.float32)
    ml = jax.ShapeDtypeStruct((n_q, 8, ROWS), jnp.float32)
    scratch = [pltpu.VMEM((n_q, HEAD + META, ROWS), jnp.bfloat16)]
    if fresh:
        scratch += [
            pltpu.VMEM((2 * len(fresh) * TOK, HEAD), jnp.bfloat16),
            pltpu.VMEM((len(fresh) * TOK, TOK), jnp.float32),
        ]
    if finish:
        outs = [jax.ShapeDtypeStruct((HEAD + META, ROWS), jnp.bfloat16)] * n_q
        scratch += [pltpu.VMEM(acc.shape, jnp.float32), pltpu.VMEM(ml.shape, jnp.float32)]
    else:
        outs = [acc, ml]
    args = list(queries) + list(kvs) + list(fresh) + list(state or ())
    pairs = n_q * (len(kvs) * CHUNK + len(fresh) * TOK) * ROWS
    return pl.pallas_call(
        functools.partial(attend_kernel, plan),
        out_shape=outs,
        in_specs=[VMEM] * len(args),
        out_specs=[VMEM] * len(outs),
        scratch_shapes=scratch,
        compiler_params=pltpu.CompilerParams(vmem_limit_bytes=24 * 2**20),
        cost_estimate=pl.CostEstimate(flops=pairs * 1024, bytes_accessed=0, transcendentals=0),
        name=name,
    )(*args)


def combine_kernel(acc_ref, ml_ref, *refs):
    parts, (att_ref, mass_ref) = refs[:-2], refs[-2:]
    total = ml_ref[0][1:2, :]
    masses = [ml_ref[0][0:1, :] + jnp.log2(total)]
    for r in parts:
        rows = r[HEAD:, :].astype(jnp.float32)
        masses.append(rows[0:1, :] + rows[1:2, :] + rows[2:3, :])
    top = functools.reduce(jnp.maximum, masses)
    weights = [jnp.exp2(m - top) for m in masses]
    den = functools.reduce(jnp.add, weights)
    mass = (top + jnp.log2(den)) * LN2
    shares = [w / den for w in weights]
    shares[0] = shares[0] / total
    for g in range(GROUP):
        lanes = slice(g * TOK, (g + 1) * TOK)
        x = acc_ref[0, :, lanes] * shares[0][:, lanes]
        for r, w in zip(parts, shares[1:]):
            x = x + r[0:HEAD, lanes].astype(jnp.float32) * w[:, lanes]
        att_ref[:, lanes] = x.T.astype(jnp.bfloat16)
    mass_ref[...] = jnp.concatenate([mass[:, g * TOK : (g + 1) * TOK] for g in range(GROUP)], 0)


def prepare(name, kernel, shape, args, specs, work, dtype=jnp.bfloat16):
    return pl.pallas_call(
        kernel,
        out_shape=jax.ShapeDtypeStruct(shape, dtype),
        in_specs=specs,
        out_specs=VMEM,
        compiler_params=pltpu.CompilerParams(vmem_limit_bytes=8 * 2**20),
        cost_estimate=pl.CostEstimate(flops=work, bytes_accessed=0, transcendentals=0),
        name=name,
    )(*args)


def per_device(queries, k, v, fk, fv, positions, order, span):
    order = order.reshape(1, TOK)
    positions = positions.reshape(2 * CHUNK // TOK, TOK)
    angle = prepare("angles", angle_kernel, (HEAD + META, TOK), (order,), [VMEM], 10**9, jnp.float32)
    q0 = prepare("turn_queries", query_kernel, (HEAD + META, ROWS), (queries, angle), [VMEM] * 2, 10**9)
    q_near = [shift(q0, "queries", -1), shift(q0, "queries", 1)]
    first = prepare(
        "turn_keys_first",
        functools.partial(key_kernel, 0),
        (2 * CHUNK, HEAD),
        (k, v, positions),
        [VMEM] * 3,
        2 * 10**9,
    )
    first_near = [shift(first, "keys", -1), shift(first, "keys", 1)]
    second = prepare(
        "turn_keys_second",
        functools.partial(key_kernel, CHUNK),
        (PLACES + META, HEAD),
        (k, v, positions, fk, fv, order, span),
        [VMEM] * 6 + [pl.BlockSpec(memory_space=pltpu.SMEM)],
        2 * 10**9,
    )

    hold = lax.optimization_barrier
    second, q0_late = hold((second, q0))
    q_far = shift(q0_late, "queries", 2)
    state = attend("own", [q0, *q_near], [first, second])
    state, second_late = hold((state, second))
    second_near = [shift(second_late, "keys", -1), shift(second_late, "keys", 1)]
    far = attend("far_early", [q_far], [first, second, *first_near])
    mine = attend("mine_first", [q0], first_near, state)
    far, mine, state, behind, ahead = hold((far, mine, state, first_near[1], second_near[0]))
    first_far = shift(behind, "keys", 1)
    second_far = shift(ahead, "keys", -1)
    near = attend("near_near", q_near, [*first_near, *second_near], state, skip=1)
    far = attend("far_second", [q_far], second_near, far)
    near, far = hold((near, far))
    fresh = [second, *second_near, second_far]
    r_ahead, r_behind = attend("near_last", q_near, [first_far, second_far], near, fresh, finish=True)
    (r_far,) = attend("far_last", [q_far], [first_far, second_far], far, fresh, finish=True)
    back = [shift(r_far, "queries", 2), shift(r_ahead, "queries", 1), shift(r_behind, "queries", -1)]
    mine = attend("mine_rest", [q0], [*second_near, first_far, second_far], mine, fresh)
    attended, mass = pl.pallas_call(
        combine_kernel,
        out_shape=[
            jax.ShapeDtypeStruct((TOK, GROUP * HEAD), jnp.bfloat16),
            jax.ShapeDtypeStruct((GROUP, TOK), jnp.float32),
        ],
        in_specs=[VMEM] * 5,
        out_specs=[VMEM] * 2,
        compiler_params=pltpu.CompilerParams(vmem_limit_bytes=8 * 2**20),
        name="combine",
    )(*mine, *back)
    return attended, mass.T


def solution(mesh):
    spec = (P("ctx", "tp"),) * 5 + (P("ctx"),) * 3
    return jax.shard_map(
        per_device,
        mesh=mesh,
        in_specs=spec,
        out_specs=(P("ctx", "tp"), P("ctx", "tp")),
        check_vma=False,
    )
```

```python
import functools

import jax
import jax.numpy as jnp
import ml_dtypes
import numpy as np
from jax import lax
from jax.experimental import pallas as pl
from jax.experimental.pallas import tpu as pltpu
from jax.sharding import PartitionSpec as P

GROUP = 8
HEAD = 128
TOK = 128
ROWS = GROUP * TOK
CACHED = 32768
SIDE = 4
CHUNK = 1024
TP = 8
KT = 256
SCALE = HEAD**-0.5 * 1.4426950408889634
LN2 = 0.6931471805599453
LOW = -1e30
TOO_BIG = 2.0**100
TOO_SMALL = 2.0**-60
META = 16

VMEM = pl.BlockSpec(memory_space=pltpu.VMEM)


def shift(block, kind, step):
    pairs = []
    for i in range(SIDE * SIDE):
        z, y = divmod(i, SIDE)
        for t in range(TP):
            if (t % 2 == 0) == (kind == "keys"):
                j = z * SIDE + (y + step) % SIDE
            else:
                j = ((z + step) % SIDE) * SIDE + y
            pairs.append((i * TP + t, j * TP + t))
    return lax.ppermute(block, ("ctx", "tp"), pairs)


def _bf(x):
    return np.asarray(x, np.float32).astype(ml_dtypes.bfloat16).astype(np.float64)


def _fit():
    t = np.cos(np.linspace(0, np.pi, 4001)) * 0.5
    u = t * t
    cos = np.polynomial.polynomial.polyfit(u, np.cos(2 * np.pi * t), 8)
    good = np.abs(t) > 1e-3
    sin = np.polynomial.polynomial.polyfit(u[good], np.sin(2 * np.pi * t[good]) / t[good], 7)
    return [float(c) for c in cos], [float(c) for c in sin]


COS, SIN = _fit()


def _turns():
    turns = 500000.0 ** (-2.0 * np.arange(64) / HEAD) / (2 * np.pi)
    first = _bf(turns)
    second = _bf(turns - first)
    return [[float(x) for x in piece] for piece in (first, second, turns - first - second)]


TURNS = _turns()


def spread(constants):
    row = lax.broadcasted_iota(jnp.int32, (8, TOK), 0)
    tiles = []
    for first in range(0, 64, 8):
        tile = jnp.full((8, TOK), constants[first + 7], jnp.float32)
        for i in range(7):
            tile = jnp.where(row == i, constants[first + i], tile)
        tiles.append(tile)
    return jnp.concatenate(tiles, 0)


def angles(positions, turns):
    a = positions * turns[0]
    a = a - jnp.round(a)
    b = positions * turns[1]
    t = a + (b - jnp.round(b)) + positions * turns[2]
    t = t - jnp.round(t)
    u = t * t
    cos = jnp.full_like(u, COS[-1])
    for c in COS[-2::-1]:
        cos = cos * u + c
    sin = jnp.full_like(u, SIN[-1])
    for c in SIN[-2::-1]:
        sin = sin * u + c
    return cos, sin * t


def turned(x, cos, sin):
    lower, upper = x[:64], x[64:]
    return jnp.concatenate([lower * cos - upper * sin, upper * cos + lower * sin], 0)


def coded(places):
    high = jnp.right_shift(places, 4)
    rows = lax.broadcasted_iota(jnp.int32, (META, TOK), 0)
    both = jnp.where(rows == 0, high, jnp.where(rows == 1, places - high * 16, 0))
    return both.astype(jnp.float32).astype(jnp.bfloat16)


def places_of(meta):
    meta = meta.astype(jnp.float32)
    return meta[0:1, :] * 16.0 + meta[1:2, :]


def angle_kernel(order_ref, out_ref):
    order = order_ref[...]
    turns = [spread(piece) for piece in TURNS]
    cos, sin = angles((order + CACHED).astype(jnp.float32), turns)
    out_ref[0:64, :] = cos
    out_ref[64:128, :] = sin
    out_ref[128:, :] = coded(order).astype(jnp.float32)


def query_kernel(q_ref, angle_ref, out_ref):
    cos, sin = angle_ref[0:64, :], angle_ref[64:128, :]
    for g in range(GROUP):
        lanes = slice(g * HEAD, (g + 1) * HEAD)
        x = q_ref[:, lanes].astype(jnp.float32).T
        out_ref[0:HEAD, lanes] = turned(x, cos, sin).astype(jnp.bfloat16)
    out_ref[HEAD:, :] = jnp.concatenate([angle_ref[128:, :].astype(jnp.bfloat16)] * GROUP, 1)


FRESH_KEYS = 2 * CHUNK
FRESH_VALUES = FRESH_KEYS + TOK
PLACES = FRESH_VALUES + TOK


def key_kernel(start, k_ref, v_ref, pos_ref, *refs):
    with_fresh = len(refs) > 1
    if with_fresh:
        fk_ref, fv_ref, order_ref, span_ref, out_ref = refs
    else:
        (out_ref,) = refs
    turns = [spread(piece) for piece in TURNS]

    def keys(x, positions):
        cos, sin = angles(positions.astype(jnp.float32), turns)
        return turned(x.astype(jnp.float32).T, cos, sin).T.astype(jnp.bfloat16)

    def values(x):
        return x.astype(jnp.float32).T.astype(jnp.bfloat16)

    for b in range(CHUNK // TOK):
        rows = slice(start + b * TOK, start + (b + 1) * TOK)
        tile = start // TOK + b
        out_ref[b * TOK : (b + 1) * TOK, :] = keys(k_ref[rows, :], pos_ref[tile : tile + 1, :])
        out_ref[CHUNK + b * TOK : CHUNK + (b + 1) * TOK, :] = values(v_ref[rows, :])
    if with_fresh:
        order = order_ref[...]
        out_ref[FRESH_KEYS:FRESH_VALUES, :] = keys(fk_ref[...], order + CACHED)
        out_ref[FRESH_VALUES:PLACES, :] = values(fv_ref[...])
        lane = lax.broadcasted_iota(jnp.int32, (1, TOK), 1)
        out_ref[PLACES:, :] = coded(jnp.where(lane < span_ref[0], order, 4000))


def dot(a, b):
    return lax.dot_general(a, b, (((1,), (0,)), ((), ())), preferred_element_type=jnp.float32)


def attend_kernel(plan, *refs):
    it = iter(refs)
    n_q, n_fresh = plan["n_q"], plan["n_fresh"]
    q_refs = [next(it) for _ in range(n_q)]
    kv_refs = [next(it) for _ in range(plan["n_kv"])]
    fresh_refs = [next(it) for _ in range(n_fresh)]
    if not plan["start"]:
        acc_in, ml_in = next(it), next(it)
    if plan["finish"]:
        out_refs = [next(it) for _ in range(n_q)]
    else:
        acc_out, ml_out = next(it), next(it)
    q_s = next(it)
    if n_fresh:
        f_s, place_s = next(it), next(it)
    if plan["finish"]:
        acc_out, ml_out = next(it), next(it)

    for i, r in enumerate(q_refs):
        q_s[i] = r[...]
    for i, r in enumerate(fresh_refs):
        f_s[i * TOK : (i + 1) * TOK, :] = r[FRESH_KEYS:FRESH_VALUES, :]
        f_s[(n_fresh + i) * TOK : (n_fresh + i + 1) * TOK, :] = r[FRESH_VALUES:PLACES, :]
        place_s[i * TOK : (i + 1) * TOK, :] = jnp.broadcast_to(places_of(r[PLACES:, :]), (TOK, TOK)).T

    def aligned(i):
        return i if isinstance(i, int) else pl.multiple_of(i, TOK)

    def k_tile(ref, first):
        return ref[pl.ds(aligned(first), KT), :]

    def v_tile(ref, first):
        return jnp.concatenate([ref[pl.ds(aligned(first + j * TOK), TOK), :] for j in range(KT // TOK)], 1)

    def scores(ref, first, item, masked):
        s = dot(k_tile(ref, first), q_s[item, 0:HEAD, :]) * SCALE
        if masked:
            mine = places_of(q_s[item, HEAD:, 0:TOK])
            mask = place_s[pl.ds(aligned(first), KT), :] <= mine
            s = jnp.where(jnp.concatenate([mask] * GROUP, 1), s, LOW)
        return s

    sources = [(ref, CHUNK, CHUNK, False) for ref in kv_refs]
    if n_fresh:
        sources.append((f_s, n_fresh * TOK, n_fresh * TOK, True))

    def old_of(item):
        if plan["start"]:
            return None
        at = item + plan["skip"]
        return ml_in[at][0:1, :], ml_in[at][1:2, :], acc_in[at]

    skip = plan["skip"]

    def put(item, m, total, acc):
        acc_out[item] = acc
        ml_out[item] = jnp.concatenate([m, total, jnp.zeros((6, ROWS), jnp.float32)], 0)

    def quick(item):
        tiles = [(ref, first, values, masked) for ref, values, n, masked in sources for first in range(0, n, KT)]
        old = old_of(item)
        total, acc = (None, None) if old is None else old[1:]
        part = jnp.zeros((8, ROWS), jnp.float32)

        def scores_of(tile):
            return scores(tile[0], tile[1], item, tile[3])

        ahead = scores_of(tiles[0])
        for j, (ref, first, values, _) in enumerate(tiles):
            s = ahead
            if j + 1 < len(tiles):
                ahead = scores_of(tiles[j + 1])
            p = jnp.exp2(s)
            part = part + jnp.sum(p.reshape(KT // 8, 8, ROWS), 0)
            pv = dot(v_tile(ref, values + first), p.astype(jnp.bfloat16))
            acc = pv if acc is None else acc + pv
        part = jnp.sum(part, 0, keepdims=True)
        put(item, jnp.zeros((1, ROWS), jnp.float32), part if total is None else total + part, acc)

    def careful(item):
        def group(g, carry):
            lanes = pl.ds(aligned(g * TOK), TOK)
            if plan["start"]:
                m = jnp.full((1, TOK), LOW, jnp.float32)
                total = jnp.zeros((1, TOK), jnp.float32)
                acc = jnp.zeros((HEAD, TOK), jnp.float32)
            else:
                at = item + skip
                m, total, acc = ml_in[at, 0:1, lanes], ml_in[at, 1:2, lanes], acc_in[at, :, lanes]
            q = q_s[item, 0:HEAD, lanes]
            for ref, values, n, masked in sources:

                def step(t, state, ref=ref, values=values, masked=masked):
                    m, total, acc = state
                    first = t * KT
                    s = dot(k_tile(ref, first), q) * SCALE
                    if masked:
                        mine = places_of(q_s[item, HEAD:, 0:TOK])
                        s = jnp.where(place_s[pl.ds(aligned(first), KT), :] <= mine, s, LOW)
                    top = jnp.maximum(m, jnp.max(s, 0, keepdims=True))
                    back = jnp.exp2(m - top)
                    p = jnp.where(s > 0.5 * LOW, jnp.exp2(s - top), 0.0)
                    total = total * back + jnp.sum(p, 0, keepdims=True)
                    acc = acc * back + dot(v_tile(ref, values + first), p.astype(jnp.bfloat16))
                    return top, total, acc

                m, total, acc = lax.fori_loop(0, n // KT, step, (m, total, acc))
            acc_out[item, :, lanes] = acc
            ml_out[item, 0:1, lanes] = m
            ml_out[item, 1:2, lanes] = total
            return carry

        lax.fori_loop(0, GROUP, group, 0)

    def everything(step):
        def body(item, carry):
            step(item)
            return carry

        if n_q == 1:
            step(0)
        else:
            lax.fori_loop(0, n_q, body, 0)

    everything(quick)
    fine = None
    for i in range(n_q):
        total = ml_out[i][1:2, :]
        good = jnp.where((total < TOO_BIG) & (total > TOO_SMALL), 1.0, 0.0)
        if not plan["start"]:
            good = jnp.where(ml_in[i + skip][0:1, :] == 0.0, good, 0.0)
        fine = good if fine is None else jnp.minimum(fine, good)

    @pl.when(jnp.min(fine) < 0.5)
    def _():
        everything(careful)

    if plan["finish"]:
        for i in range(n_q):
            m, total = ml_out[i][0:1, :], ml_out[i][1:2, :]
            out_refs[i][0:HEAD, :] = (acc_out[i] * (1.0 / total)).astype(jnp.bfloat16)
            out_refs[i][HEAD:, :] = coded_mass(m + jnp.log2(total))


def coded_mass(mass):
    a = mass.astype(jnp.bfloat16).astype(jnp.float32)
    b = (mass - a).astype(jnp.bfloat16).astype(jnp.float32)
    c = mass - a - b
    rows = lax.broadcasted_iota(jnp.int32, (META, ROWS), 0)
    return jnp.where(rows == 0, a, jnp.where(rows == 1, b, jnp.where(rows == 2, c, 0.0))).astype(jnp.bfloat16)


def attend(name, queries, kvs, state=None, fresh=(), finish=False, skip=0):
    n_q = len(queries)
    plan = dict(
        n_q=n_q,
        n_kv=len(kvs),
        n_fresh=len(fresh),
        start=state is None,
        finish=finish,
        skip=skip,
    )
    acc = jax.ShapeDtypeStruct((n_q, HEAD, ROWS), jnp.float32)
    ml = jax.ShapeDtypeStruct((n_q, 8, ROWS), jnp.float32)
    scratch = [pltpu.VMEM((n_q, HEAD + META, ROWS), jnp.bfloat16)]
    if fresh:
        scratch += [
            pltpu.VMEM((2 * len(fresh) * TOK, HEAD), jnp.bfloat16),
            pltpu.VMEM((len(fresh) * TOK, TOK), jnp.float32),
        ]
    if finish:
        outs = [jax.ShapeDtypeStruct((HEAD + META, ROWS), jnp.bfloat16)] * n_q
        scratch += [pltpu.VMEM(acc.shape, jnp.float32), pltpu.VMEM(ml.shape, jnp.float32)]
    else:
        outs = [acc, ml]
    args = list(queries) + list(kvs) + list(fresh) + list(state or ())
    pairs = n_q * (len(kvs) * CHUNK + len(fresh) * TOK) * ROWS
    return pl.pallas_call(
        functools.partial(attend_kernel, plan),
        out_shape=outs,
        in_specs=[VMEM] * len(args),
        out_specs=[VMEM] * len(outs),
        scratch_shapes=scratch,
        compiler_params=pltpu.CompilerParams(vmem_limit_bytes=24 * 2**20),
        cost_estimate=pl.CostEstimate(flops=pairs * 1024, bytes_accessed=0, transcendentals=0),
        name=name,
    )(*args)


def combine_kernel(acc_ref, ml_ref, *refs):
    parts, (att_ref, mass_ref) = refs[:-2], refs[-2:]
    total = ml_ref[0][1:2, :]
    masses = [ml_ref[0][0:1, :] + jnp.log2(total)]
    for r in parts:
        rows = r[HEAD:, :].astype(jnp.float32)
        masses.append(rows[0:1, :] + rows[1:2, :] + rows[2:3, :])
    top = functools.reduce(jnp.maximum, masses)
    weights = [jnp.exp2(m - top) for m in masses]
    den = functools.reduce(jnp.add, weights)
    mass = (top + jnp.log2(den)) * LN2
    shares = [w / den for w in weights]
    shares[0] = shares[0] / total
    for g in range(GROUP):
        lanes = slice(g * TOK, (g + 1) * TOK)
        x = acc_ref[0, :, lanes] * shares[0][:, lanes]
        for r, w in zip(parts, shares[1:]):
            x = x + r[0:HEAD, lanes].astype(jnp.float32) * w[:, lanes]
        att_ref[:, lanes] = x.T.astype(jnp.bfloat16)
    mass_ref[...] = jnp.concatenate([mass[:, g * TOK : (g + 1) * TOK] for g in range(GROUP)], 0)


def prepare(name, kernel, shape, args, specs, work, dtype=jnp.bfloat16):
    return pl.pallas_call(
        kernel,
        out_shape=jax.ShapeDtypeStruct(shape, dtype),
        in_specs=specs,
        out_specs=VMEM,
        compiler_params=pltpu.CompilerParams(vmem_limit_bytes=8 * 2**20),
        cost_estimate=pl.CostEstimate(flops=work, bytes_accessed=0, transcendentals=0),
        name=name,
    )(*args)


def per_device(queries, k, v, fk, fv, positions, order, span):
    order = order.reshape(1, TOK)
    positions = positions.reshape(2 * CHUNK // TOK, TOK)
    angle = prepare("angles", angle_kernel, (HEAD + META, TOK), (order,), [VMEM], 10**9, jnp.float32)
    q0 = prepare("turn_queries", query_kernel, (HEAD + META, ROWS), (queries, angle), [VMEM] * 2, 10**9)
    q_near = [shift(q0, "queries", -1), shift(q0, "queries", 1)]
    q_far = shift(q0, "queries", 2)

    first = prepare(
        "turn_keys_first",
        functools.partial(key_kernel, 0),
        (2 * CHUNK, HEAD),
        (k, v, positions),
        [VMEM] * 3,
        2 * 10**9,
    )
    first_near = [shift(first, "keys", -1), shift(first, "keys", 1)]
    second = prepare(
        "turn_keys_second",
        functools.partial(key_kernel, CHUNK),
        (PLACES + META, HEAD),
        (k, v, positions, fk, fv, order, span),
        [VMEM] * 6 + [pl.BlockSpec(memory_space=pltpu.SMEM)],
        2 * 10**9,
    )
    second_near = [shift(second, "keys", -1), shift(second, "keys", 1)]

    mine = attend("mine_own", [q0], [first, second])
    state = attend("others_own", [q_far, *q_near], [first, second])
    far = attend("far_first", [q_far], first_near, state)
    far, state, behind, ahead = lax.optimization_barrier((far, state, first_near[1], second_near[0]))
    first_far = shift(behind, "keys", 1)
    second_far = shift(ahead, "keys", -1)
    near = attend("near_near", q_near, [*first_near, *second_near], state, skip=1)
    far = attend("far_second", [q_far], second_near, far)
    near, far = lax.optimization_barrier((near, far))
    fresh = [second, *second_near, second_far]
    r_ahead, r_behind = attend("near_last", q_near, [first_far, second_far], near, fresh, finish=True)
    (r_far,) = attend("far_last", [q_far], [first_far, second_far], far, fresh, finish=True)
    back = [shift(r_far, "queries", 2), shift(r_ahead, "queries", 1), shift(r_behind, "queries", -1)]
    mine = attend("mine_rest", [q0], [*first_near, *second_near, first_far, second_far], mine, fresh)
    attended, mass = pl.pallas_call(
        combine_kernel,
        out_shape=[
            jax.ShapeDtypeStruct((TOK, GROUP * HEAD), jnp.bfloat16),
            jax.ShapeDtypeStruct((GROUP, TOK), jnp.float32),
        ],
        in_specs=[VMEM] * 5,
        out_specs=[VMEM] * 2,
        compiler_params=pltpu.CompilerParams(vmem_limit_bytes=8 * 2**20),
        name="combine",
    )(*mine, *back)
    return attended, mass.T


def solution(mesh):
    spec = (P("ctx", "tp"),) * 5 + (P("ctx"),) * 3
    return jax.shard_map(
        per_device,
        mesh=mesh,
        in_specs=spec,
        out_specs=(P("ctx", "tp"), P("ctx", "tp")),
        check_vma=False,
    )
```

```python
import functools

import jax
import jax.numpy as jnp
import ml_dtypes
import numpy as np
from jax import lax
from jax.experimental import pallas as pl
from jax.experimental.pallas import tpu as pltpu
from jax.sharding import PartitionSpec as P

GROUP = 8
HEAD = 128
TOK = 128
ROWS = GROUP * TOK
CACHED = 32768
SIDE = 4
CHUNK = 1024
TP = 8
KT = 256
SCALE = HEAD**-0.5 * 1.4426950408889634
LN2 = 0.6931471805599453
LOW = -1e30
TOO_BIG = 2.0**100
TOO_SMALL = 2.0**-60
META = 16

VMEM = pl.BlockSpec(memory_space=pltpu.VMEM)


def shift(block, kind, step):
    pairs = []
    for i in range(SIDE * SIDE):
        z, y = divmod(i, SIDE)
        for t in range(TP):
            if (t % 2 == 0) == (kind == "keys"):
                j = z * SIDE + (y + step) % SIDE
            else:
                j = ((z + step) % SIDE) * SIDE + y
            pairs.append((i * TP + t, j * TP + t))
    return lax.ppermute(block, ("ctx", "tp"), pairs)


def _bf(x):
    return np.asarray(x, np.float32).astype(ml_dtypes.bfloat16).astype(np.float64)


def _fit():
    t = np.cos(np.linspace(0, np.pi, 4001)) * 0.5
    u = t * t
    cos = np.polynomial.polynomial.polyfit(u, np.cos(2 * np.pi * t), 8)
    good = np.abs(t) > 1e-3
    sin = np.polynomial.polynomial.polyfit(u[good], np.sin(2 * np.pi * t[good]) / t[good], 7)
    return [float(c) for c in cos], [float(c) for c in sin]


COS, SIN = _fit()


def _turns():
    turns = 500000.0 ** (-2.0 * np.arange(64) / HEAD) / (2 * np.pi)
    first = _bf(turns)
    second = _bf(turns - first)
    return [[float(x) for x in piece] for piece in (first, second, turns - first - second)]


TURNS = _turns()


def spread(constants):
    row = lax.broadcasted_iota(jnp.int32, (8, TOK), 0)
    tiles = []
    for first in range(0, 64, 8):
        tile = jnp.full((8, TOK), constants[first + 7], jnp.float32)
        for i in range(7):
            tile = jnp.where(row == i, constants[first + i], tile)
        tiles.append(tile)
    return jnp.concatenate(tiles, 0)


def angles(positions, turns):
    a = positions * turns[0]
    a = a - jnp.round(a)
    b = positions * turns[1]
    t = a + (b - jnp.round(b)) + positions * turns[2]
    t = t - jnp.round(t)
    u = t * t
    cos = jnp.full_like(u, COS[-1])
    for c in COS[-2::-1]:
        cos = cos * u + c
    sin = jnp.full_like(u, SIN[-1])
    for c in SIN[-2::-1]:
        sin = sin * u + c
    return cos, sin * t


def turned(x, cos, sin):
    lower, upper = x[:64], x[64:]
    return jnp.concatenate([lower * cos - upper * sin, upper * cos + lower * sin], 0)


def coded(places):
    high = jnp.right_shift(places, 4)
    rows = lax.broadcasted_iota(jnp.int32, (META, TOK), 0)
    both = jnp.where(rows == 0, high, jnp.where(rows == 1, places - high * 16, 0))
    return both.astype(jnp.float32).astype(jnp.bfloat16)


def places_of(meta):
    meta = meta.astype(jnp.float32)
    return meta[0:1, :] * 16.0 + meta[1:2, :]


def angle_kernel(order_ref, out_ref):
    order = order_ref[...]
    turns = [spread(piece) for piece in TURNS]
    cos, sin = angles((order + CACHED).astype(jnp.float32), turns)
    out_ref[0:64, :] = cos
    out_ref[64:128, :] = sin
    out_ref[128:, :] = coded(order).astype(jnp.float32)


def query_kernel(q_ref, angle_ref, out_ref):
    cos, sin = angle_ref[0:64, :], angle_ref[64:128, :]
    for g in range(GROUP):
        lanes = slice(g * HEAD, (g + 1) * HEAD)
        x = q_ref[:, lanes].astype(jnp.float32).T
        out_ref[0:HEAD, lanes] = turned(x, cos, sin).astype(jnp.bfloat16)
    out_ref[HEAD:, :] = jnp.concatenate([angle_ref[128:, :].astype(jnp.bfloat16)] * GROUP, 1)


FRESH_KEYS = 2 * CHUNK
FRESH_VALUES = FRESH_KEYS + TOK
PLACES = FRESH_VALUES + TOK


def key_kernel(start, k_ref, v_ref, pos_ref, *refs):
    with_fresh = len(refs) > 1
    if with_fresh:
        fk_ref, fv_ref, order_ref, span_ref, out_ref = refs
    else:
        (out_ref,) = refs
    turns = [spread(piece) for piece in TURNS]

    def keys(x, positions):
        cos, sin = angles(positions.astype(jnp.float32), turns)
        return turned(x.astype(jnp.float32).T, cos, sin).T.astype(jnp.bfloat16)

    def values(x):
        return x.astype(jnp.float32).T.astype(jnp.bfloat16)

    for b in range(CHUNK // TOK):
        rows = slice(start + b * TOK, start + (b + 1) * TOK)
        tile = start // TOK + b
        out_ref[b * TOK : (b + 1) * TOK, :] = keys(k_ref[rows, :], pos_ref[tile : tile + 1, :])
        out_ref[CHUNK + b * TOK : CHUNK + (b + 1) * TOK, :] = values(v_ref[rows, :])
    if with_fresh:
        order = order_ref[...]
        out_ref[FRESH_KEYS:FRESH_VALUES, :] = keys(fk_ref[...], order + CACHED)
        out_ref[FRESH_VALUES:PLACES, :] = values(fv_ref[...])
        lane = lax.broadcasted_iota(jnp.int32, (1, TOK), 1)
        out_ref[PLACES:, :] = coded(jnp.where(lane < span_ref[0], order, 4000))


def dot(a, b):
    return lax.dot_general(a, b, (((1,), (0,)), ((), ())), preferred_element_type=jnp.float32)


def attend_kernel(plan, *refs):
    it = iter(refs)
    n_q, n_fresh = plan["n_q"], plan["n_fresh"]
    q_refs = [next(it) for _ in range(n_q)]
    kv_refs = [next(it) for _ in range(plan["n_kv"])]
    fresh_refs = [next(it) for _ in range(n_fresh)]
    if not plan["start"]:
        acc_in, ml_in = next(it), next(it)
    if plan["finish"]:
        out_refs = [next(it) for _ in range(n_q)]
    else:
        acc_out, ml_out = next(it), next(it)
    q_s = next(it)
    if n_fresh:
        f_s, place_s = next(it), next(it)
    if plan["finish"]:
        acc_out, ml_out = next(it), next(it)

    for i, r in enumerate(q_refs):
        q_s[i] = r[...]
    for i, r in enumerate(fresh_refs):
        f_s[i * TOK : (i + 1) * TOK, :] = r[FRESH_KEYS:FRESH_VALUES, :]
        f_s[(n_fresh + i) * TOK : (n_fresh + i + 1) * TOK, :] = r[FRESH_VALUES:PLACES, :]
        place_s[i * TOK : (i + 1) * TOK, :] = jnp.broadcast_to(places_of(r[PLACES:, :]), (TOK, TOK)).T

    def aligned(i):
        return i if isinstance(i, int) else pl.multiple_of(i, TOK)

    def k_tile(ref, first):
        return ref[pl.ds(aligned(first), KT), :]

    def v_tile(ref, first):
        return jnp.concatenate([ref[pl.ds(aligned(first + j * TOK), TOK), :] for j in range(KT // TOK)], 1)

    def scores(ref, first, item, masked):
        s = dot(k_tile(ref, first), q_s[item, 0:HEAD, :]) * SCALE
        if masked:
            mine = places_of(q_s[item, HEAD:, 0:TOK])
            mask = place_s[pl.ds(aligned(first), KT), :] <= mine
            s = jnp.where(jnp.concatenate([mask] * GROUP, 1), s, LOW)
        return s

    sources = [(ref, CHUNK, CHUNK, False) for ref in kv_refs]
    if n_fresh:
        sources.append((f_s, n_fresh * TOK, n_fresh * TOK, True))

    def old_of(item):
        if plan["start"]:
            return None
        at = item + plan["skip"]
        return ml_in[at][0:1, :], ml_in[at][1:2, :], acc_in[at]

    skip = plan["skip"]

    def put(item, m, total, acc):
        acc_out[item] = acc
        ml_out[item] = jnp.concatenate([m, total, jnp.zeros((6, ROWS), jnp.float32)], 0)

    def quick(item):
        tiles = [(ref, first, values, masked) for ref, values, n, masked in sources for first in range(0, n, KT)]
        old = old_of(item)
        total, acc = (None, None) if old is None else old[1:]
        part = jnp.zeros((8, ROWS), jnp.float32)

        def scores_of(tile):
            return scores(tile[0], tile[1], item, tile[3])

        ahead = scores_of(tiles[0])
        for j, (ref, first, values, _) in enumerate(tiles):
            s = ahead
            if j + 1 < len(tiles):
                ahead = scores_of(tiles[j + 1])
            p = jnp.exp2(s)
            part = part + jnp.sum(p.reshape(KT // 8, 8, ROWS), 0)
            pv = dot(v_tile(ref, values + first), p.astype(jnp.bfloat16))
            acc = pv if acc is None else acc + pv
        part = jnp.sum(part, 0, keepdims=True)
        put(item, jnp.zeros((1, ROWS), jnp.float32), part if total is None else total + part, acc)

    def careful(item):
        def group(g, carry):
            lanes = pl.ds(aligned(g * TOK), TOK)
            if plan["start"]:
                m = jnp.full((1, TOK), LOW, jnp.float32)
                total = jnp.zeros((1, TOK), jnp.float32)
                acc = jnp.zeros((HEAD, TOK), jnp.float32)
            else:
                at = item + skip
                m, total, acc = ml_in[at, 0:1, lanes], ml_in[at, 1:2, lanes], acc_in[at, :, lanes]
            q = q_s[item, 0:HEAD, lanes]
            for ref, values, n, masked in sources:

                def step(t, state, ref=ref, values=values, masked=masked):
                    m, total, acc = state
                    first = t * KT
                    s = dot(k_tile(ref, first), q) * SCALE
                    if masked:
                        mine = places_of(q_s[item, HEAD:, 0:TOK])
                        s = jnp.where(place_s[pl.ds(aligned(first), KT), :] <= mine, s, LOW)
                    top = jnp.maximum(m, jnp.max(s, 0, keepdims=True))
                    back = jnp.exp2(m - top)
                    p = jnp.where(s > 0.5 * LOW, jnp.exp2(s - top), 0.0)
                    total = total * back + jnp.sum(p, 0, keepdims=True)
                    acc = acc * back + dot(v_tile(ref, values + first), p.astype(jnp.bfloat16))
                    return top, total, acc

                m, total, acc = lax.fori_loop(0, n // KT, step, (m, total, acc))
            acc_out[item, :, lanes] = acc
            ml_out[item, 0:1, lanes] = m
            ml_out[item, 1:2, lanes] = total
            return carry

        lax.fori_loop(0, GROUP, group, 0)

    def everything(step):
        def body(item, carry):
            step(item)
            return carry

        if n_q == 1:
            step(0)
        else:
            lax.fori_loop(0, n_q, body, 0)

    everything(quick)
    fine = None
    for i in range(n_q):
        total = ml_out[i][1:2, :]
        good = jnp.where((total < TOO_BIG) & (total > TOO_SMALL), 1.0, 0.0)
        if not plan["start"]:
            good = jnp.where(ml_in[i + skip][0:1, :] == 0.0, good, 0.0)
        fine = good if fine is None else jnp.minimum(fine, good)

    @pl.when(jnp.min(fine) < 0.5)
    def _():
        everything(careful)

    if plan["finish"]:
        for i in range(n_q):
            m, total = ml_out[i][0:1, :], ml_out[i][1:2, :]
            out_refs[i][0:HEAD, :] = (acc_out[i] * (1.0 / total)).astype(jnp.bfloat16)
            out_refs[i][HEAD:, :] = coded_mass(m + jnp.log2(total))


def coded_mass(mass):
    a = mass.astype(jnp.bfloat16).astype(jnp.float32)
    b = (mass - a).astype(jnp.bfloat16).astype(jnp.float32)
    c = mass - a - b
    rows = lax.broadcasted_iota(jnp.int32, (META, ROWS), 0)
    return jnp.where(rows == 0, a, jnp.where(rows == 1, b, jnp.where(rows == 2, c, 0.0))).astype(jnp.bfloat16)


def attend(name, queries, kvs, state=None, fresh=(), finish=False, skip=0):
    n_q = len(queries)
    plan = dict(
        n_q=n_q,
        n_kv=len(kvs),
        n_fresh=len(fresh),
        start=state is None,
        finish=finish,
        skip=skip,
    )
    acc = jax.ShapeDtypeStruct((n_q, HEAD, ROWS), jnp.float32)
    ml = jax.ShapeDtypeStruct((n_q, 8, ROWS), jnp.float32)
    scratch = [pltpu.VMEM((n_q, HEAD + META, ROWS), jnp.bfloat16)]
    if fresh:
        scratch += [
            pltpu.VMEM((2 * len(fresh) * TOK, HEAD), jnp.bfloat16),
            pltpu.VMEM((len(fresh) * TOK, TOK), jnp.float32),
        ]
    if finish:
        outs = [jax.ShapeDtypeStruct((HEAD + META, ROWS), jnp.bfloat16)] * n_q
        scratch += [pltpu.VMEM(acc.shape, jnp.float32), pltpu.VMEM(ml.shape, jnp.float32)]
    else:
        outs = [acc, ml]
    args = list(queries) + list(kvs) + list(fresh) + list(state or ())
    pairs = n_q * (len(kvs) * CHUNK + len(fresh) * TOK) * ROWS
    return pl.pallas_call(
        functools.partial(attend_kernel, plan),
        out_shape=outs,
        in_specs=[VMEM] * len(args),
        out_specs=[VMEM] * len(outs),
        scratch_shapes=scratch,
        compiler_params=pltpu.CompilerParams(vmem_limit_bytes=24 * 2**20),
        cost_estimate=pl.CostEstimate(flops=pairs * 1024, bytes_accessed=0, transcendentals=0),
        name=name,
    )(*args)


def combine_kernel(acc_ref, ml_ref, *refs):
    parts, (att_ref, mass_ref) = refs[:-2], refs[-2:]
    total = ml_ref[0][1:2, :]
    masses = [ml_ref[0][0:1, :] + jnp.log2(total)]
    for r in parts:
        rows = r[HEAD:, :].astype(jnp.float32)
        masses.append(rows[0:1, :] + rows[1:2, :] + rows[2:3, :])
    top = functools.reduce(jnp.maximum, masses)
    weights = [jnp.exp2(m - top) for m in masses]
    den = functools.reduce(jnp.add, weights)
    mass = (top + jnp.log2(den)) * LN2
    shares = [w / den for w in weights]
    shares[0] = shares[0] / total
    for g in range(GROUP):
        lanes = slice(g * TOK, (g + 1) * TOK)
        x = acc_ref[0, :, lanes] * shares[0][:, lanes]
        for r, w in zip(parts, shares[1:]):
            x = x + r[0:HEAD, lanes].astype(jnp.float32) * w[:, lanes]
        att_ref[:, lanes] = x.T.astype(jnp.bfloat16)
    mass_ref[...] = jnp.concatenate([mass[:, g * TOK : (g + 1) * TOK] for g in range(GROUP)], 0)


def prepare(name, kernel, shape, args, specs, work, dtype=jnp.bfloat16):
    return pl.pallas_call(
        kernel,
        out_shape=jax.ShapeDtypeStruct(shape, dtype),
        in_specs=specs,
        out_specs=VMEM,
        compiler_params=pltpu.CompilerParams(vmem_limit_bytes=8 * 2**20),
        cost_estimate=pl.CostEstimate(flops=work, bytes_accessed=0, transcendentals=0),
        name=name,
    )(*args)


def per_device(queries, k, v, fk, fv, positions, order, span):
    order = order.reshape(1, TOK)
    positions = positions.reshape(2 * CHUNK // TOK, TOK)
    angle = prepare("angles", angle_kernel, (HEAD + META, TOK), (order,), [VMEM], 10**9, jnp.float32)
    q0 = prepare("turn_queries", query_kernel, (HEAD + META, ROWS), (queries, angle), [VMEM] * 2, 10**9)
    q_near = [shift(q0, "queries", -1), shift(q0, "queries", 1)]
    first = prepare(
        "turn_keys_first",
        functools.partial(key_kernel, 0),
        (2 * CHUNK, HEAD),
        (k, v, positions),
        [VMEM] * 3,
        2 * 10**9,
    )
    first, q0_late = lax.optimization_barrier((first, q0))
    q_far = shift(q0_late, "queries", 2)
    first_near = [shift(first, "keys", -1), shift(first, "keys", 1)]
    second = prepare(
        "turn_keys_second",
        functools.partial(key_kernel, CHUNK),
        (PLACES + META, HEAD),
        (k, v, positions, fk, fv, order, span),
        [VMEM] * 6 + [pl.BlockSpec(memory_space=pltpu.SMEM)],
        2 * 10**9,
    )
    second_late, q_near = lax.optimization_barrier((second, q_near))
    second_near = [shift(second_late, "keys", -1), shift(second_late, "keys", 1)]

    mine = attend("mine_own", [q0], [first, second])
    state = attend("others_own", [*q_near, q_far], [first, second])
    far = attend("far_first", [q_far], first_near, state, skip=2)
    far, state, behind, ahead = lax.optimization_barrier((far, state, first_near[1], second_near[0]))
    first_far = shift(behind, "keys", 1)
    second_far = shift(ahead, "keys", -1)
    near = attend("near_near", q_near, [*first_near, *second_near], state)
    far = attend("far_second", [q_far], second_near, far)
    near, far = lax.optimization_barrier((near, far))
    fresh = [second, *second_near, second_far]
    r_ahead, r_behind = attend("near_last", q_near, [first_far, second_far], near, fresh, finish=True)
    (r_far,) = attend("far_last", [q_far], [first_far, second_far], far, fresh, finish=True)
    back = [shift(r_far, "queries", 2), shift(r_ahead, "queries", 1), shift(r_behind, "queries", -1)]
    mine = attend("mine_rest", [q0], [*first_near, *second_near, first_far, second_far], mine, fresh)
    attended, mass = pl.pallas_call(
        combine_kernel,
        out_shape=[
            jax.ShapeDtypeStruct((TOK, GROUP * HEAD), jnp.bfloat16),
            jax.ShapeDtypeStruct((GROUP, TOK), jnp.float32),
        ],
        in_specs=[VMEM] * 5,
        out_specs=[VMEM] * 2,
        compiler_params=pltpu.CompilerParams(vmem_limit_bytes=8 * 2**20),
        name="combine",
    )(*mine, *back)
    return attended, mass.T


def solution(mesh):
    spec = (P("ctx", "tp"),) * 5 + (P("ctx"),) * 3
    return jax.shard_map(
        per_device,
        mesh=mesh,
        in_specs=spec,
        out_specs=(P("ctx", "tp"), P("ctx", "tp")),
        check_vma=False,
    )
```

```python
import functools

import jax
import jax.numpy as jnp
import ml_dtypes
import numpy as np
from jax import lax
from jax.experimental import pallas as pl
from jax.experimental.pallas import tpu as pltpu
from jax.sharding import PartitionSpec as P

GROUP = 8
HEAD = 128
TOK = 128
ROWS = GROUP * TOK
CACHED = 32768
SIDE = 4
CHUNK = 1024
TP = 8
KT = 256
SCALE = HEAD**-0.5 * 1.4426950408889634
LN2 = 0.6931471805599453
LOW = -1e30
TOO_BIG = 2.0**100
TOO_SMALL = 2.0**-60
META = 16

VMEM = pl.BlockSpec(memory_space=pltpu.VMEM)


def shift(block, kind, step):
    pairs = []
    for i in range(SIDE * SIDE):
        z, y = divmod(i, SIDE)
        for t in range(TP):
            if (t % 2 == 0) == (kind == "keys"):
                j = z * SIDE + (y + step) % SIDE
            else:
                j = ((z + step) % SIDE) * SIDE + y
            pairs.append((i * TP + t, j * TP + t))
    return lax.ppermute(block, ("ctx", "tp"), pairs)


def _bf(x):
    return np.asarray(x, np.float32).astype(ml_dtypes.bfloat16).astype(np.float64)


def _fit():
    t = np.cos(np.linspace(0, np.pi, 4001)) * 0.5
    u = t * t
    cos = np.polynomial.polynomial.polyfit(u, np.cos(2 * np.pi * t), 8)
    good = np.abs(t) > 1e-3
    sin = np.polynomial.polynomial.polyfit(u[good], np.sin(2 * np.pi * t[good]) / t[good], 7)
    return [float(c) for c in cos], [float(c) for c in sin]


COS, SIN = _fit()


def _turns():
    turns = 500000.0 ** (-2.0 * np.arange(64) / HEAD) / (2 * np.pi)
    first = _bf(turns)
    second = _bf(turns - first)
    return [[float(x) for x in piece] for piece in (first, second, turns - first - second)]


TURNS = _turns()


def spread(constants):
    row = lax.broadcasted_iota(jnp.int32, (8, TOK), 0)
    tiles = []
    for first in range(0, 64, 8):
        tile = jnp.full((8, TOK), constants[first + 7], jnp.float32)
        for i in range(7):
            tile = jnp.where(row == i, constants[first + i], tile)
        tiles.append(tile)
    return jnp.concatenate(tiles, 0)


def angles(positions, turns):
    a = positions * turns[0]
    a = a - jnp.round(a)
    b = positions * turns[1]
    t = a + (b - jnp.round(b)) + positions * turns[2]
    t = t - jnp.round(t)
    u = t * t
    cos = jnp.full_like(u, COS[-1])
    for c in COS[-2::-1]:
        cos = cos * u + c
    sin = jnp.full_like(u, SIN[-1])
    for c in SIN[-2::-1]:
        sin = sin * u + c
    return cos, sin * t


def turned(x, cos, sin):
    lower, upper = x[:64], x[64:]
    return jnp.concatenate([lower * cos - upper * sin, upper * cos + lower * sin], 0)


def coded(places):
    high = jnp.right_shift(places, 4)
    rows = lax.broadcasted_iota(jnp.int32, (META, TOK), 0)
    both = jnp.where(rows == 0, high, jnp.where(rows == 1, places - high * 16, 0))
    return both.astype(jnp.float32).astype(jnp.bfloat16)


def places_of(meta):
    meta = meta.astype(jnp.float32)
    return meta[0:1, :] * 16.0 + meta[1:2, :]


def angle_kernel(order_ref, out_ref):
    order = order_ref[...]
    turns = [spread(piece) for piece in TURNS]
    cos, sin = angles((order + CACHED).astype(jnp.float32), turns)
    out_ref[0:64, :] = cos
    out_ref[64:128, :] = sin
    out_ref[128:, :] = coded(order).astype(jnp.float32)


def query_kernel(q_ref, angle_ref, out_ref):
    cos, sin = angle_ref[0:64, :], angle_ref[64:128, :]
    for g in range(GROUP):
        lanes = slice(g * HEAD, (g + 1) * HEAD)
        x = q_ref[:, lanes].astype(jnp.float32).T
        out_ref[0:HEAD, lanes] = turned(x, cos, sin).astype(jnp.bfloat16)
    out_ref[HEAD:, :] = jnp.concatenate([angle_ref[128:, :].astype(jnp.bfloat16)] * GROUP, 1)


FRESH_KEYS = 2 * CHUNK
FRESH_VALUES = FRESH_KEYS + TOK
PLACES = FRESH_VALUES + TOK


def key_kernel(start, k_ref, v_ref, pos_ref, *refs):
    with_fresh = len(refs) > 1
    if with_fresh:
        fk_ref, fv_ref, order_ref, span_ref, out_ref = refs
    else:
        (out_ref,) = refs
    turns = [spread(piece) for piece in TURNS]

    def keys(x, positions):
        cos, sin = angles(positions.astype(jnp.float32), turns)
        return turned(x.astype(jnp.float32).T, cos, sin).T.astype(jnp.bfloat16)

    def values(x):
        return x.astype(jnp.float32).T.astype(jnp.bfloat16)

    for b in range(CHUNK // TOK):
        rows = slice(start + b * TOK, start + (b + 1) * TOK)
        tile = start // TOK + b
        out_ref[b * TOK : (b + 1) * TOK, :] = keys(k_ref[rows, :], pos_ref[tile : tile + 1, :])
        out_ref[CHUNK + b * TOK : CHUNK + (b + 1) * TOK, :] = values(v_ref[rows, :])
    if with_fresh:
        order = order_ref[...]
        out_ref[FRESH_KEYS:FRESH_VALUES, :] = keys(fk_ref[...], order + CACHED)
        out_ref[FRESH_VALUES:PLACES, :] = values(fv_ref[...])
        lane = lax.broadcasted_iota(jnp.int32, (1, TOK), 1)
        out_ref[PLACES:, :] = coded(jnp.where(lane < span_ref[0], order, 4000))


def dot(a, b):
    return lax.dot_general(a, b, (((1,), (0,)), ((), ())), preferred_element_type=jnp.float32)


def attend_kernel(plan, *refs):
    it = iter(refs)
    n_q, n_fresh = plan["n_q"], plan["n_fresh"]
    q_refs = [next(it) for _ in range(n_q)]
    kv_refs = [next(it) for _ in range(plan["n_kv"])]
    fresh_refs = [next(it) for _ in range(n_fresh)]
    if not plan["start"]:
        acc_in, ml_in = next(it), next(it)
    if plan["finish"]:
        out_refs = [next(it) for _ in range(n_q)]
    else:
        acc_out, ml_out = next(it), next(it)
    q_s = next(it)
    if n_fresh:
        f_s, place_s = next(it), next(it)
    if plan["finish"]:
        acc_out, ml_out = next(it), next(it)

    for i, r in enumerate(q_refs):
        q_s[i] = r[...]
    for i, r in enumerate(fresh_refs):
        f_s[i * TOK : (i + 1) * TOK, :] = r[FRESH_KEYS:FRESH_VALUES, :]
        f_s[(n_fresh + i) * TOK : (n_fresh + i + 1) * TOK, :] = r[FRESH_VALUES:PLACES, :]
        place_s[i * TOK : (i + 1) * TOK, :] = jnp.broadcast_to(places_of(r[PLACES:, :]), (TOK, TOK)).T

    def aligned(i):
        return i if isinstance(i, int) else pl.multiple_of(i, TOK)

    def k_tile(ref, first):
        return ref[pl.ds(aligned(first), KT), :]

    def v_tile(ref, first):
        return jnp.concatenate([ref[pl.ds(aligned(first + j * TOK), TOK), :] for j in range(KT // TOK)], 1)

    def scores(ref, first, item, masked):
        s = dot(k_tile(ref, first), q_s[item, 0:HEAD, :]) * SCALE
        if masked:
            mine = places_of(q_s[item, HEAD:, 0:TOK])
            mask = place_s[pl.ds(aligned(first), KT), :] <= mine
            s = jnp.where(jnp.concatenate([mask] * GROUP, 1), s, LOW)
        return s

    sources = [(ref, CHUNK, CHUNK, False) for ref in kv_refs]
    if n_fresh:
        sources.append((f_s, n_fresh * TOK, n_fresh * TOK, True))

    def old_of(item):
        if plan["start"]:
            return None
        at = item + plan["skip"]
        return ml_in[at][0:1, :], ml_in[at][1:2, :], acc_in[at]

    skip = plan["skip"]

    def put(item, m, total, acc):
        acc_out[item] = acc
        ml_out[item] = jnp.concatenate([m, total, jnp.zeros((6, ROWS), jnp.float32)], 0)

    def quick(item):
        tiles = [(ref, first, values, masked) for ref, values, n, masked in sources for first in range(0, n, KT)]
        old = old_of(item)
        total, acc = (None, None) if old is None else old[1:]
        part = jnp.zeros((8, ROWS), jnp.float32)

        def scores_of(tile):
            return scores(tile[0], tile[1], item, tile[3])

        ahead = scores_of(tiles[0])
        for j, (ref, first, values, _) in enumerate(tiles):
            s = ahead
            if j + 1 < len(tiles):
                ahead = scores_of(tiles[j + 1])
            p = jnp.exp2(s)
            part = part + jnp.sum(p.reshape(KT // 8, 8, ROWS), 0)
            pv = dot(v_tile(ref, values + first), p.astype(jnp.bfloat16))
            acc = pv if acc is None else acc + pv
        part = jnp.sum(part, 0, keepdims=True)
        put(item, jnp.zeros((1, ROWS), jnp.float32), part if total is None else total + part, acc)

    def careful(item):
        def group(g, carry):
            lanes = pl.ds(aligned(g * TOK), TOK)
            if plan["start"]:
                m = jnp.full((1, TOK), LOW, jnp.float32)
                total = jnp.zeros((1, TOK), jnp.float32)
                acc = jnp.zeros((HEAD, TOK), jnp.float32)
            else:
                at = item + skip
                m, total, acc = ml_in[at, 0:1, lanes], ml_in[at, 1:2, lanes], acc_in[at, :, lanes]
            q = q_s[item, 0:HEAD, lanes]
            for ref, values, n, masked in sources:

                def step(t, state, ref=ref, values=values, masked=masked):
                    m, total, acc = state
                    first = t * KT
                    s = dot(k_tile(ref, first), q) * SCALE
                    if masked:
                        mine = places_of(q_s[item, HEAD:, 0:TOK])
                        s = jnp.where(place_s[pl.ds(aligned(first), KT), :] <= mine, s, LOW)
                    top = jnp.maximum(m, jnp.max(s, 0, keepdims=True))
                    back = jnp.exp2(m - top)
                    p = jnp.where(s > 0.5 * LOW, jnp.exp2(s - top), 0.0)
                    total = total * back + jnp.sum(p, 0, keepdims=True)
                    acc = acc * back + dot(v_tile(ref, values + first), p.astype(jnp.bfloat16))
                    return top, total, acc

                m, total, acc = lax.fori_loop(0, n // KT, step, (m, total, acc))
            acc_out[item, :, lanes] = acc
            ml_out[item, 0:1, lanes] = m
            ml_out[item, 1:2, lanes] = total
            return carry

        lax.fori_loop(0, GROUP, group, 0)

    def everything(step):
        def body(item, carry):
            step(item)
            return carry

        if n_q == 1:
            step(0)
        else:
            lax.fori_loop(0, n_q, body, 0)

    everything(quick)
    fine = None
    for i in range(n_q):
        total = ml_out[i][1:2, :]
        good = jnp.where((total < TOO_BIG) & (total > TOO_SMALL), 1.0, 0.0)
        if not plan["start"]:
            good = jnp.where(ml_in[i + skip][0:1, :] == 0.0, good, 0.0)
        fine = good if fine is None else jnp.minimum(fine, good)

    @pl.when(jnp.min(fine) < 0.5)
    def _():
        everything(careful)

    if plan["finish"]:
        for i in range(n_q):
            m, total = ml_out[i][0:1, :], ml_out[i][1:2, :]
            out_refs[i][0:HEAD, :] = (acc_out[i] * (1.0 / total)).astype(jnp.bfloat16)
            out_refs[i][HEAD:, :] = coded_mass(m + jnp.log2(total))


def coded_mass(mass):
    a = mass.astype(jnp.bfloat16).astype(jnp.float32)
    b = (mass - a).astype(jnp.bfloat16).astype(jnp.float32)
    c = mass - a - b
    rows = lax.broadcasted_iota(jnp.int32, (META, ROWS), 0)
    return jnp.where(rows == 0, a, jnp.where(rows == 1, b, jnp.where(rows == 2, c, 0.0))).astype(jnp.bfloat16)


def attend(name, queries, kvs, state=None, fresh=(), finish=False, skip=0):
    n_q = len(queries)
    plan = dict(
        n_q=n_q,
        n_kv=len(kvs),
        n_fresh=len(fresh),
        start=state is None,
        finish=finish,
        skip=skip,
    )
    acc = jax.ShapeDtypeStruct((n_q, HEAD, ROWS), jnp.float32)
    ml = jax.ShapeDtypeStruct((n_q, 8, ROWS), jnp.float32)
    scratch = [pltpu.VMEM((n_q, HEAD + META, ROWS), jnp.bfloat16)]
    if fresh:
        scratch += [
            pltpu.VMEM((2 * len(fresh) * TOK, HEAD), jnp.bfloat16),
            pltpu.VMEM((len(fresh) * TOK, TOK), jnp.float32),
        ]
    if finish:
        outs = [jax.ShapeDtypeStruct((HEAD + META, ROWS), jnp.bfloat16)] * n_q
        scratch += [pltpu.VMEM(acc.shape, jnp.float32), pltpu.VMEM(ml.shape, jnp.float32)]
    else:
        outs = [acc, ml]
    args = list(queries) + list(kvs) + list(fresh) + list(state or ())
    pairs = n_q * (len(kvs) * CHUNK + len(fresh) * TOK) * ROWS
    return pl.pallas_call(
        functools.partial(attend_kernel, plan),
        out_shape=outs,
        in_specs=[VMEM] * len(args),
        out_specs=[VMEM] * len(outs),
        scratch_shapes=scratch,
        compiler_params=pltpu.CompilerParams(vmem_limit_bytes=24 * 2**20),
        cost_estimate=pl.CostEstimate(flops=pairs * 1024, bytes_accessed=0, transcendentals=0),
        name=name,
    )(*args)


def combine_kernel(acc_ref, ml_ref, *refs):
    parts, (att_ref, mass_ref) = refs[:-2], refs[-2:]
    total = ml_ref[0][1:2, :]
    masses = [ml_ref[0][0:1, :] + jnp.log2(total)]
    for r in parts:
        rows = r[HEAD:, :].astype(jnp.float32)
        masses.append(rows[0:1, :] + rows[1:2, :] + rows[2:3, :])
    top = functools.reduce(jnp.maximum, masses)
    weights = [jnp.exp2(m - top) for m in masses]
    den = functools.reduce(jnp.add, weights)
    mass = (top + jnp.log2(den)) * LN2
    shares = [w / den for w in weights]
    shares[0] = shares[0] / total
    for g in range(GROUP):
        lanes = slice(g * TOK, (g + 1) * TOK)
        x = acc_ref[0, :, lanes] * shares[0][:, lanes]
        for r, w in zip(parts, shares[1:]):
            x = x + r[0:HEAD, lanes].astype(jnp.float32) * w[:, lanes]
        att_ref[:, lanes] = x.T.astype(jnp.bfloat16)
    mass_ref[...] = jnp.concatenate([mass[:, g * TOK : (g + 1) * TOK] for g in range(GROUP)], 0)


def prepare(name, kernel, shape, args, specs, work, dtype=jnp.bfloat16):
    return pl.pallas_call(
        kernel,
        out_shape=jax.ShapeDtypeStruct(shape, dtype),
        in_specs=specs,
        out_specs=VMEM,
        compiler_params=pltpu.CompilerParams(vmem_limit_bytes=8 * 2**20),
        cost_estimate=pl.CostEstimate(flops=work, bytes_accessed=0, transcendentals=0),
        name=name,
    )(*args)


def per_device(queries, k, v, fk, fv, positions, order, span):
    order = order.reshape(1, TOK)
    positions = positions.reshape(2 * CHUNK // TOK, TOK)
    angle = prepare("angles", angle_kernel, (HEAD + META, TOK), (order,), [VMEM], 10**9, jnp.float32)
    q0 = prepare("turn_queries", query_kernel, (HEAD + META, ROWS), (queries, angle), [VMEM] * 2, 10**9)
    q_near = [shift(q0, "queries", -1), shift(q0, "queries", 1)]
    q_far = shift(q0, "queries", 2)

    first = prepare(
        "turn_keys_first",
        functools.partial(key_kernel, 0),
        (2 * CHUNK, HEAD),
        (k, v, positions),
        [VMEM] * 3,
        2 * 10**9,
    )
    first_near = [shift(first, "keys", -1), shift(first, "keys", 1)]
    second = prepare(
        "turn_keys_second",
        functools.partial(key_kernel, CHUNK),
        (PLACES + META, HEAD),
        (k, v, positions, fk, fv, order, span),
        [VMEM] * 6 + [pl.BlockSpec(memory_space=pltpu.SMEM)],
        2 * 10**9,
    )
    second_near = [shift(second, "keys", -1), shift(second, "keys", 1)]

    first_far = shift(first_near[1], "keys", 1)
    second_far = shift(second_near[0], "keys", -1)
    fresh = [second, *second_near, second_far]

    others = [q_far, *q_near]
    mine = attend("mine_own", [q0], [first, second])
    state = attend("others_own", others, [first, second])
    state = attend("others_near", others, [*first_near, *second_near], state)
    (r_far,) = attend("far_last", [q_far], [first_far, second_far], state, fresh, finish=True)
    r_ahead, r_behind = attend("near_last", q_near, [first_far, second_far], state, fresh, finish=True, skip=1)
    back = [shift(r_far, "queries", 2), shift(r_ahead, "queries", 1), shift(r_behind, "queries", -1)]
    mine = attend("mine_rest", [q0], [*first_near, *second_near, first_far, second_far], mine, fresh)
    attended, mass = pl.pallas_call(
        combine_kernel,
        out_shape=[
            jax.ShapeDtypeStruct((TOK, GROUP * HEAD), jnp.bfloat16),
            jax.ShapeDtypeStruct((GROUP, TOK), jnp.float32),
        ],
        in_specs=[VMEM] * 5,
        out_specs=[VMEM] * 2,
        compiler_params=pltpu.CompilerParams(vmem_limit_bytes=8 * 2**20),
        name="combine",
    )(*mine, *back)
    return attended, mass.T


def solution(mesh):
    spec = (P("ctx", "tp"),) * 5 + (P("ctx"),) * 3
    return jax.shard_map(
        per_device,
        mesh=mesh,
        in_specs=spec,
        out_specs=(P("ctx", "tp"), P("ctx", "tp")),
        check_vma=False,
    )
```

```python
import functools

import jax
import jax.numpy as jnp
import ml_dtypes
import numpy as np
from jax import lax
from jax.experimental import pallas as pl
from jax.experimental.pallas import tpu as pltpu
from jax.sharding import PartitionSpec as P

GROUP = 8
HEAD = 128
TOK = 128
ROWS = GROUP * TOK
CACHED = 32768
SIDE = 4
CHUNK = 1024
TP = 8
KT = 256
SCALE = HEAD**-0.5 * 1.4426950408889634
LN2 = 0.6931471805599453
LOW = -1e30
TOO_BIG = 2.0**100
TOO_SMALL = 2.0**-60
META = 16

VMEM = pl.BlockSpec(memory_space=pltpu.VMEM)


def shift(block, kind, step):
    pairs = []
    for i in range(SIDE * SIDE):
        z, y = divmod(i, SIDE)
        for t in range(TP):
            if (t % 2 == 0) == (kind == "keys"):
                j = z * SIDE + (y + step) % SIDE
            else:
                j = ((z + step) % SIDE) * SIDE + y
            pairs.append((i * TP + t, j * TP + t))
    return lax.ppermute(block, ("ctx", "tp"), pairs)


def _bf(x):
    return np.asarray(x, np.float32).astype(ml_dtypes.bfloat16).astype(np.float64)


def _fit():
    t = np.cos(np.linspace(0, np.pi, 4001)) * 0.5
    u = t * t
    cos = np.polynomial.polynomial.polyfit(u, np.cos(2 * np.pi * t), 8)
    good = np.abs(t) > 1e-3
    sin = np.polynomial.polynomial.polyfit(u[good], np.sin(2 * np.pi * t[good]) / t[good], 7)
    return [float(c) for c in cos], [float(c) for c in sin]


COS, SIN = _fit()


def _turns():
    turns = 500000.0 ** (-2.0 * np.arange(64) / HEAD) / (2 * np.pi)
    first = _bf(turns)
    second = _bf(turns - first)
    return [[float(x) for x in piece] for piece in (first, second, turns - first - second)]


TURNS = _turns()


def spread(constants):
    row = lax.broadcasted_iota(jnp.int32, (8, TOK), 0)
    tiles = []
    for first in range(0, 64, 8):
        tile = jnp.full((8, TOK), constants[first + 7], jnp.float32)
        for i in range(7):
            tile = jnp.where(row == i, constants[first + i], tile)
        tiles.append(tile)
    return jnp.concatenate(tiles, 0)


def angles(positions, turns):
    a = positions * turns[0]
    a = a - jnp.round(a)
    b = positions * turns[1]
    t = a + (b - jnp.round(b)) + positions * turns[2]
    t = t - jnp.round(t)
    u = t * t
    cos = jnp.full_like(u, COS[-1])
    for c in COS[-2::-1]:
        cos = cos * u + c
    sin = jnp.full_like(u, SIN[-1])
    for c in SIN[-2::-1]:
        sin = sin * u + c
    return cos, sin * t


def turned(x, cos, sin):
    lower, upper = x[:64], x[64:]
    return jnp.concatenate([lower * cos - upper * sin, upper * cos + lower * sin], 0)


def coded(places):
    high = jnp.right_shift(places, 4)
    rows = lax.broadcasted_iota(jnp.int32, (META, TOK), 0)
    both = jnp.where(rows == 0, high, jnp.where(rows == 1, places - high * 16, 0))
    return both.astype(jnp.float32).astype(jnp.bfloat16)


def places_of(meta):
    meta = meta.astype(jnp.float32)
    return meta[0:1, :] * 16.0 + meta[1:2, :]


def angle_kernel(order_ref, out_ref):
    order = order_ref[...]
    turns = [spread(piece) for piece in TURNS]
    cos, sin = angles((order + CACHED).astype(jnp.float32), turns)
    out_ref[0:64, :] = cos
    out_ref[64:128, :] = sin
    out_ref[128:, :] = coded(order).astype(jnp.float32)


def query_kernel(q_ref, angle_ref, out_ref):
    cos, sin = angle_ref[0:64, :], angle_ref[64:128, :]
    for g in range(GROUP):
        lanes = slice(g * HEAD, (g + 1) * HEAD)
        x = q_ref[:, lanes].astype(jnp.float32).T
        out_ref[0:HEAD, lanes] = turned(x, cos, sin).astype(jnp.bfloat16)
    out_ref[HEAD:, :] = jnp.concatenate([angle_ref[128:, :].astype(jnp.bfloat16)] * GROUP, 1)


FRESH_KEYS = 2 * CHUNK
FRESH_VALUES = FRESH_KEYS + TOK
PLACES = FRESH_VALUES + TOK


def key_kernel(start, k_ref, v_ref, pos_ref, *refs):
    with_fresh = len(refs) > 1
    if with_fresh:
        fk_ref, fv_ref, order_ref, span_ref, out_ref = refs
    else:
        (out_ref,) = refs
    turns = [spread(piece) for piece in TURNS]

    def keys(x, positions):
        cos, sin = angles(positions.astype(jnp.float32), turns)
        return turned(x.astype(jnp.float32).T, cos, sin).T.astype(jnp.bfloat16)

    def values(x):
        return x.astype(jnp.float32).T.astype(jnp.bfloat16)

    for b in range(CHUNK // TOK):
        rows = slice(start + b * TOK, start + (b + 1) * TOK)
        tile = start // TOK + b
        out_ref[b * TOK : (b + 1) * TOK, :] = keys(k_ref[rows, :], pos_ref[tile : tile + 1, :])
        out_ref[CHUNK + b * TOK : CHUNK + (b + 1) * TOK, :] = values(v_ref[rows, :])
    if with_fresh:
        order = order_ref[...]
        out_ref[FRESH_KEYS:FRESH_VALUES, :] = keys(fk_ref[...], order + CACHED)
        out_ref[FRESH_VALUES:PLACES, :] = values(fv_ref[...])
        lane = lax.broadcasted_iota(jnp.int32, (1, TOK), 1)
        out_ref[PLACES:, :] = coded(jnp.where(lane < span_ref[0], order, 4000))


def dot(a, b):
    return lax.dot_general(a, b, (((1,), (0,)), ((), ())), preferred_element_type=jnp.float32)


def attend_kernel(plan, *refs):
    it = iter(refs)
    n_q, n_fresh = plan["n_q"], plan["n_fresh"]
    q_refs = [next(it) for _ in range(n_q)]
    kv_refs = [next(it) for _ in range(plan["n_kv"])]
    fresh_refs = [next(it) for _ in range(n_fresh)]
    if not plan["start"]:
        acc_in, ml_in = next(it), next(it)
    if plan["finish"]:
        out_refs = [next(it) for _ in range(n_q)]
    else:
        acc_out, ml_out = next(it), next(it)
    q_s = next(it)
    if n_fresh:
        f_s, place_s = next(it), next(it)
    if plan["finish"]:
        acc_out, ml_out = next(it), next(it)

    for i, r in enumerate(q_refs):
        q_s[i] = r[...]
    for i, r in enumerate(fresh_refs):
        f_s[i * TOK : (i + 1) * TOK, :] = r[FRESH_KEYS:FRESH_VALUES, :]
        f_s[(n_fresh + i) * TOK : (n_fresh + i + 1) * TOK, :] = r[FRESH_VALUES:PLACES, :]
        place_s[i * TOK : (i + 1) * TOK, :] = jnp.broadcast_to(places_of(r[PLACES:, :]), (TOK, TOK)).T

    def aligned(i):
        return i if isinstance(i, int) else pl.multiple_of(i, TOK)

    def k_tile(ref, first):
        return ref[pl.ds(aligned(first), KT), :]

    def v_tile(ref, first):
        return jnp.concatenate([ref[pl.ds(aligned(first + j * TOK), TOK), :] for j in range(KT // TOK)], 1)

    def scores(ref, first, item, masked):
        s = dot(k_tile(ref, first), q_s[item, 0:HEAD, :]) * SCALE
        if masked:
            mine = places_of(q_s[item, HEAD:, 0:TOK])
            mask = place_s[pl.ds(aligned(first), KT), :] <= mine
            s = jnp.where(jnp.concatenate([mask] * GROUP, 1), s, LOW)
        return s

    sources = [(ref, CHUNK, CHUNK, False) for ref in kv_refs]
    if n_fresh:
        sources.append((f_s, n_fresh * TOK, n_fresh * TOK, True))

    def old_of(item):
        if plan["start"]:
            return None
        at = item + plan["skip"]
        return ml_in[at][0:1, :], ml_in[at][1:2, :], acc_in[at]

    skip = plan["skip"]

    def put(item, m, total, acc):
        acc_out[item] = acc
        ml_out[item] = jnp.concatenate([m, total, jnp.zeros((6, ROWS), jnp.float32)], 0)

    def quick(item):
        tiles = [(ref, first, values, masked) for ref, values, n, masked in sources for first in range(0, n, KT)]
        old = old_of(item)
        total, acc = (None, None) if old is None else old[1:]
        part = jnp.zeros((8, ROWS), jnp.float32)

        def scores_of(tile):
            return scores(tile[0], tile[1], item, tile[3])

        ahead = scores_of(tiles[0])
        for j, (ref, first, values, _) in enumerate(tiles):
            s = ahead
            if j + 1 < len(tiles):
                ahead = scores_of(tiles[j + 1])
            p = jnp.exp2(s)
            part = part + jnp.sum(p.reshape(KT // 8, 8, ROWS), 0)
            pv = dot(v_tile(ref, values + first), p.astype(jnp.bfloat16))
            acc = pv if acc is None else acc + pv
        part = jnp.sum(part, 0, keepdims=True)
        put(item, jnp.zeros((1, ROWS), jnp.float32), part if total is None else total + part, acc)

    def careful(item):
        def group(g, carry):
            lanes = pl.ds(aligned(g * TOK), TOK)
            if plan["start"]:
                m = jnp.full((1, TOK), LOW, jnp.float32)
                total = jnp.zeros((1, TOK), jnp.float32)
                acc = jnp.zeros((HEAD, TOK), jnp.float32)
            else:
                at = item + skip
                m, total, acc = ml_in[at, 0:1, lanes], ml_in[at, 1:2, lanes], acc_in[at, :, lanes]
            q = q_s[item, 0:HEAD, lanes]
            for ref, values, n, masked in sources:

                def step(t, state, ref=ref, values=values, masked=masked):
                    m, total, acc = state
                    first = t * KT
                    s = dot(k_tile(ref, first), q) * SCALE
                    if masked:
                        mine = places_of(q_s[item, HEAD:, 0:TOK])
                        s = jnp.where(place_s[pl.ds(aligned(first), KT), :] <= mine, s, LOW)
                    top = jnp.maximum(m, jnp.max(s, 0, keepdims=True))
                    back = jnp.exp2(m - top)
                    p = jnp.where(s > 0.5 * LOW, jnp.exp2(s - top), 0.0)
                    total = total * back + jnp.sum(p, 0, keepdims=True)
                    acc = acc * back + dot(v_tile(ref, values + first), p.astype(jnp.bfloat16))
                    return top, total, acc

                m, total, acc = lax.fori_loop(0, n // KT, step, (m, total, acc))
            acc_out[item, :, lanes] = acc
            ml_out[item, 0:1, lanes] = m
            ml_out[item, 1:2, lanes] = total
            return carry

        lax.fori_loop(0, GROUP, group, 0)

    def everything(step):
        def body(item, carry):
            step(item)
            return carry

        if n_q == 1:
            step(0)
        else:
            lax.fori_loop(0, n_q, body, 0)

    everything(quick)
    fine = None
    for i in range(n_q):
        total = ml_out[i][1:2, :]
        good = jnp.where((total < TOO_BIG) & (total > TOO_SMALL), 1.0, 0.0)
        if not plan["start"]:
            good = jnp.where(ml_in[i + skip][0:1, :] == 0.0, good, 0.0)
        fine = good if fine is None else jnp.minimum(fine, good)

    @pl.when(jnp.min(fine) < 0.5)
    def _():
        everything(careful)

    if plan["finish"]:
        for i in range(n_q):
            m, total = ml_out[i][0:1, :], ml_out[i][1:2, :]
            out_refs[i][0:HEAD, :] = (acc_out[i] * (1.0 / total)).astype(jnp.bfloat16)
            out_refs[i][HEAD:, :] = coded_mass(m + jnp.log2(total))


def coded_mass(mass):
    a = mass.astype(jnp.bfloat16).astype(jnp.float32)
    b = (mass - a).astype(jnp.bfloat16).astype(jnp.float32)
    c = mass - a - b
    rows = lax.broadcasted_iota(jnp.int32, (META, ROWS), 0)
    return jnp.where(rows == 0, a, jnp.where(rows == 1, b, jnp.where(rows == 2, c, 0.0))).astype(jnp.bfloat16)


def attend(name, queries, kvs, state=None, fresh=(), finish=False, skip=0):
    n_q = len(queries)
    plan = dict(
        n_q=n_q,
        n_kv=len(kvs),
        n_fresh=len(fresh),
        start=state is None,
        finish=finish,
        skip=skip,
    )
    acc = jax.ShapeDtypeStruct((n_q, HEAD, ROWS), jnp.float32)
    ml = jax.ShapeDtypeStruct((n_q, 8, ROWS), jnp.float32)
    scratch = [pltpu.VMEM((n_q, HEAD + META, ROWS), jnp.bfloat16)]
    if fresh:
        scratch += [
            pltpu.VMEM((2 * len(fresh) * TOK, HEAD), jnp.bfloat16),
            pltpu.VMEM((len(fresh) * TOK, TOK), jnp.float32),
        ]
    if finish:
        outs = [jax.ShapeDtypeStruct((HEAD + META, ROWS), jnp.bfloat16)] * n_q
        scratch += [pltpu.VMEM(acc.shape, jnp.float32), pltpu.VMEM(ml.shape, jnp.float32)]
    else:
        outs = [acc, ml]
    args = list(queries) + list(kvs) + list(fresh) + list(state or ())
    pairs = n_q * (len(kvs) * CHUNK + len(fresh) * TOK) * ROWS
    return pl.pallas_call(
        functools.partial(attend_kernel, plan),
        out_shape=outs,
        in_specs=[VMEM] * len(args),
        out_specs=[VMEM] * len(outs),
        scratch_shapes=scratch,
        compiler_params=pltpu.CompilerParams(vmem_limit_bytes=24 * 2**20),
        cost_estimate=pl.CostEstimate(flops=pairs * 1024, bytes_accessed=0, transcendentals=0),
        name=name,
    )(*args)


def combine_kernel(acc_ref, ml_ref, *refs):
    parts, (att_ref, mass_ref) = refs[:-2], refs[-2:]
    total = ml_ref[0][1:2, :]
    masses = [ml_ref[0][0:1, :] + jnp.log2(total)]
    for r in parts:
        rows = r[HEAD:, :].astype(jnp.float32)
        masses.append(rows[0:1, :] + rows[1:2, :] + rows[2:3, :])
    top = functools.reduce(jnp.maximum, masses)
    weights = [jnp.exp2(m - top) for m in masses]
    den = functools.reduce(jnp.add, weights)
    mass = (top + jnp.log2(den)) * LN2
    shares = [w / den for w in weights]
    shares[0] = shares[0] / total
    for g in range(GROUP):
        lanes = slice(g * TOK, (g + 1) * TOK)
        x = acc_ref[0, :, lanes] * shares[0][:, lanes]
        for r, w in zip(parts, shares[1:]):
            x = x + r[0:HEAD, lanes].astype(jnp.float32) * w[:, lanes]
        att_ref[:, lanes] = x.T.astype(jnp.bfloat16)
    mass_ref[...] = jnp.concatenate([mass[:, g * TOK : (g + 1) * TOK] for g in range(GROUP)], 0)


def prepare(name, kernel, shape, args, specs, work, dtype=jnp.bfloat16):
    return pl.pallas_call(
        kernel,
        out_shape=jax.ShapeDtypeStruct(shape, dtype),
        in_specs=specs,
        out_specs=VMEM,
        compiler_params=pltpu.CompilerParams(vmem_limit_bytes=8 * 2**20),
        cost_estimate=pl.CostEstimate(flops=work, bytes_accessed=0, transcendentals=0),
        name=name,
    )(*args)


def per_device(queries, k, v, fk, fv, positions, order, span):
    order = order.reshape(1, TOK)
    positions = positions.reshape(2 * CHUNK // TOK, TOK)
    angle = prepare("angles", angle_kernel, (HEAD + META, TOK), (order,), [VMEM], 10**9, jnp.float32)
    q0 = prepare("turn_queries", query_kernel, (HEAD + META, ROWS), (queries, angle), [VMEM] * 2, 10**9)
    q_near = [shift(q0, "queries", -1), shift(q0, "queries", 1)]
    q_far = shift(q0, "queries", 2)

    first = prepare(
        "turn_keys_first",
        functools.partial(key_kernel, 0),
        (2 * CHUNK, HEAD),
        (k, v, positions),
        [VMEM] * 3,
        2 * 10**9,
    )
    first_near = [shift(first, "keys", -1), shift(first, "keys", 1)]
    second = prepare(
        "turn_keys_second",
        functools.partial(key_kernel, CHUNK),
        (PLACES + META, HEAD),
        (k, v, positions, fk, fv, order, span),
        [VMEM] * 6 + [pl.BlockSpec(memory_space=pltpu.SMEM)],
        2 * 10**9,
    )
    mine = attend("mine_own", [q0], [first, second])
    q_far, second_late = lax.optimization_barrier((q_far, second))
    second_near = [shift(second_late, "keys", -1), shift(second_late, "keys", 1)]

    behind, ahead = lax.optimization_barrier((first_near[1], second_near[0]))
    first_far = shift(behind, "keys", 1)
    second_far = shift(ahead, "keys", -1)
    fresh = [second, *second_near, second_far]

    others = [q_far, *q_near]
    state = attend("others_own", others, [first, second])
    state = attend("others_near", others, [*first_near, *second_near], state)
    (r_far,) = attend("far_last", [q_far], [first_far, second_far], state, fresh, finish=True)
    r_ahead, r_behind = attend("near_last", q_near, [first_far, second_far], state, fresh, finish=True, skip=1)
    back = [shift(r_far, "queries", 2), shift(r_ahead, "queries", 1), shift(r_behind, "queries", -1)]
    mine = attend("mine_rest", [q0], [*first_near, *second_near, first_far, second_far], mine, fresh)
    attended, mass = pl.pallas_call(
        combine_kernel,
        out_shape=[
            jax.ShapeDtypeStruct((TOK, GROUP * HEAD), jnp.bfloat16),
            jax.ShapeDtypeStruct((GROUP, TOK), jnp.float32),
        ],
        in_specs=[VMEM] * 5,
        out_specs=[VMEM] * 2,
        compiler_params=pltpu.CompilerParams(vmem_limit_bytes=8 * 2**20),
        name="combine",
    )(*mine, *back)
    return attended, mass.T


def solution(mesh):
    spec = (P("ctx", "tp"),) * 5 + (P("ctx"),) * 3
    return jax.shard_map(
        per_device,
        mesh=mesh,
        in_specs=spec,
        out_specs=(P("ctx", "tp"), P("ctx", "tp")),
        check_vma=False,
    )
```

```python
import functools

import jax
import jax.numpy as jnp
import ml_dtypes
import numpy as np
from jax import lax
from jax.experimental import pallas as pl
from jax.experimental.pallas import tpu as pltpu
from jax.sharding import PartitionSpec as P

GROUP = 8
HEAD = 128
TOK = 128
ROWS = GROUP * TOK
CACHED = 32768
SIDE = 4
CHUNK = 1024
TP = 8
KT = 256
SCALE = HEAD**-0.5 * 1.4426950408889634
LN2 = 0.6931471805599453
LOW = -1e30
TOO_BIG = 2.0**100
TOO_SMALL = 2.0**-60
META = 16

VMEM = pl.BlockSpec(memory_space=pltpu.VMEM)


def shift(block, kind, step):
    pairs = []
    for i in range(SIDE * SIDE):
        z, y = divmod(i, SIDE)
        for t in range(TP):
            if (t % 2 == 0) == (kind == "keys"):
                j = z * SIDE + (y + step) % SIDE
            else:
                j = ((z + step) % SIDE) * SIDE + y
            pairs.append((i * TP + t, j * TP + t))
    return lax.ppermute(block, ("ctx", "tp"), pairs)


def _bf(x):
    return np.asarray(x, np.float32).astype(ml_dtypes.bfloat16).astype(np.float64)


def _fit():
    t = np.cos(np.linspace(0, np.pi, 4001)) * 0.5
    u = t * t
    cos = np.polynomial.polynomial.polyfit(u, np.cos(2 * np.pi * t), 8)
    good = np.abs(t) > 1e-3
    sin = np.polynomial.polynomial.polyfit(u[good], np.sin(2 * np.pi * t[good]) / t[good], 7)
    return [float(c) for c in cos], [float(c) for c in sin]


COS, SIN = _fit()


def _turns():
    turns = 500000.0 ** (-2.0 * np.arange(64) / HEAD) / (2 * np.pi)
    first = _bf(turns)
    second = _bf(turns - first)
    return [[float(x) for x in piece] for piece in (first, second, turns - first - second)]


TURNS = _turns()


def spread(constants):
    row = lax.broadcasted_iota(jnp.int32, (8, TOK), 0)
    tiles = []
    for first in range(0, 64, 8):
        tile = jnp.full((8, TOK), constants[first + 7], jnp.float32)
        for i in range(7):
            tile = jnp.where(row == i, constants[first + i], tile)
        tiles.append(tile)
    return jnp.concatenate(tiles, 0)


def angles(positions, turns):
    a = positions * turns[0]
    a = a - jnp.round(a)
    b = positions * turns[1]
    t = a + (b - jnp.round(b)) + positions * turns[2]
    t = t - jnp.round(t)
    u = t * t
    cos = jnp.full_like(u, COS[-1])
    for c in COS[-2::-1]:
        cos = cos * u + c
    sin = jnp.full_like(u, SIN[-1])
    for c in SIN[-2::-1]:
        sin = sin * u + c
    return cos, sin * t


def turned(x, cos, sin):
    lower, upper = x[:64], x[64:]
    return jnp.concatenate([lower * cos - upper * sin, upper * cos + lower * sin], 0)


def coded(places):
    high = jnp.right_shift(places, 4)
    rows = lax.broadcasted_iota(jnp.int32, (META, TOK), 0)
    both = jnp.where(rows == 0, high, jnp.where(rows == 1, places - high * 16, 0))
    return both.astype(jnp.float32).astype(jnp.bfloat16)


def places_of(meta):
    meta = meta.astype(jnp.float32)
    return meta[0:1, :] * 16.0 + meta[1:2, :]


def angle_kernel(order_ref, out_ref):
    order = order_ref[...]
    turns = [spread(piece) for piece in TURNS]
    cos, sin = angles((order + CACHED).astype(jnp.float32), turns)
    out_ref[0:64, :] = cos
    out_ref[64:128, :] = sin
    out_ref[128:, :] = coded(order).astype(jnp.float32)


def query_kernel(q_ref, angle_ref, out_ref):
    cos, sin = angle_ref[0:64, :], angle_ref[64:128, :]
    for g in range(GROUP):
        lanes = slice(g * HEAD, (g + 1) * HEAD)
        x = q_ref[:, lanes].astype(jnp.float32).T
        out_ref[0:HEAD, lanes] = turned(x, cos, sin).astype(jnp.bfloat16)
    out_ref[HEAD:, :] = jnp.concatenate([angle_ref[128:, :].astype(jnp.bfloat16)] * GROUP, 1)


FRESH_KEYS = 2 * CHUNK
FRESH_VALUES = FRESH_KEYS + TOK
PLACES = FRESH_VALUES + TOK


def key_kernel(start, k_ref, v_ref, pos_ref, *refs):
    with_fresh = len(refs) > 1
    if with_fresh:
        fk_ref, fv_ref, order_ref, span_ref, out_ref = refs
    else:
        (out_ref,) = refs
    turns = [spread(piece) for piece in TURNS]

    def keys(x, positions):
        cos, sin = angles(positions.astype(jnp.float32), turns)
        return turned(x.astype(jnp.float32).T, cos, sin).T.astype(jnp.bfloat16)

    def values(x):
        return x.astype(jnp.float32).T.astype(jnp.bfloat16)

    for b in range(CHUNK // TOK):
        rows = slice(start + b * TOK, start + (b + 1) * TOK)
        tile = start // TOK + b
        out_ref[b * TOK : (b + 1) * TOK, :] = keys(k_ref[rows, :], pos_ref[tile : tile + 1, :])
        out_ref[CHUNK + b * TOK : CHUNK + (b + 1) * TOK, :] = values(v_ref[rows, :])
    if with_fresh:
        order = order_ref[...]
        out_ref[FRESH_KEYS:FRESH_VALUES, :] = keys(fk_ref[...], order + CACHED)
        out_ref[FRESH_VALUES:PLACES, :] = values(fv_ref[...])
        lane = lax.broadcasted_iota(jnp.int32, (1, TOK), 1)
        out_ref[PLACES:, :] = coded(jnp.where(lane < span_ref[0], order, 4000))


def dot(a, b):
    return lax.dot_general(a, b, (((1,), (0,)), ((), ())), preferred_element_type=jnp.float32)


def attend_kernel(plan, *refs):
    it = iter(refs)
    n_q, n_fresh = plan["n_q"], plan["n_fresh"]
    q_refs = [next(it) for _ in range(n_q)]
    kv_refs = [next(it) for _ in range(plan["n_kv"])]
    fresh_refs = [next(it) for _ in range(n_fresh)]
    if not plan["start"]:
        acc_in, ml_in = next(it), next(it)
    if plan["finish"]:
        out_refs = [next(it) for _ in range(n_q)]
    else:
        acc_out, ml_out = next(it), next(it)
    q_s = next(it)
    if n_fresh:
        f_s, place_s = next(it), next(it)
    if plan["finish"]:
        acc_out, ml_out = next(it), next(it)

    for i, r in enumerate(q_refs):
        q_s[i] = r[...]
    for i, r in enumerate(fresh_refs):
        f_s[i * TOK : (i + 1) * TOK, :] = r[FRESH_KEYS:FRESH_VALUES, :]
        f_s[(n_fresh + i) * TOK : (n_fresh + i + 1) * TOK, :] = r[FRESH_VALUES:PLACES, :]
        place_s[i * TOK : (i + 1) * TOK, :] = jnp.broadcast_to(places_of(r[PLACES:, :]), (TOK, TOK)).T

    def aligned(i):
        return i if isinstance(i, int) else pl.multiple_of(i, TOK)

    def k_tile(ref, first):
        return ref[pl.ds(aligned(first), KT), :]

    def v_tile(ref, first):
        return jnp.concatenate([ref[pl.ds(aligned(first + j * TOK), TOK), :] for j in range(KT // TOK)], 1)

    def scores(ref, first, item, masked):
        s = dot(k_tile(ref, first), q_s[item, 0:HEAD, :]) * SCALE
        if masked:
            mine = places_of(q_s[item, HEAD:, 0:TOK])
            mask = place_s[pl.ds(aligned(first), KT), :] <= mine
            s = jnp.where(jnp.concatenate([mask] * GROUP, 1), s, LOW)
        return s

    sources = [(ref, CHUNK, CHUNK, False) for ref in kv_refs]
    if n_fresh:
        sources.append((f_s, n_fresh * TOK, n_fresh * TOK, True))

    def old_of(item):
        if plan["start"]:
            return None
        at = item + plan["skip"]
        return ml_in[at][0:1, :], ml_in[at][1:2, :], acc_in[at]

    skip = plan["skip"]

    def put(item, m, total, acc):
        acc_out[item] = acc
        ml_out[item] = jnp.concatenate([m, total, jnp.zeros((6, ROWS), jnp.float32)], 0)

    def quick(item):
        tiles = [(ref, first, values, masked) for ref, values, n, masked in sources for first in range(0, n, KT)]
        old = old_of(item)
        total, acc = (None, None) if old is None else old[1:]
        part = jnp.zeros((8, ROWS), jnp.float32)

        def scores_of(tile):
            return scores(tile[0], tile[1], item, tile[3])

        ahead = scores_of(tiles[0])
        for j, (ref, first, values, _) in enumerate(tiles):
            s = ahead
            if j + 1 < len(tiles):
                ahead = scores_of(tiles[j + 1])
            p = jnp.exp2(s)
            part = part + jnp.sum(p.reshape(KT // 8, 8, ROWS), 0)
            pv = dot(v_tile(ref, values + first), p.astype(jnp.bfloat16))
            acc = pv if acc is None else acc + pv
        part = jnp.sum(part, 0, keepdims=True)
        put(item, jnp.zeros((1, ROWS), jnp.float32), part if total is None else total + part, acc)

    def careful(item):
        def group(g, carry):
            lanes = pl.ds(aligned(g * TOK), TOK)
            if plan["start"]:
                m = jnp.full((1, TOK), LOW, jnp.float32)
                total = jnp.zeros((1, TOK), jnp.float32)
                acc = jnp.zeros((HEAD, TOK), jnp.float32)
            else:
                at = item + skip
                m, total, acc = ml_in[at, 0:1, lanes], ml_in[at, 1:2, lanes], acc_in[at, :, lanes]
            q = q_s[item, 0:HEAD, lanes]
            for ref, values, n, masked in sources:

                def step(t, state, ref=ref, values=values, masked=masked):
                    m, total, acc = state
                    first = t * KT
                    s = dot(k_tile(ref, first), q) * SCALE
                    if masked:
                        mine = places_of(q_s[item, HEAD:, 0:TOK])
                        s = jnp.where(place_s[pl.ds(aligned(first), KT), :] <= mine, s, LOW)
                    top = jnp.maximum(m, jnp.max(s, 0, keepdims=True))
                    back = jnp.exp2(m - top)
                    p = jnp.where(s > 0.5 * LOW, jnp.exp2(s - top), 0.0)
                    total = total * back + jnp.sum(p, 0, keepdims=True)
                    acc = acc * back + dot(v_tile(ref, values + first), p.astype(jnp.bfloat16))
                    return top, total, acc

                m, total, acc = lax.fori_loop(0, n // KT, step, (m, total, acc))
            acc_out[item, :, lanes] = acc
            ml_out[item, 0:1, lanes] = m
            ml_out[item, 1:2, lanes] = total
            return carry

        lax.fori_loop(0, GROUP, group, 0)

    def everything(step):
        def body(item, carry):
            step(item)
            return carry

        if n_q == 1:
            step(0)
        else:
            lax.fori_loop(0, n_q, body, 0)

    everything(quick)
    fine = None
    for i in range(n_q):
        total = ml_out[i][1:2, :]
        good = jnp.where((total < TOO_BIG) & (total > TOO_SMALL), 1.0, 0.0)
        if not plan["start"]:
            good = jnp.where(ml_in[i + skip][0:1, :] == 0.0, good, 0.0)
        fine = good if fine is None else jnp.minimum(fine, good)

    @pl.when(jnp.min(fine) < 0.5)
    def _():
        everything(careful)

    if plan["finish"]:
        for i in range(n_q):
            m, total = ml_out[i][0:1, :], ml_out[i][1:2, :]
            out_refs[i][0:HEAD, :] = (acc_out[i] * (1.0 / total)).astype(jnp.bfloat16)
            out_refs[i][HEAD:, :] = coded_mass(m + jnp.log2(total))


def coded_mass(mass):
    a = mass.astype(jnp.bfloat16).astype(jnp.float32)
    b = (mass - a).astype(jnp.bfloat16).astype(jnp.float32)
    c = mass - a - b
    rows = lax.broadcasted_iota(jnp.int32, (META, ROWS), 0)
    return jnp.where(rows == 0, a, jnp.where(rows == 1, b, jnp.where(rows == 2, c, 0.0))).astype(jnp.bfloat16)


def attend(name, queries, kvs, state=None, fresh=(), finish=False, skip=0):
    n_q = len(queries)
    plan = dict(
        n_q=n_q,
        n_kv=len(kvs),
        n_fresh=len(fresh),
        start=state is None,
        finish=finish,
        skip=skip,
    )
    acc = jax.ShapeDtypeStruct((n_q, HEAD, ROWS), jnp.float32)
    ml = jax.ShapeDtypeStruct((n_q, 8, ROWS), jnp.float32)
    scratch = [pltpu.VMEM((n_q, HEAD + META, ROWS), jnp.bfloat16)]
    if fresh:
        scratch += [
            pltpu.VMEM((2 * len(fresh) * TOK, HEAD), jnp.bfloat16),
            pltpu.VMEM((len(fresh) * TOK, TOK), jnp.float32),
        ]
    if finish:
        outs = [jax.ShapeDtypeStruct((HEAD + META, ROWS), jnp.bfloat16)] * n_q
        scratch += [pltpu.VMEM(acc.shape, jnp.float32), pltpu.VMEM(ml.shape, jnp.float32)]
    else:
        outs = [acc, ml]
    args = list(queries) + list(kvs) + list(fresh) + list(state or ())
    pairs = n_q * (len(kvs) * CHUNK + len(fresh) * TOK) * ROWS
    return pl.pallas_call(
        functools.partial(attend_kernel, plan),
        out_shape=outs,
        in_specs=[VMEM] * len(args),
        out_specs=[VMEM] * len(outs),
        scratch_shapes=scratch,
        compiler_params=pltpu.CompilerParams(vmem_limit_bytes=24 * 2**20),
        cost_estimate=pl.CostEstimate(flops=pairs * 1024, bytes_accessed=0, transcendentals=0),
        name=name,
    )(*args)


def combine_kernel(acc_ref, ml_ref, *refs):
    parts, (att_ref, mass_ref) = refs[:-2], refs[-2:]
    total = ml_ref[0][1:2, :]
    masses = [ml_ref[0][0:1, :] + jnp.log2(total)]
    for r in parts:
        rows = r[HEAD:, :].astype(jnp.float32)
        masses.append(rows[0:1, :] + rows[1:2, :] + rows[2:3, :])
    top = functools.reduce(jnp.maximum, masses)
    weights = [jnp.exp2(m - top) for m in masses]
    den = functools.reduce(jnp.add, weights)
    mass = (top + jnp.log2(den)) * LN2
    shares = [w / den for w in weights]
    shares[0] = shares[0] / total
    for g in range(GROUP):
        lanes = slice(g * TOK, (g + 1) * TOK)
        x = acc_ref[0, :, lanes] * shares[0][:, lanes]
        for r, w in zip(parts, shares[1:]):
            x = x + r[0:HEAD, lanes].astype(jnp.float32) * w[:, lanes]
        att_ref[:, lanes] = x.T.astype(jnp.bfloat16)
    mass_ref[...] = jnp.concatenate([mass[:, g * TOK : (g + 1) * TOK] for g in range(GROUP)], 0)


def prepare(name, kernel, shape, args, specs, work, dtype=jnp.bfloat16):
    return pl.pallas_call(
        kernel,
        out_shape=jax.ShapeDtypeStruct(shape, dtype),
        in_specs=specs,
        out_specs=VMEM,
        compiler_params=pltpu.CompilerParams(vmem_limit_bytes=8 * 2**20),
        cost_estimate=pl.CostEstimate(flops=work, bytes_accessed=0, transcendentals=0),
        name=name,
    )(*args)


def per_device(queries, k, v, fk, fv, positions, order, span):
    order = order.reshape(1, TOK)
    positions = positions.reshape(2 * CHUNK // TOK, TOK)
    angle = prepare("angles", angle_kernel, (HEAD + META, TOK), (order,), [VMEM], 10**9, jnp.float32)
    q0 = prepare("turn_queries", query_kernel, (HEAD + META, ROWS), (queries, angle), [VMEM] * 2, 10**9)
    q_near = [shift(q0, "queries", -1), shift(q0, "queries", 1)]
    q_far = shift(q0, "queries", 2)

    first = prepare(
        "turn_keys_first",
        functools.partial(key_kernel, 0),
        (PLACES + META, HEAD),
        (k, v, positions, fk, fv, order, span),
        [VMEM] * 6 + [pl.BlockSpec(memory_space=pltpu.SMEM)],
        2 * 10**9,
    )
    first_near = [shift(first, "keys", -1), shift(first, "keys", 1)]
    second = prepare(
        "turn_keys_second",
        functools.partial(key_kernel, CHUNK),
        (2 * CHUNK, HEAD),
        (k, v, positions),
        [VMEM] * 3,
        2 * 10**9,
    )
    second_near = [shift(second, "keys", -1), shift(second, "keys", 1)]

    mine = attend("mine_own", [q0], [first, second])
    state = attend("others_own", [q_far, *q_near], [first, second])
    far = attend("far_first", [q_far], first_near, state)
    far, state, behind, ahead = lax.optimization_barrier((far, state, first_near[1], second_near[0]))
    first_far = shift(behind, "keys", 1)
    second_far = shift(ahead, "keys", -1)
    near = attend("near_near", q_near, [*first_near, *second_near], state, skip=1)
    far = attend("far_second", [q_far], second_near, far)
    near, far = lax.optimization_barrier((near, far))
    fresh = [first, *first_near, first_far]
    r_ahead, r_behind = attend("near_last", q_near, [first_far, second_far], near, fresh, finish=True)
    (r_far,) = attend("far_last", [q_far], [first_far, second_far], far, fresh, finish=True)
    back = [shift(r_far, "queries", 2), shift(r_ahead, "queries", 1), shift(r_behind, "queries", -1)]
    mine = attend("mine_rest", [q0], [*first_near, *second_near, first_far, second_far], mine, fresh)
    attended, mass = pl.pallas_call(
        combine_kernel,
        out_shape=[
            jax.ShapeDtypeStruct((TOK, GROUP * HEAD), jnp.bfloat16),
            jax.ShapeDtypeStruct((GROUP, TOK), jnp.float32),
        ],
        in_specs=[VMEM] * 5,
        out_specs=[VMEM] * 2,
        compiler_params=pltpu.CompilerParams(vmem_limit_bytes=8 * 2**20),
        name="combine",
    )(*mine, *back)
    return attended, mass.T


def solution(mesh):
    spec = (P("ctx", "tp"),) * 5 + (P("ctx"),) * 3
    return jax.shard_map(
        per_device,
        mesh=mesh,
        in_specs=spec,
        out_specs=(P("ctx", "tp"), P("ctx", "tp")),
        check_vma=False,
    )
```

```python
import functools

import jax
import jax.numpy as jnp
import ml_dtypes
import numpy as np
from jax import lax
from jax.experimental import pallas as pl
from jax.experimental.pallas import tpu as pltpu
from jax.sharding import PartitionSpec as P

GROUP = 8
HEAD = 128
TOK = 128
ROWS = GROUP * TOK
CACHED = 32768
SIDE = 4
CHUNK = 1280
LATER = 768
TP = 8
KT = 256
SCALE = HEAD**-0.5 * 1.4426950408889634
LN2 = 0.6931471805599453
LOW = -1e30
TOO_BIG = 2.0**100
TOO_SMALL = 2.0**-60
META = 16

VMEM = pl.BlockSpec(memory_space=pltpu.VMEM)


def shift(block, kind, step):
    pairs = []
    for i in range(SIDE * SIDE):
        z, y = divmod(i, SIDE)
        for t in range(TP):
            if (t % 2 == 0) == (kind == "keys"):
                j = z * SIDE + (y + step) % SIDE
            else:
                j = ((z + step) % SIDE) * SIDE + y
            pairs.append((i * TP + t, j * TP + t))
    return lax.ppermute(block, ("ctx", "tp"), pairs)


def _bf(x):
    return np.asarray(x, np.float32).astype(ml_dtypes.bfloat16).astype(np.float64)


def _fit():
    t = np.cos(np.linspace(0, np.pi, 4001)) * 0.5
    u = t * t
    cos = np.polynomial.polynomial.polyfit(u, np.cos(2 * np.pi * t), 8)
    good = np.abs(t) > 1e-3
    sin = np.polynomial.polynomial.polyfit(u[good], np.sin(2 * np.pi * t[good]) / t[good], 7)
    return [float(c) for c in cos], [float(c) for c in sin]


COS, SIN = _fit()


def _turns():
    turns = 500000.0 ** (-2.0 * np.arange(64) / HEAD) / (2 * np.pi)
    first = _bf(turns)
    second = _bf(turns - first)
    return [[float(x) for x in piece] for piece in (first, second, turns - first - second)]


TURNS = _turns()


def spread(constants):
    row = lax.broadcasted_iota(jnp.int32, (8, TOK), 0)
    tiles = []
    for first in range(0, 64, 8):
        tile = jnp.full((8, TOK), constants[first + 7], jnp.float32)
        for i in range(7):
            tile = jnp.where(row == i, constants[first + i], tile)
        tiles.append(tile)
    return jnp.concatenate(tiles, 0)


def angles(positions, turns):
    a = positions * turns[0]
    a = a - jnp.round(a)
    b = positions * turns[1]
    t = a + (b - jnp.round(b)) + positions * turns[2]
    t = t - jnp.round(t)
    u = t * t
    cos = jnp.full_like(u, COS[-1])
    for c in COS[-2::-1]:
        cos = cos * u + c
    sin = jnp.full_like(u, SIN[-1])
    for c in SIN[-2::-1]:
        sin = sin * u + c
    return cos, sin * t


def turned(x, cos, sin):
    lower, upper = x[:64], x[64:]
    return jnp.concatenate([lower * cos - upper * sin, upper * cos + lower * sin], 0)


def coded(places):
    high = jnp.right_shift(places, 4)
    rows = lax.broadcasted_iota(jnp.int32, (META, TOK), 0)
    both = jnp.where(rows == 0, high, jnp.where(rows == 1, places - high * 16, 0))
    return both.astype(jnp.float32).astype(jnp.bfloat16)


def places_of(meta):
    meta = meta.astype(jnp.float32)
    return meta[0:1, :] * 16.0 + meta[1:2, :]


def angle_kernel(order_ref, out_ref):
    order = order_ref[...]
    turns = [spread(piece) for piece in TURNS]
    cos, sin = angles((order + CACHED).astype(jnp.float32), turns)
    out_ref[0:64, :] = cos
    out_ref[64:128, :] = sin
    out_ref[128:, :] = coded(order).astype(jnp.float32)


def query_kernel(q_ref, angle_ref, out_ref):
    cos, sin = angle_ref[0:64, :], angle_ref[64:128, :]
    for g in range(GROUP):
        lanes = slice(g * HEAD, (g + 1) * HEAD)
        x = q_ref[:, lanes].astype(jnp.float32).T
        out_ref[0:HEAD, lanes] = turned(x, cos, sin).astype(jnp.bfloat16)
    out_ref[HEAD:, :] = jnp.concatenate([angle_ref[128:, :].astype(jnp.bfloat16)] * GROUP, 1)


FRESH_KEYS = 2 * CHUNK
FRESH_VALUES = FRESH_KEYS + TOK
PLACES = FRESH_VALUES + TOK


def key_kernel(start, k_ref, v_ref, pos_ref, *refs):
    with_fresh = len(refs) > 1
    if with_fresh:
        fk_ref, fv_ref, order_ref, span_ref, out_ref = refs
    else:
        (out_ref,) = refs
    turns = [spread(piece) for piece in TURNS]

    def keys(x, positions):
        cos, sin = angles(positions.astype(jnp.float32), turns)
        return turned(x.astype(jnp.float32).T, cos, sin).T.astype(jnp.bfloat16)

    def values(x):
        return x.astype(jnp.float32).T.astype(jnp.bfloat16)

    size = CHUNK if with_fresh else LATER
    for b in range(size // TOK):
        rows = slice(start + b * TOK, start + (b + 1) * TOK)
        tile = start // TOK + b
        out_ref[b * TOK : (b + 1) * TOK, :] = keys(k_ref[rows, :], pos_ref[tile : tile + 1, :])
        out_ref[size + b * TOK : size + (b + 1) * TOK, :] = values(v_ref[rows, :])
    if with_fresh:
        order = order_ref[...]
        out_ref[FRESH_KEYS:FRESH_VALUES, :] = keys(fk_ref[...], order + CACHED)
        out_ref[FRESH_VALUES:PLACES, :] = values(fv_ref[...])
        lane = lax.broadcasted_iota(jnp.int32, (1, TOK), 1)
        out_ref[PLACES:, :] = coded(jnp.where(lane < span_ref[0], order, 4000))


def dot(a, b):
    return lax.dot_general(a, b, (((1,), (0,)), ((), ())), preferred_element_type=jnp.float32)


def attend_kernel(plan, *refs):
    it = iter(refs)
    n_q, n_fresh = plan["n_q"], plan["n_fresh"]
    q_refs = [next(it) for _ in range(n_q)]
    kv_refs = [next(it) for _ in range(plan["n_kv"])]
    fresh_refs = [next(it) for _ in range(n_fresh)]
    if not plan["start"]:
        acc_in, ml_in = next(it), next(it)
    if plan["finish"]:
        out_refs = [next(it) for _ in range(n_q)]
    else:
        acc_out, ml_out = next(it), next(it)
    q_s = next(it)
    if n_fresh:
        f_s, place_s = next(it), next(it)
    if plan["finish"]:
        acc_out, ml_out = next(it), next(it)

    for i, r in enumerate(q_refs):
        q_s[i] = r[...]
    for i, r in enumerate(fresh_refs):
        f_s[i * TOK : (i + 1) * TOK, :] = r[FRESH_KEYS:FRESH_VALUES, :]
        f_s[(n_fresh + i) * TOK : (n_fresh + i + 1) * TOK, :] = r[FRESH_VALUES:PLACES, :]
        place_s[i * TOK : (i + 1) * TOK, :] = jnp.broadcast_to(places_of(r[PLACES:, :]), (TOK, TOK)).T

    def aligned(i):
        return i if isinstance(i, int) else pl.multiple_of(i, TOK)

    def k_tile(ref, first):
        return ref[pl.ds(aligned(first), KT), :]

    def v_tile(ref, first):
        return jnp.concatenate([ref[pl.ds(aligned(first + j * TOK), TOK), :] for j in range(KT // TOK)], 1)

    def scores(ref, first, item, masked):
        s = dot(k_tile(ref, first), q_s[item, 0:HEAD, :]) * SCALE
        if masked:
            mine = places_of(q_s[item, HEAD:, 0:TOK])
            mask = place_s[pl.ds(aligned(first), KT), :] <= mine
            s = jnp.where(jnp.concatenate([mask] * GROUP, 1), s, LOW)
        return s

    sizes = [LATER if ref.shape[0] == 2 * LATER else CHUNK for ref in kv_refs]
    sources = [(ref, n, n, False) for ref, n in zip(kv_refs, sizes)]
    if n_fresh:
        sources.append((f_s, n_fresh * TOK, n_fresh * TOK, True))

    def old_of(item):
        if plan["start"]:
            return None
        at = item + plan["skip"]
        return ml_in[at][0:1, :], ml_in[at][1:2, :], acc_in[at]

    skip = plan["skip"]

    def put(item, m, total, acc):
        acc_out[item] = acc
        ml_out[item] = jnp.concatenate([m, total, jnp.zeros((6, ROWS), jnp.float32)], 0)

    def quick(item):
        tiles = [(ref, first, values, masked) for ref, values, n, masked in sources for first in range(0, n, KT)]
        old = old_of(item)
        total, acc = (None, None) if old is None else old[1:]
        part = jnp.zeros((8, ROWS), jnp.float32)

        def scores_of(tile):
            return scores(tile[0], tile[1], item, tile[3])

        ahead = scores_of(tiles[0])
        for j, (ref, first, values, _) in enumerate(tiles):
            s = ahead
            if j + 1 < len(tiles):
                ahead = scores_of(tiles[j + 1])
            p = jnp.exp2(s)
            part = part + jnp.sum(p.reshape(KT // 8, 8, ROWS), 0)
            pv = dot(v_tile(ref, values + first), p.astype(jnp.bfloat16))
            acc = pv if acc is None else acc + pv
        part = jnp.sum(part, 0, keepdims=True)
        put(item, jnp.zeros((1, ROWS), jnp.float32), part if total is None else total + part, acc)

    def careful(item):
        def group(g, carry):
            lanes = pl.ds(aligned(g * TOK), TOK)
            if plan["start"]:
                m = jnp.full((1, TOK), LOW, jnp.float32)
                total = jnp.zeros((1, TOK), jnp.float32)
                acc = jnp.zeros((HEAD, TOK), jnp.float32)
            else:
                at = item + skip
                m, total, acc = ml_in[at, 0:1, lanes], ml_in[at, 1:2, lanes], acc_in[at, :, lanes]
            q = q_s[item, 0:HEAD, lanes]
            for ref, values, n, masked in sources:

                def step(t, state, ref=ref, values=values, masked=masked):
                    m, total, acc = state
                    first = t * KT
                    s = dot(k_tile(ref, first), q) * SCALE
                    if masked:
                        mine = places_of(q_s[item, HEAD:, 0:TOK])
                        s = jnp.where(place_s[pl.ds(aligned(first), KT), :] <= mine, s, LOW)
                    top = jnp.maximum(m, jnp.max(s, 0, keepdims=True))
                    back = jnp.exp2(m - top)
                    p = jnp.where(s > 0.5 * LOW, jnp.exp2(s - top), 0.0)
                    total = total * back + jnp.sum(p, 0, keepdims=True)
                    acc = acc * back + dot(v_tile(ref, values + first), p.astype(jnp.bfloat16))
                    return top, total, acc

                m, total, acc = lax.fori_loop(0, n // KT, step, (m, total, acc))
            acc_out[item, :, lanes] = acc
            ml_out[item, 0:1, lanes] = m
            ml_out[item, 1:2, lanes] = total
            return carry

        lax.fori_loop(0, GROUP, group, 0)

    def everything(step):
        def body(item, carry):
            step(item)
            return carry

        if n_q == 1:
            step(0)
        else:
            lax.fori_loop(0, n_q, body, 0)

    everything(quick)
    fine = None
    for i in range(n_q):
        total = ml_out[i][1:2, :]
        good = jnp.where((total < TOO_BIG) & (total > TOO_SMALL), 1.0, 0.0)
        if not plan["start"]:
            good = jnp.where(ml_in[i + skip][0:1, :] == 0.0, good, 0.0)
        fine = good if fine is None else jnp.minimum(fine, good)

    @pl.when(jnp.min(fine) < 0.5)
    def _():
        everything(careful)

    if plan["finish"]:
        for i in range(n_q):
            m, total = ml_out[i][0:1, :], ml_out[i][1:2, :]
            out_refs[i][0:HEAD, :] = (acc_out[i] * (1.0 / total)).astype(jnp.bfloat16)
            out_refs[i][HEAD:, :] = coded_mass(m + jnp.log2(total))


def coded_mass(mass):
    a = mass.astype(jnp.bfloat16).astype(jnp.float32)
    b = (mass - a).astype(jnp.bfloat16).astype(jnp.float32)
    c = mass - a - b
    rows = lax.broadcasted_iota(jnp.int32, (META, ROWS), 0)
    return jnp.where(rows == 0, a, jnp.where(rows == 1, b, jnp.where(rows == 2, c, 0.0))).astype(jnp.bfloat16)


def attend(name, queries, kvs, state=None, fresh=(), finish=False, skip=0):
    n_q = len(queries)
    plan = dict(
        n_q=n_q,
        n_kv=len(kvs),
        n_fresh=len(fresh),
        start=state is None,
        finish=finish,
        skip=skip,
    )
    acc = jax.ShapeDtypeStruct((n_q, HEAD, ROWS), jnp.float32)
    ml = jax.ShapeDtypeStruct((n_q, 8, ROWS), jnp.float32)
    scratch = [pltpu.VMEM((n_q, HEAD + META, ROWS), jnp.bfloat16)]
    if fresh:
        scratch += [
            pltpu.VMEM((2 * len(fresh) * TOK, HEAD), jnp.bfloat16),
            pltpu.VMEM((len(fresh) * TOK, TOK), jnp.float32),
        ]
    if finish:
        outs = [jax.ShapeDtypeStruct((HEAD + META, ROWS), jnp.bfloat16)] * n_q
        scratch += [pltpu.VMEM(acc.shape, jnp.float32), pltpu.VMEM(ml.shape, jnp.float32)]
    else:
        outs = [acc, ml]
    args = list(queries) + list(kvs) + list(fresh) + list(state or ())
    pairs = n_q * (len(kvs) * (CHUNK + LATER) // 2 + len(fresh) * TOK) * ROWS
    return pl.pallas_call(
        functools.partial(attend_kernel, plan),
        out_shape=outs,
        in_specs=[VMEM] * len(args),
        out_specs=[VMEM] * len(outs),
        scratch_shapes=scratch,
        compiler_params=pltpu.CompilerParams(vmem_limit_bytes=24 * 2**20),
        cost_estimate=pl.CostEstimate(flops=pairs * 1024, bytes_accessed=0, transcendentals=0),
        name=name,
    )(*args)


def combine_kernel(acc_ref, ml_ref, *refs):
    parts, (att_ref, mass_ref) = refs[:-2], refs[-2:]
    total = ml_ref[0][1:2, :]
    masses = [ml_ref[0][0:1, :] + jnp.log2(total)]
    for r in parts:
        rows = r[HEAD:, :].astype(jnp.float32)
        masses.append(rows[0:1, :] + rows[1:2, :] + rows[2:3, :])
    top = functools.reduce(jnp.maximum, masses)
    weights = [jnp.exp2(m - top) for m in masses]
    den = functools.reduce(jnp.add, weights)
    mass = (top + jnp.log2(den)) * LN2
    shares = [w / den for w in weights]
    shares[0] = shares[0] / total
    for g in range(GROUP):
        lanes = slice(g * TOK, (g + 1) * TOK)
        x = acc_ref[0, :, lanes] * shares[0][:, lanes]
        for r, w in zip(parts, shares[1:]):
            x = x + r[0:HEAD, lanes].astype(jnp.float32) * w[:, lanes]
        att_ref[:, lanes] = x.T.astype(jnp.bfloat16)
    mass_ref[...] = jnp.concatenate([mass[:, g * TOK : (g + 1) * TOK] for g in range(GROUP)], 0)


def prepare(name, kernel, shape, args, specs, work, dtype=jnp.bfloat16):
    return pl.pallas_call(
        kernel,
        out_shape=jax.ShapeDtypeStruct(shape, dtype),
        in_specs=specs,
        out_specs=VMEM,
        compiler_params=pltpu.CompilerParams(vmem_limit_bytes=8 * 2**20),
        cost_estimate=pl.CostEstimate(flops=work, bytes_accessed=0, transcendentals=0),
        name=name,
    )(*args)


def per_device(queries, k, v, fk, fv, positions, order, span):
    order = order.reshape(1, TOK)
    positions = positions.reshape((CHUNK + LATER) // TOK, TOK)
    angle = prepare("angles", angle_kernel, (HEAD + META, TOK), (order,), [VMEM], 10**9, jnp.float32)
    q0 = prepare("turn_queries", query_kernel, (HEAD + META, ROWS), (queries, angle), [VMEM] * 2, 10**9)
    q_near = [shift(q0, "queries", -1), shift(q0, "queries", 1)]
    q_far = shift(q0, "queries", 2)

    first = prepare(
        "turn_keys_first",
        functools.partial(key_kernel, 0),
        (PLACES + META, HEAD),
        (k, v, positions, fk, fv, order, span),
        [VMEM] * 6 + [pl.BlockSpec(memory_space=pltpu.SMEM)],
        2 * 10**9,
    )
    first_near = [shift(first, "keys", -1), shift(first, "keys", 1)]
    second = prepare(
        "turn_keys_second",
        functools.partial(key_kernel, CHUNK),
        (2 * LATER, HEAD),
        (k, v, positions),
        [VMEM] * 3,
        2 * 10**9,
    )
    second_near = [shift(second, "keys", -1), shift(second, "keys", 1)]

    mine = attend("mine_own", [q0], [first, second])
    state = attend("others_own", [q_far, *q_near], [first, second])
    far = attend("far_first", [q_far], first_near, state)
    far, state, behind, ahead = lax.optimization_barrier((far, state, first_near[1], second_near[0]))
    first_far = shift(behind, "keys", 1)
    second_far = shift(ahead, "keys", -1)
    near = attend("near_near", q_near, [*first_near, *second_near], state, skip=1)
    far = attend("far_second", [q_far], second_near, far)
    near, far = lax.optimization_barrier((near, far))
    fresh = [first, *first_near, first_far]
    r_ahead, r_behind = attend("near_last", q_near, [first_far, second_far], near, fresh, finish=True)
    (r_far,) = attend("far_last", [q_far], [first_far, second_far], far, fresh, finish=True)
    back = [shift(r_far, "queries", 2), shift(r_ahead, "queries", 1), shift(r_behind, "queries", -1)]
    mine = attend("mine_rest", [q0], [*first_near, *second_near, first_far, second_far], mine, fresh)
    attended, mass = pl.pallas_call(
        combine_kernel,
        out_shape=[
            jax.ShapeDtypeStruct((TOK, GROUP * HEAD), jnp.bfloat16),
            jax.ShapeDtypeStruct((GROUP, TOK), jnp.float32),
        ],
        in_specs=[VMEM] * 5,
        out_specs=[VMEM] * 2,
        compiler_params=pltpu.CompilerParams(vmem_limit_bytes=8 * 2**20),
        name="combine",
    )(*mine, *back)
    return attended, mass.T


def solution(mesh):
    spec = (P("ctx", "tp"),) * 5 + (P("ctx"),) * 3
    return jax.shard_map(
        per_device,
        mesh=mesh,
        in_specs=spec,
        out_specs=(P("ctx", "tp"), P("ctx", "tp")),
        check_vma=False,
    )
```
